32 devices in a mesh: section: 2 (over x), expert: 16 (over z, y, core).
Axes of the slice: x: 2, y: 2, z: 4, core: 2. Of those that a mesh axis runs over, the one named last changes fastest.
Arguments:
- fwd_act: bfloat16 [2, 128, 2048], P('section', 'expert'), may hold values from -6 to 6
- fwd_routes: int32 [2, 128, 8], P('section', 'expert'), may hold values from 0 to 15, all different within a row; in each aligned block of 8 rows (0 to 7, 8 to 15, ..., all dimensions but the last counted through in order) at most 8 rows name the same one
- bwd_saved: bfloat16 [2, 128, 2048], P('section', 'expert'), may hold values from -6 to 6
- bwd_grad: bfloat16 [2, 128, 2048], P('section', 'expert'), may hold values from -6 to 6
- bwd_routes: int32 [2, 128, 8], P('section', 'expert'), may hold values from 0 to 15, all different within a row; in each aligned block of 8 rows (0 to 7, 8 to 15, ..., all dimensions but the last counted through in order) at most 8 rows name the same one
- norm_gain: float32 [2, 2048], P('section'), may hold values from 0.1 to 1.9
- router: bfloat16 [2048, 16], replicated, may hold values from -0.125 to 0.125
- w_gate: bfloat16 [16, 2048, 768], P('expert'), may hold values from -0.125 to 0.125
- w_up: bfloat16 [16, 2048, 768], P('expert'), may hold values from -0.125 to 0.125
- w_down: bfloat16 [16, 768, 2048], P('expert'), may hold values from -0.875 to 0.875
Outputs:
- fwd_next: bfloat16 [2, 128, 2048], P('section', 'expert')
- grad_prev: bfloat16 [2, 128, 2048], P('section', 'expert')
The draws below stay inside these ranges and needn't reach their ends.
Inputs may be any that keep to these rules, and one draw needn't show every extreme that they name: `fwd_routes`: each token names 8 different experts. Within one section, the 8 tokens of one expert-axis device (aligned blocks of rows) name any one expert at most 8 times, and in every draw some block names some expert exactly 8 times. `bwd_routes`: as for fwd_routes, drawn independently.
All inputs are finite; a program needn't handle non-finite values.
Results may differ from the reference program's by a relative error of at most 0.01.
Values may be sent and summed in bfloat16 or wider, within the bound.
No kernel may reach another device: no remote copies, remote signals or barrier semaphores. Data moves between devices by JAX's collectives and lax.ppermute only.
A program may use at most 64 MiB of HBM per device.

```python
import math
import jax
import jax.numpy as jnp
import numpy as np
from jax import lax

D = 2048
FF = 768
TOP = 8
TOK_DEV = 8
EXPERTS = 16
TOKENS = 128
SECTIONS = 2
CAP = 8
N_EXPERT = 16


def levels(stream_key, extent, split, least, top_value):
    loudness, own = 1.0, jax.random.fold_in(stream_key, 6)
    for dim, blocks in split:
        steps = jnp.exp(jax.random.uniform(jax.random.fold_in(own, dim), (blocks,), jnp.float32, least / len(split), top_value / len(split)))
        loudness = loudness * jnp.repeat(steps, extent[dim] // blocks).reshape([-1 if axis == dim else 1 for axis in range(len(extent))])
    return loudness


def assign_block(rng, own, number, rows, number_of, top, most, slope):
    order = jax.random.permutation(rng, number_of)
    crowded, ordinary = portions_of(number_of, rows * top, most, slope, True), portions_of(number_of, rows * top, most, slope, False)
    places = jnp.arange(number_of)

    def named(sizes, turn):
        used = int((sizes > 0).sum())
        fixed = max(1, used // 4)
        moved = fixed + (places - fixed + turn * (used - fixed)) % max(1, number_of - fixed)
        return jnp.zeros((number_of,), jnp.int32).at[order[jnp.where(places < fixed, places, moved)]].set(jnp.asarray(sizes, jnp.int32))

    sizes = jnp.where(number % 4 == 0, named(crowded, number // 4), named(ordinary, number - number // 4 - 1))
    mixed = jax.random.permutation(jax.random.fold_in(own, 3), number_of)
    giver, receiver = mixed[0:number_of // 2 * 2:2], mixed[1:number_of // 2 * 2:2]
    slack = jnp.minimum(sizes[giver] - 1, most - sizes[receiver]) // 2
    slack = jnp.where((giver == order[0]) | (receiver == order[0]) | (sizes[receiver] == 0), 0, jnp.maximum(slack, 0))
    moved = jax.random.randint(jax.random.fold_in(own, 4), (number_of // 2,), 0, 1 << 20) % (slack + 1)
    sizes = sizes.at[giver].add(-moved).at[receiver].add(moved)
    items = jnp.searchsorted(jnp.cumsum(sizes), jnp.arange(rows * top), side="right").astype(jnp.int32)
    table = items.reshape(top, rows).T
    table = table[jax.random.permutation(jax.random.fold_in(own, 1), rows)]
    turn = jax.random.randint(jax.random.fold_in(own, 2), (rows, 1), 0, top)
    return jnp.take_along_axis(table, (jnp.arange(top)[None, :] + turn) % top, axis=1)


def portions_of(count, total, reach, skew, full):
    loads = [(1 << 20) // math.isqrt(standing ** skew) + 1 for standing in range(1, count + 1)]
    largest = reach if full else min(reach, max(-(-total // count), total * loads[0] // sum(loads)))
    least = 1 if total - largest >= count - 1 else 0
    holding, surplus = [largest] + [least] * (count - 1), total - largest - least * (count - 1)
    while surplus > 0:
        candidates = [i for i in range(1, count) if holding[i] < largest] or [i for i in range(1, count) if holding[i] < reach]
        mass, remaining = sum([loads[i] for i in candidates]), surplus
        for i in candidates:
            addition = min(reach - holding[i], max(1, remaining * loads[i] // mass), surplus)
            holding[i] = holding[i] + addition
            surplus = surplus - addition
    return np.array(holding)


def centred(own_key, dims, width, bound, split=(), kind=jnp.bfloat16):
    values = jax.random.normal(own_key, dims, jnp.float32) * width
    if len(split) > 0:
        values = levels(own_key, dims, split, -0.22, 0.18) * values
    return jnp.clip(values, min=-bound, max=bound).astype(kind)


def setup_inputs(seed: int = 0) -> dict:
    key_of = jax.random.split(jax.random.key(seed), 11)
    fwd_act = centred(key_of[0], (SECTIONS, TOKENS, D), 1.0, 6.0, ((0, 2), (1, 16)))
    fwd_routes_keys = jax.random.split(jax.random.fold_in(key_of[1], 1), SECTIONS * TOKENS // TOK_DEV)
    fwd_routes_turns = jax.random.permutation(jax.random.fold_in(key_of[1], 3), SECTIONS * TOKENS // TOK_DEV)
    fwd_routes = jax.vmap(lambda own, number: assign_block(jax.random.fold_in(key_of[1], 2), own, number, TOK_DEV, EXPERTS, TOP, CAP, 2))(fwd_routes_keys, fwd_routes_turns).reshape((SECTIONS, TOKENS, TOP))
    bwd_saved = centred(key_of[2], (SECTIONS, TOKENS, D), 1.0, 6.0, ((0, 2), (1, 16)))
    bwd_grad = centred(key_of[3], (SECTIONS, TOKENS, D), 1.0, 6.0, ((0, 2), (1, 16)))
    bwd_routes_keys = jax.random.split(jax.random.fold_in(key_of[4], 1), SECTIONS * TOKENS // TOK_DEV)
    bwd_routes_turns = jax.random.permutation(jax.random.fold_in(key_of[4], 3), SECTIONS * TOKENS // TOK_DEV)
    bwd_routes = jax.vmap(lambda own, number: assign_block(jax.random.fold_in(key_of[4], 2), own, number, TOK_DEV, EXPERTS, TOP, CAP, 2))(bwd_routes_keys, bwd_routes_turns).reshape((SECTIONS, TOKENS, TOP))
    norm_gain = jnp.clip(1.0 + 0.18 * jax.random.normal(key_of[5], (SECTIONS, D), jnp.float32), 0.1, 1.9)
    router = centred(key_of[6], (D, EXPERTS), D ** -0.5, 0.125)
    w_gate = centred(key_of[7], (EXPERTS, D, FF), D ** -0.5, 0.125, ((0, 16),))
    w_up = centred(key_of[8], (EXPERTS, D, FF), D ** -0.5, 0.125, ((0, 16),))
    w_down = centred(key_of[9], (EXPERTS, FF, D), (FF // 16) ** -0.5, 0.875, ((0, 16),))
    return dict(fwd_act=fwd_act, fwd_routes=fwd_routes, bwd_saved=bwd_saved, bwd_grad=bwd_grad, bwd_routes=bwd_routes, norm_gain=norm_gain, router=router, w_gate=w_gate, w_up=w_up, w_down=w_down)


EPSILON = 1e-06

def normalize(acts_in, gain_row):
    values = acts_in.astype(jnp.float32)
    factor = lax.rsqrt(lax.optimization_barrier(jnp.mean(values * values, axis=-1, keepdims=True)) + EPSILON)
    unit_rows = values * factor
    return ((unit_rows * gain_row).astype(jnp.bfloat16), unit_rows, factor)

def gate_values(normed, router, routes):
    logits = jnp.dot(normed, router, preferred_element_type=jnp.float32)
    chosen = jnp.take_along_axis(logits, routes, axis=1)
    raised = jnp.exp(chosen)
    return raised / lax.optimization_barrier(jnp.sum(raised, axis=-1, keepdims=True))

def expert_forward(rows_in, gate_mat, up_mat, down_mat):
    pre_gate = jnp.dot(rows_in, gate_mat, preferred_element_type=jnp.float32)
    pre_up = jnp.dot(rows_in, up_mat, preferred_element_type=jnp.float32)
    sigma = jax.nn.sigmoid(pre_gate)
    hidden = (pre_gate * sigma * pre_up).astype(jnp.bfloat16)
    return jnp.dot(hidden, down_mat, preferred_element_type=jnp.float32).astype(jnp.bfloat16)

def expert_backward(rows_in, grads_in, gate_mat, up_mat, down_mat):
    pre_gate = jnp.dot(rows_in, gate_mat, preferred_element_type=jnp.float32)
    pre_up = jnp.dot(rows_in, up_mat, preferred_element_type=jnp.float32)
    sigma = jax.nn.sigmoid(pre_gate)
    silu_val = pre_gate * sigma
    hidden = (silu_val * pre_up).astype(jnp.bfloat16)
    expert_out = jnp.dot(hidden, down_mat, preferred_element_type=jnp.float32).astype(jnp.bfloat16)
    dgate = lax.optimization_barrier(jnp.sum(grads_in.astype(jnp.float32) * expert_out.astype(jnp.float32), axis=-1)).astype(jnp.bfloat16)
    contract = (((1,), (1,)), ((), ()))
    d_hidden = lax.dot_general(grads_in, down_mat, contract, preferred_element_type=jnp.float32)
    d_up = (d_hidden * silu_val).astype(jnp.bfloat16)
    d_pre = (d_hidden * pre_up * sigma * (1.0 + pre_gate * (1.0 - sigma))).astype(jnp.bfloat16)
    d_rows = lax.dot_general(d_pre, gate_mat, contract, preferred_element_type=jnp.float32)
    d_rows = d_rows + lax.dot_general(d_up, up_mat, contract, preferred_element_type=jnp.float32)
    return (d_rows.astype(jnp.bfloat16), dgate)

def input_gradient(gates, dgate, pair_grads, routes, router, unit_rows, factor, gain_row, grads_in):
    d_normed = lax.optimization_barrier(jnp.sum(gates[:, :, None] * pair_grads, axis=1))
    d_chosen = gates * (dgate - lax.optimization_barrier(jnp.sum(gates * dgate, axis=-1, keepdims=True)))
    labels = jnp.arange(router.shape[1], dtype=jnp.int32)
    hits = (routes[:, :, None] == labels[None, None, :]).astype(jnp.float32)
    d_logits = lax.optimization_barrier(jnp.sum(hits * d_chosen[:, :, None], axis=1))
    d_normed = d_normed + lax.dot_general(d_logits, router.astype(jnp.float32), (((1,), (1,)), ((), ())), precision=lax.Precision.HIGHEST)
    d_unit = d_normed * gain_row
    result = factor * (d_unit - unit_rows * lax.optimization_barrier(jnp.mean(d_unit * unit_rows, axis=-1, keepdims=True)))
    return (result + grads_in.astype(jnp.float32)).astype(jnp.bfloat16)

def places(routes):
    blocks = routes.reshape(N_EXPERT, TOK_DEV * TOP)
    labels = jnp.arange(EXPERTS, dtype=jnp.int32)
    onehot = (blocks[:, :, None] == labels[None, None, :]).astype(jnp.int32)
    before = jnp.cumsum(onehot, axis=1) - onehot
    slot_ids = lax.optimization_barrier(jnp.sum(before * onehot, axis=2)).astype(jnp.int32)
    sources = jnp.arange(N_EXPERT, dtype=jnp.int32)[:, None]
    return (sources * CAP + slot_ids).reshape(TOKENS, TOP).astype(jnp.int32)

def reference(fwd_act, fwd_routes, bwd_saved, bwd_grad, bwd_routes, norm_gain, router, w_gate, w_up, w_down):
    row_total = N_EXPERT * CAP

    def run_section(operands):
        acts_f, routes_f, saved_b, grads_b, routes_b, gain_row = operands
        normed_f, unused_unit, unused_factor = normalize(acts_f, gain_row)
        gates_f = gate_values(normed_f, router, routes_f)
        rows_f = places(routes_f)
        spread_f = jnp.broadcast_to(normed_f[:, None, :], (TOKENS, TOP, D))
        buffer_f = jnp.zeros((EXPERTS, row_total, D), jnp.bfloat16).at[routes_f, rows_f].set(spread_f)
        outputs_f = lax.map(lambda members: expert_forward(members[3], members[0], members[1], members[2]), (w_gate, w_up, w_down, buffer_f))
        picked_f = outputs_f[routes_f, rows_f].astype(jnp.float32)
        layer_out = (acts_f.astype(jnp.float32) + lax.optimization_barrier(jnp.sum(gates_f[:, :, None] * picked_f, axis=1))).astype(jnp.bfloat16)
        normed_b, unit_b, factor_b = normalize(saved_b, gain_row)
        gates_b = gate_values(normed_b, router, routes_b)
        rows_b = places(routes_b)
        spread_x = jnp.broadcast_to(normed_b[:, None, :], (TOKENS, TOP, D))
        spread_g = jnp.broadcast_to(grads_b[:, None, :], (TOKENS, TOP, D))
        buffer_x = jnp.zeros((EXPERTS, row_total, D), jnp.bfloat16).at[routes_b, rows_b].set(spread_x)
        buffer_g = jnp.zeros((EXPERTS, row_total, D), jnp.bfloat16).at[routes_b, rows_b].set(spread_g)
        d_rows, d_gates = lax.map(lambda members: expert_backward(members[3], members[4], members[0], members[1], members[2]), (w_gate, w_up, w_down, buffer_x, buffer_g))
        pair_grads = d_rows[routes_b, rows_b].astype(jnp.float32)
        dgate = d_gates[routes_b, rows_b].astype(jnp.float32)
        d_input = input_gradient(gates_b, dgate, pair_grads, routes_b, router, unit_b, factor_b, gain_row, grads_b)
        return (layer_out, d_input)
    outs_f, outs_b = lax.map(run_section, (fwd_act, fwd_routes, bwd_saved, bwd_grad, bwd_routes, norm_gain))
    zero_block = jnp.zeros((1, TOKENS, D), jnp.bfloat16)
    fwd_next = jnp.concatenate([zero_block, outs_f[:-1]], axis=0)
    grad_prev = jnp.concatenate([outs_b[1:], zero_block], axis=0)
    return (fwd_next, grad_prev)
```

```python
import jax
import jax.numpy as jnp
from jax import lax
from jax.experimental import pallas as pl
from jax.experimental.pallas import tpu as pltpu
from jax.sharding import PartitionSpec as P

EPSILON = 1e-06


def shifted(block, axis, distance):
    devices = range(lax.axis_size(axis))
    route = [(i - distance, i) for i in devices if i - distance in devices]
    return lax.ppermute(block, axis, route)


def normalize(acts_in, gain_row):
    values = acts_in.astype(jnp.float32)
    factor = lax.rsqrt(jnp.mean(values * values, axis=-1, keepdims=True) + EPSILON)
    unit_rows = values * factor
    return ((unit_rows * gain_row).astype(jnp.bfloat16), unit_rows, factor)


def gate_values(normed, router, routes):
    logits = jnp.dot(normed, router, preferred_element_type=jnp.float32)
    chosen = jnp.take_along_axis(logits, routes, axis=1)
    raised = jnp.exp(chosen)
    return raised / jnp.sum(raised, axis=-1, keepdims=True)


def expert_forward(rows_in, gate_mat, up_mat, down_mat):
    pre_gate = jnp.dot(rows_in, gate_mat, preferred_element_type=jnp.float32)
    pre_up = jnp.dot(rows_in, up_mat, preferred_element_type=jnp.float32)
    sigma = jax.nn.sigmoid(pre_gate)
    hidden = (pre_gate * sigma * pre_up).astype(jnp.bfloat16)
    return jnp.dot(hidden, down_mat, preferred_element_type=jnp.float32).astype(jnp.bfloat16)


def expert_backward(rows_in, grads_in, gate_mat, up_mat, down_mat):
    pre_gate = jnp.dot(rows_in, gate_mat, preferred_element_type=jnp.float32)
    pre_up = jnp.dot(rows_in, up_mat, preferred_element_type=jnp.float32)
    sigma = jax.nn.sigmoid(pre_gate)
    silu_val = pre_gate * sigma
    hidden = (silu_val * pre_up).astype(jnp.bfloat16)
    expert_out = jnp.dot(hidden, down_mat, preferred_element_type=jnp.float32).astype(jnp.bfloat16)
    dgate = jnp.sum(grads_in.astype(jnp.float32) * expert_out.astype(jnp.float32), axis=-1).astype(
        jnp.bfloat16
    )
    contract = (((1,), (1,)), ((), ()))
    d_hidden = lax.dot_general(grads_in, down_mat, contract, preferred_element_type=jnp.float32)
    d_up = (d_hidden * silu_val).astype(jnp.bfloat16)
    d_pre = (d_hidden * pre_up * sigma * (1.0 + pre_gate * (1.0 - sigma))).astype(jnp.bfloat16)
    d_rows = lax.dot_general(d_pre, gate_mat, contract, preferred_element_type=jnp.float32)
    d_rows = d_rows + lax.dot_general(d_up, up_mat, contract, preferred_element_type=jnp.float32)
    return (d_rows.astype(jnp.bfloat16), dgate)


def input_gradient(gates, dgate, pair_grads, routes, router, unit_rows, factor, gain_row, grads_in):
    d_normed = jnp.sum(gates[:, :, None] * pair_grads, axis=1)
    d_chosen = gates * (dgate - jnp.sum(gates * dgate, axis=-1, keepdims=True))
    labels = jnp.arange(router.shape[1], dtype=jnp.int32)
    hits = (routes[:, :, None] == labels[None, None, :]).astype(jnp.float32)
    d_logits = jnp.sum(hits * d_chosen[:, :, None], axis=1)
    d_normed = d_normed + lax.dot_general(
        d_logits,
        router.astype(jnp.float32),
        (((1,), (1,)), ((), ())),
        precision=lax.Precision.HIGHEST,
    )
    d_unit = d_normed * gain_row
    result = factor * (d_unit - unit_rows * jnp.mean(d_unit * unit_rows, axis=-1, keepdims=True))
    return (result + grads_in.astype(jnp.float32)).astype(jnp.bfloat16)


def placement(routes, expert_count, capacity):
    flat_ids = routes.reshape(-1)
    labels = jnp.arange(expert_count, dtype=jnp.int32)
    onehot = (flat_ids[:, None] == labels[None, :]).astype(jnp.int32)
    before = jnp.cumsum(onehot, axis=0) - onehot
    slot_ids = jnp.sum(before * onehot, axis=1)
    target = flat_ids * capacity + slot_ids
    slot_labels = jnp.arange(expert_count * capacity, dtype=jnp.int32)
    select = (slot_labels[:, None] == target[None, :]).astype(jnp.bfloat16)
    spread = jnp.sum(
        select.reshape(expert_count * capacity, routes.shape[0], routes.shape[1]), axis=2
    )
    return (target, spread)


def dispatch(spread, rows_in, expert_count, capacity):
    placed = jnp.dot(spread, rows_in, preferred_element_type=jnp.float32).astype(jnp.bfloat16)
    return placed.reshape(expert_count, capacity, rows_in.shape[1])


def routed_plan(
    fwd_act, fwd_routes, bwd_saved, bwd_grad, bwd_routes, norm_gain, router, w_gate, w_up, w_down
):
    tok_count = fwd_act.shape[1]
    top_count = fwd_routes.shape[2]
    model_width = fwd_act.shape[2]
    expert_count = router.shape[1]
    capacity = min(tok_count, max(2, 2 * tok_count * top_count // expert_count))
    gain_row = norm_gain[0]
    gate_mat = w_gate[0]
    up_mat = w_up[0]
    down_mat = w_down[0]
    acts_f = fwd_act[0]
    routes_f = fwd_routes[0]
    normed_f, unused_unit, unused_factor = normalize(acts_f, gain_row)
    gates_f = gate_values(normed_f, router, routes_f)
    target_f, spread_f = placement(routes_f, expert_count, capacity)
    send_f = dispatch(spread_f, normed_f, expert_count, capacity)
    saved_b = bwd_saved[0]
    grads_b = bwd_grad[0]
    routes_b = bwd_routes[0]
    normed_b, unit_b, factor_b = normalize(saved_b, gain_row)
    gates_b = gate_values(normed_b, router, routes_b)
    target_b, spread_b = placement(routes_b, expert_count, capacity)
    send_x = dispatch(spread_b, normed_b, expert_count, capacity)
    send_g = dispatch(spread_b, grads_b, expert_count, capacity)
    rows_in = lax.all_to_all(send_f, "expert", split_axis=0, concat_axis=0, tiled=True)
    sources = rows_in.shape[0]
    slots = rows_in.shape[1]
    result = expert_forward(rows_in.reshape(-1, model_width), gate_mat, up_mat, down_mat)
    back_f = lax.all_to_all(
        result.reshape(sources, slots, model_width),
        "expert",
        split_axis=0,
        concat_axis=0,
        tiled=True,
    )
    rows_in = lax.all_to_all(send_x, "expert", split_axis=0, concat_axis=0, tiled=True)
    grads_in = lax.all_to_all(send_g, "expert", split_axis=0, concat_axis=0, tiled=True)
    sources = rows_in.shape[0]
    slots = rows_in.shape[1]
    d_rows, d_gates = expert_backward(
        rows_in.reshape(-1, model_width),
        grads_in.reshape(-1, model_width),
        gate_mat,
        up_mat,
        down_mat,
    )
    back_rows = lax.all_to_all(
        d_rows.reshape(sources, slots, model_width),
        "expert",
        split_axis=0,
        concat_axis=0,
        tiled=True,
    )
    back_gates = lax.all_to_all(
        d_gates.reshape(sources, slots), "expert", split_axis=0, concat_axis=0, tiled=True
    )
    picked_f = jnp.take(back_f.reshape(expert_count * capacity, model_width), target_f, axis=0)
    picked_f = picked_f.reshape(tok_count, top_count, model_width).astype(jnp.float32)
    layer_out = (
        acts_f.astype(jnp.float32) + jnp.sum(gates_f[:, :, None] * picked_f, axis=1)
    ).astype(jnp.bfloat16)
    fwd_next = shifted(layer_out[None], "section", 1)
    pair_grads = jnp.take(back_rows.reshape(expert_count * capacity, model_width), target_b, axis=0)
    pair_grads = pair_grads.reshape(tok_count, top_count, model_width).astype(jnp.float32)
    dgate = (
        jnp.take(back_gates.reshape(-1), target_b, axis=0)
        .reshape(tok_count, top_count)
        .astype(jnp.float32)
    )
    d_input = input_gradient(
        gates_b, dgate, pair_grads, routes_b, router, unit_b, factor_b, gain_row, grads_b
    )
    grad_prev = shifted(d_input[None], "section", -1)
    return (fwd_next, grad_prev)


AXES = ("section", "expert")
SQUARE = 8
CORE, HALF, SECTION = 1, 8, 16
LANES = 128


def swapped(block, distance):
    count = lax.axis_size(AXES)
    return lax.ppermute(block, AXES, [(i, i ^ distance) for i in range(count)])


def expert_kernel(
    where_ref, near_ref, far_ref, gain_ref, gain_far_ref, router_ref,
    gate_hbm, up_hbm, down_hbm, kept_ref, sent_ref,
    gate_ref, up_ref, down_ref, sems,
):
    width = gain_ref.shape[1]
    hidden_count = gate_ref.shape[1]
    step = 256 if hidden_count % 256 == 0 else hidden_count
    pieces = hidden_count // step
    copies = []
    for piece in range(pieces):
        cols = pl.ds(piece * step, step)
        copies.append((
            pltpu.make_async_copy(gate_hbm.at[:, cols], gate_ref.at[:, cols], sems.at[0, piece]),
            pltpu.make_async_copy(up_hbm.at[:, cols], up_ref.at[:, cols], sems.at[1, piece]),
            pltpu.make_async_copy(down_hbm.at[cols, :], down_ref.at[cols, :], sems.at[2, piece]),
        ))
        for copy in copies[-1]:
            copy.start()

    first_section = where_ref[0] == 0
    own_expert = where_ref[1]
    gain_here = gain_ref[...]
    gain_there = gain_far_ref[...]
    gain_f = jnp.where(first_section, gain_here, gain_there)
    gain_b = jnp.where(first_section, gain_there, gain_here)

    chunks = []
    for ref in (near_ref, far_ref):
        rows = ref[...].astype(jnp.float32)
        chunks += [rows[24 * k : 24 * k + 24] for k in range(SQUARE // 2)]
    acts = jnp.concatenate([c[0:8] for c in chunks] + [c[8:16] for c in chunks], axis=0)
    grads = jnp.concatenate([c[16:24, :width] for c in chunks], axis=0)
    routes = acts[:, width:]
    acts = acts[:, :width]
    half = acts.shape[0] // 2

    factor = lax.rsqrt(jnp.mean(acts * acts, axis=-1, keepdims=True) + EPSILON)
    unit = acts * factor
    normed = jnp.concatenate([unit[:half] * gain_f, unit[half:] * gain_b], axis=0)
    normed = normed.astype(jnp.bfloat16)
    grads_low = grads.astype(jnp.bfloat16)

    router = router_ref[...]
    experts = router.shape[1]
    logits = jnp.dot(normed, router, preferred_element_type=jnp.float32)
    labels = lax.broadcasted_iota(jnp.int32, logits.shape, 1)
    labels_real = labels.astype(jnp.float32)
    chosen = routes[:, 0:1] == labels_real
    for k in range(1, TOP_COUNT):
        chosen = jnp.logical_or(chosen, routes[:, k : k + 1] == labels_real)
    raised = jnp.where(chosen, jnp.exp(logits), 0.0)
    gates = raised / jnp.sum(raised, axis=-1, keepdims=True)
    own = labels == own_expert
    gate_own = jnp.sum(jnp.where(own, gates, 0.0), axis=-1, keepdims=True)

    contract = (((1,), (1,)), ((), ()))
    expert_out = None
    pair_grad = None
    for piece in range(pieces):
        cols = slice(piece * step, piece * step + step)
        for copy in copies[piece]:
            copy.wait()
        gate_mat = gate_ref[:, cols]
        up_mat = up_ref[:, cols]
        down_mat = down_ref[cols, :]
        pre_gate = jnp.dot(normed, gate_mat, preferred_element_type=jnp.float32)
        pre_up = jnp.dot(normed, up_mat, preferred_element_type=jnp.float32)
        sigma = jax.nn.sigmoid(pre_gate)
        silu_val = pre_gate * sigma
        hidden = (silu_val * pre_up).astype(jnp.bfloat16)
        part = jnp.dot(hidden, down_mat, preferred_element_type=jnp.float32)
        expert_out = part if expert_out is None else expert_out + part
        d_hidden = lax.dot_general(
            grads_low, down_mat, contract, preferred_element_type=jnp.float32
        )
        d_up = (d_hidden * silu_val[half:]).astype(jnp.bfloat16)
        sigma_b = sigma[half:]
        slope = sigma_b * (1.0 + pre_gate[half:] * (1.0 - sigma_b))
        d_pre = (d_hidden * pre_up[half:] * slope).astype(jnp.bfloat16)
        part = lax.dot_general(d_pre, gate_mat, contract, preferred_element_type=jnp.float32)
        part = part + lax.dot_general(d_up, up_mat, contract, preferred_element_type=jnp.float32)
        pair_grad = part if pair_grad is None else pair_grad + part

    out_f = gate_own[:half] * expert_out[:half]
    dgate = jnp.sum(grads * expert_out[half:], axis=-1, keepdims=True)
    gate_b = gate_own[half:]
    spread = gate_b * dgate * (jnp.where(own[half:], 1.0, 0.0) - gates[half:])
    spread_high = spread.astype(jnp.bfloat16)
    spread_low = (spread - spread_high.astype(jnp.float32)).astype(jnp.bfloat16)
    d_normed = gate_b * pair_grad
    d_normed = d_normed + lax.dot_general(
        spread_high, router, contract, preferred_element_type=jnp.float32
    )
    d_normed = d_normed + lax.dot_general(
        spread_low, router, contract, preferred_element_type=jnp.float32
    )
    d_unit = d_normed * gain_b
    unit_b = unit[half:]
    out_b = factor[half:] * (
        d_unit - unit_b * jnp.mean(d_unit * unit_b, axis=-1, keepdims=True)
    )

    head_f = out_f[0:8] + jnp.where(first_section, 0.0, acts[0:8])
    head_b = out_b[0:8] + jnp.where(first_section, grads[0:8], 0.0)
    parts = []
    for k in range(SQUARE):
        parts.append(head_f if k == 0 else out_f[8 * k : 8 * k + 8])
        parts.append(head_b if k == 0 else out_b[8 * k : 8 * k + 8])
    kept_ref[...] = jnp.concatenate(parts[:SQUARE], axis=0).astype(jnp.bfloat16)
    sent_ref[...] = jnp.concatenate(parts[SQUARE:], axis=0).astype(jnp.bfloat16)


TOP_COUNT = 8


def run_experts(where, near, far, gain_row, gain_far, router, gate_mat, up_mat, down_mat):
    width, hidden_count = gate_mat.shape
    rows = SQUARE // 2 * 16
    vmem = pl.BlockSpec(memory_space=pltpu.VMEM)
    hbm = pl.BlockSpec(memory_space=pl.ANY)
    return pl.pallas_call(
        expert_kernel,
        out_shape=[jax.ShapeDtypeStruct((rows, width), jnp.bfloat16)] * 2,
        in_specs=[pl.BlockSpec(memory_space=pltpu.SMEM)] + [vmem] * 5 + [hbm] * 3,
        out_specs=[vmem] * 2,
        scratch_shapes=[
            pltpu.VMEM((width, hidden_count), jnp.bfloat16),
            pltpu.VMEM((width, hidden_count), jnp.bfloat16),
            pltpu.VMEM((hidden_count, width), jnp.bfloat16),
            pltpu.SemaphoreType.DMA((3, max(1, hidden_count // 256))),
        ],
        compiler_params=pltpu.CompilerParams(vmem_limit_bytes=40 * 1024 * 1024),
        name="experts",
    )(where, near, far, gain_row, gain_far, router, gate_mat, up_mat, down_mat)


def added(*blocks):
    return sum(block.astype(jnp.float32) for block in blocks)


def paired_plan(
    fwd_act, fwd_routes, bwd_saved, bwd_grad, bwd_routes, norm_gain, router, w_gate, w_up, w_down
):
    section = lax.axis_index("section")
    first = section == 0
    where = jnp.stack([section, lax.axis_index("expert")]).astype(jnp.int32)

    acts = jnp.where(first, fwd_act[0], bwd_saved[0])
    routes = jnp.where(first, fwd_routes[0], bwd_routes[0]).astype(jnp.bfloat16)
    tail = jnp.pad(routes, ((0, 0), (0, LANES - routes.shape[1])))
    own_rows = jnp.concatenate(
        [
            jnp.concatenate([acts, tail], axis=1),
            jnp.pad(bwd_grad[0], ((0, 0), (0, LANES))),
        ],
        axis=0,
    )
    across = swapped(own_rows, SECTION)
    along = swapped(own_rows, HALF)
    gain_far = swapped(norm_gain, SECTION)
    forward = jnp.where(first, along[:8], across[:8])
    backward = jnp.where(first, across, along)
    mine = jnp.concatenate([forward, backward], axis=0)
    near = jnp.concatenate([mine] + [swapped(mine, k) for k in (2, 4, 6)], axis=0)
    far = swapped(near, CORE)

    kept, sent = run_experts(
        where, near, far, norm_gain, gain_far, router, w_gate[0], w_up[0], w_down[0]
    )

    chip = added(kept, swapped(sent, CORE)).astype(jnp.bfloat16)
    total = added(
        chip[0:16], swapped(chip[16:32], 2), swapped(chip[32:48], 4), swapped(chip[48:64], 6)
    )
    total = total.astype(jnp.bfloat16)
    leaving = jnp.where(first, total[:8], total[8:])
    staying = jnp.where(first, total[8:], total[:8])
    result = added(staying, swapped(leaving, SECTION + HALF)).astype(jnp.bfloat16)
    nothing = jnp.zeros_like(result)
    fwd_next = jnp.where(first, nothing, result)[None]
    grad_prev = jnp.where(first, result, nothing)[None]
    return (fwd_next, grad_prev)


def solution(mesh):
    in_specs = (
        P("section", "expert", None),
        P("section", "expert", None),
        P("section", "expert", None),
        P("section", "expert", None),
        P("section", "expert", None),
        P("section", None),
        P(),
        P("expert", None, None),
        P("expert", None, None),
        P("expert", None, None),
    )
    out_specs = (P("section", "expert", None), P("section", "expert", None))
    shape = dict(mesh.shape)
    paired = shape["section"] == 2 and shape["expert"] == 2 * SQUARE
    return jax.shard_map(
        paired_plan if paired else routed_plan, mesh=mesh, in_specs=in_specs, out_specs=out_specs, check_vma=False
    )
```

```python
import jax
import jax.numpy as jnp
from jax import lax
from jax.experimental import pallas as pl
from jax.experimental.pallas import tpu as pltpu
from jax.sharding import PartitionSpec as P

EPSILON = 1e-06


def shifted(block, axis, distance):
    devices = range(lax.axis_size(axis))
    route = [(i - distance, i) for i in devices if i - distance in devices]
    return lax.ppermute(block, axis, route)


def normalize(acts_in, gain_row):
    values = acts_in.astype(jnp.float32)
    factor = lax.rsqrt(jnp.mean(values * values, axis=-1, keepdims=True) + EPSILON)
    unit_rows = values * factor
    return ((unit_rows * gain_row).astype(jnp.bfloat16), unit_rows, factor)


def gate_values(normed, router, routes):
    logits = jnp.dot(normed, router, preferred_element_type=jnp.float32)
    chosen = jnp.take_along_axis(logits, routes, axis=1)
    raised = jnp.exp(chosen)
    return raised / jnp.sum(raised, axis=-1, keepdims=True)


def expert_forward(rows_in, gate_mat, up_mat, down_mat):
    pre_gate = jnp.dot(rows_in, gate_mat, preferred_element_type=jnp.float32)
    pre_up = jnp.dot(rows_in, up_mat, preferred_element_type=jnp.float32)
    sigma = jax.nn.sigmoid(pre_gate)
    hidden = (pre_gate * sigma * pre_up).astype(jnp.bfloat16)
    return jnp.dot(hidden, down_mat, preferred_element_type=jnp.float32).astype(jnp.bfloat16)


def expert_backward(rows_in, grads_in, gate_mat, up_mat, down_mat):
    pre_gate = jnp.dot(rows_in, gate_mat, preferred_element_type=jnp.float32)
    pre_up = jnp.dot(rows_in, up_mat, preferred_element_type=jnp.float32)
    sigma = jax.nn.sigmoid(pre_gate)
    silu_val = pre_gate * sigma
    hidden = (silu_val * pre_up).astype(jnp.bfloat16)
    expert_out = jnp.dot(hidden, down_mat, preferred_element_type=jnp.float32).astype(jnp.bfloat16)
    dgate = jnp.sum(grads_in.astype(jnp.float32) * expert_out.astype(jnp.float32), axis=-1).astype(
        jnp.bfloat16
    )
    contract = (((1,), (1,)), ((), ()))
    d_hidden = lax.dot_general(grads_in, down_mat, contract, preferred_element_type=jnp.float32)
    d_up = (d_hidden * silu_val).astype(jnp.bfloat16)
    d_pre = (d_hidden * pre_up * sigma * (1.0 + pre_gate * (1.0 - sigma))).astype(jnp.bfloat16)
    d_rows = lax.dot_general(d_pre, gate_mat, contract, preferred_element_type=jnp.float32)
    d_rows = d_rows + lax.dot_general(d_up, up_mat, contract, preferred_element_type=jnp.float32)
    return (d_rows.astype(jnp.bfloat16), dgate)


def input_gradient(gates, dgate, pair_grads, routes, router, unit_rows, factor, gain_row, grads_in):
    d_normed = jnp.sum(gates[:, :, None] * pair_grads, axis=1)
    d_chosen = gates * (dgate - jnp.sum(gates * dgate, axis=-1, keepdims=True))
    labels = jnp.arange(router.shape[1], dtype=jnp.int32)
    hits = (routes[:, :, None] == labels[None, None, :]).astype(jnp.float32)
    d_logits = jnp.sum(hits * d_chosen[:, :, None], axis=1)
    d_normed = d_normed + lax.dot_general(
        d_logits,
        router.astype(jnp.float32),
        (((1,), (1,)), ((), ())),
        precision=lax.Precision.HIGHEST,
    )
    d_unit = d_normed * gain_row
    result = factor * (d_unit - unit_rows * jnp.mean(d_unit * unit_rows, axis=-1, keepdims=True))
    return (result + grads_in.astype(jnp.float32)).astype(jnp.bfloat16)


def placement(routes, expert_count, capacity):
    flat_ids = routes.reshape(-1)
    labels = jnp.arange(expert_count, dtype=jnp.int32)
    onehot = (flat_ids[:, None] == labels[None, :]).astype(jnp.int32)
    before = jnp.cumsum(onehot, axis=0) - onehot
    slot_ids = jnp.sum(before * onehot, axis=1)
    target = flat_ids * capacity + slot_ids
    slot_labels = jnp.arange(expert_count * capacity, dtype=jnp.int32)
    select = (slot_labels[:, None] == target[None, :]).astype(jnp.bfloat16)
    spread = jnp.sum(
        select.reshape(expert_count * capacity, routes.shape[0], routes.shape[1]), axis=2
    )
    return (target, spread)


def dispatch(spread, rows_in, expert_count, capacity):
    placed = jnp.dot(spread, rows_in, preferred_element_type=jnp.float32).astype(jnp.bfloat16)
    return placed.reshape(expert_count, capacity, rows_in.shape[1])


def routed_plan(
    fwd_act, fwd_routes, bwd_saved, bwd_grad, bwd_routes, norm_gain, router, w_gate, w_up, w_down
):
    tok_count = fwd_act.shape[1]
    top_count = fwd_routes.shape[2]
    model_width = fwd_act.shape[2]
    expert_count = router.shape[1]
    capacity = min(tok_count, max(2, 2 * tok_count * top_count // expert_count))
    gain_row = norm_gain[0]
    gate_mat = w_gate[0]
    up_mat = w_up[0]
    down_mat = w_down[0]
    acts_f = fwd_act[0]
    routes_f = fwd_routes[0]
    normed_f, unused_unit, unused_factor = normalize(acts_f, gain_row)
    gates_f = gate_values(normed_f, router, routes_f)
    target_f, spread_f = placement(routes_f, expert_count, capacity)
    send_f = dispatch(spread_f, normed_f, expert_count, capacity)
    saved_b = bwd_saved[0]
    grads_b = bwd_grad[0]
    routes_b = bwd_routes[0]
    normed_b, unit_b, factor_b = normalize(saved_b, gain_row)
    gates_b = gate_values(normed_b, router, routes_b)
    target_b, spread_b = placement(routes_b, expert_count, capacity)
    send_x = dispatch(spread_b, normed_b, expert_count, capacity)
    send_g = dispatch(spread_b, grads_b, expert_count, capacity)
    rows_in = lax.all_to_all(send_f, "expert", split_axis=0, concat_axis=0, tiled=True)
    sources = rows_in.shape[0]
    slots = rows_in.shape[1]
    result = expert_forward(rows_in.reshape(-1, model_width), gate_mat, up_mat, down_mat)
    back_f = lax.all_to_all(
        result.reshape(sources, slots, model_width),
        "expert",
        split_axis=0,
        concat_axis=0,
        tiled=True,
    )
    rows_in = lax.all_to_all(send_x, "expert", split_axis=0, concat_axis=0, tiled=True)
    grads_in = lax.all_to_all(send_g, "expert", split_axis=0, concat_axis=0, tiled=True)
    sources = rows_in.shape[0]
    slots = rows_in.shape[1]
    d_rows, d_gates = expert_backward(
        rows_in.reshape(-1, model_width),
        grads_in.reshape(-1, model_width),
        gate_mat,
        up_mat,
        down_mat,
    )
    back_rows = lax.all_to_all(
        d_rows.reshape(sources, slots, model_width),
        "expert",
        split_axis=0,
        concat_axis=0,
        tiled=True,
    )
    back_gates = lax.all_to_all(
        d_gates.reshape(sources, slots), "expert", split_axis=0, concat_axis=0, tiled=True
    )
    picked_f = jnp.take(back_f.reshape(expert_count * capacity, model_width), target_f, axis=0)
    picked_f = picked_f.reshape(tok_count, top_count, model_width).astype(jnp.float32)
    layer_out = (
        acts_f.astype(jnp.float32) + jnp.sum(gates_f[:, :, None] * picked_f, axis=1)
    ).astype(jnp.bfloat16)
    fwd_next = shifted(layer_out[None], "section", 1)
    pair_grads = jnp.take(back_rows.reshape(expert_count * capacity, model_width), target_b, axis=0)
    pair_grads = pair_grads.reshape(tok_count, top_count, model_width).astype(jnp.float32)
    dgate = (
        jnp.take(back_gates.reshape(-1), target_b, axis=0)
        .reshape(tok_count, top_count)
        .astype(jnp.float32)
    )
    d_input = input_gradient(
        gates_b, dgate, pair_grads, routes_b, router, unit_b, factor_b, gain_row, grads_b
    )
    grad_prev = shifted(d_input[None], "section", -1)
    return (fwd_next, grad_prev)


AXES = ("section", "expert")
SQUARE = 8
CORE, HALF, SECTION = 1, 8, 16
LANES = 128


def swapped(block, distance):
    count = lax.axis_size(AXES)
    return lax.ppermute(block, AXES, [(i, i ^ distance) for i in range(count)])


def expert_kernel(
    where_ref, near_ref, far_ref, across_ref, gain_ref, router_ref,
    gate_ref, up_ref, down_ref, kept_ref, sent_ref,
):
    width = gain_ref.shape[1]
    hidden_count = gate_ref.shape[1]
    step = 256 if hidden_count % 256 == 0 else hidden_count
    pieces = hidden_count // step
    first_section = where_ref[0] == 0
    own_expert = where_ref[1]
    gain_here = gain_ref[...]
    packed = across_ref[...].astype(jnp.float32)[:, width + LANES :]
    packed = packed[:, :LANES] + packed[:, LANES:]
    gain_there = jnp.concatenate([packed[k : k + 1] for k in range(16)], axis=1)
    gain_f = jnp.where(first_section, gain_here, gain_there)
    gain_b = jnp.where(first_section, gain_there, gain_here)

    chunks = []
    for ref in (near_ref, far_ref):
        rows = ref[...].astype(jnp.float32)
        chunks += [rows[24 * k : 24 * k + 24] for k in range(SQUARE // 2)]
    acts = jnp.concatenate([c[0:8] for c in chunks] + [c[8:16] for c in chunks], axis=0)
    grads = jnp.concatenate([c[16:24, :width] for c in chunks], axis=0)
    routes = acts[:, width:]
    acts = acts[:, :width]
    half = acts.shape[0] // 2

    factor = lax.rsqrt(jnp.mean(acts * acts, axis=-1, keepdims=True) + EPSILON)
    unit = acts * factor
    normed = jnp.concatenate([unit[:half] * gain_f, unit[half:] * gain_b], axis=0)
    normed = normed.astype(jnp.bfloat16)
    grads_low = grads.astype(jnp.bfloat16)

    router = router_ref[...]
    contract = (((1,), (1,)), ((), ()))
    logits = lax.dot_general(normed, router, contract, preferred_element_type=jnp.float32)
    labels = lax.broadcasted_iota(jnp.int32, logits.shape, 1)
    labels_real = labels.astype(jnp.float32)
    chosen = routes[:, 0:1] == labels_real
    for k in range(1, TOP_COUNT):
        chosen = jnp.logical_or(chosen, routes[:, k : k + 1] == labels_real)
    raised = jnp.where(chosen, jnp.exp(logits), 0.0)
    gates = raised / jnp.sum(raised, axis=-1, keepdims=True)
    own = labels == own_expert
    gate_own = jnp.sum(jnp.where(own, gates, 0.0), axis=-1, keepdims=True)

    expert_out = None
    pair_grad = None
    for piece in range(pieces):
        cols = slice(piece * step, piece * step + step)
        gate_mat = gate_ref[:, cols]
        up_mat = up_ref[:, cols]
        down_mat = down_ref[cols, :]
        pre_gate = jnp.dot(normed, gate_mat, preferred_element_type=jnp.float32)
        pre_up = jnp.dot(normed, up_mat, preferred_element_type=jnp.float32)
        sigma = jax.nn.sigmoid(pre_gate)
        silu_val = pre_gate * sigma
        hidden = (silu_val * pre_up).astype(jnp.bfloat16)
        part = jnp.dot(hidden, down_mat, preferred_element_type=jnp.float32)
        expert_out = part if expert_out is None else expert_out + part
        d_hidden = lax.dot_general(
            grads_low, down_mat, contract, preferred_element_type=jnp.float32
        )
        d_up = (d_hidden * silu_val[half:]).astype(jnp.bfloat16)
        sigma_b = sigma[half:]
        slope = sigma_b * (1.0 + pre_gate[half:] * (1.0 - sigma_b))
        d_pre = (d_hidden * pre_up[half:] * slope).astype(jnp.bfloat16)
        part = lax.dot_general(d_pre, gate_mat, contract, preferred_element_type=jnp.float32)
        part = part + lax.dot_general(d_up, up_mat, contract, preferred_element_type=jnp.float32)
        pair_grad = part if pair_grad is None else pair_grad + part

    out_f = gate_own[:half] * expert_out[:half]
    dgate = jnp.sum(grads * expert_out[half:], axis=-1, keepdims=True)
    gate_b = gate_own[half:]
    spread = gate_b * dgate * (jnp.where(own[half:], 1.0, 0.0) - gates[half:])
    spread_high = spread.astype(jnp.bfloat16)
    spread_low = (spread - spread_high.astype(jnp.float32)).astype(jnp.bfloat16)
    d_normed = gate_b * pair_grad
    d_normed = d_normed + jnp.dot(spread_high, router, preferred_element_type=jnp.float32)
    d_normed = d_normed + jnp.dot(spread_low, router, preferred_element_type=jnp.float32)
    d_unit = d_normed * gain_b
    unit_b = unit[half:]
    out_b = factor[half:] * (
        d_unit - unit_b * jnp.mean(d_unit * unit_b, axis=-1, keepdims=True)
    )

    head_f = out_f[0:8] + jnp.where(first_section, 0.0, acts[0:8])
    head_b = out_b[0:8] + jnp.where(first_section, grads[0:8], 0.0)
    parts = []
    for k in range(SQUARE):
        parts.append(head_f if k == 0 else out_f[8 * k : 8 * k + 8])
        parts.append(head_b if k == 0 else out_b[8 * k : 8 * k + 8])
    kept_ref[...] = jnp.concatenate(parts[:SQUARE], axis=0).astype(jnp.bfloat16)
    sent_ref[...] = jnp.concatenate(parts[SQUARE:], axis=0).astype(jnp.bfloat16)


TOP_COUNT = 8


def in_hbm(array):
    return pltpu.with_memory_space_constraint(array, pltpu.HBM)


def pack_kernel(
    where_ref, fwd_act, fwd_routes, bwd_saved, bwd_grad, bwd_routes, gain, router,
    rows_ref, gain_ref, router_ref, acts_ref, grads_ref, routes_ref, sems,
):
    first_section = where_ref[0] == 0
    grad_copy = pltpu.make_async_copy(bwd_grad.at[0], grads_ref, sems.at[0])
    gain_copy = pltpu.make_async_copy(gain, gain_ref, sems.at[1])
    router_copy = pltpu.make_async_copy(router, router_ref, sems.at[4])
    grad_copy.start()
    gain_copy.start()
    router_copy.start()

    @pl.when(first_section)
    def _():
        pltpu.make_async_copy(fwd_act.at[0], acts_ref, sems.at[2]).start()
        pltpu.make_async_copy(fwd_routes.at[0], routes_ref, sems.at[3]).start()

    @pl.when(jnp.logical_not(first_section))
    def _():
        pltpu.make_async_copy(bwd_saved.at[0], acts_ref, sems.at[2]).start()
        pltpu.make_async_copy(bwd_routes.at[0], routes_ref, sems.at[3]).start()

    grad_copy.wait()
    gain_copy.wait()
    router_copy.wait()
    pltpu.make_async_copy(fwd_act.at[0], acts_ref, sems.at[2]).wait()
    pltpu.make_async_copy(fwd_routes.at[0], routes_ref, sems.at[3]).wait()

    body = jnp.concatenate(
        [acts_ref[...].astype(jnp.float32), grads_ref[...].astype(jnp.float32)], axis=0
    )
    rows = body.shape[0]
    routes = routes_ref[...].astype(jnp.float32)
    routes = jnp.concatenate([routes, jnp.zeros((8, LANES - TOP_COUNT), jnp.float32)], axis=1)
    tail = jnp.concatenate([routes, jnp.zeros((rows - 8, LANES), jnp.float32)], axis=0)
    gain_row = gain_ref[...]
    gain_rows = jnp.concatenate(
        [gain_row[:, LANES * k : LANES * k + LANES] for k in range(rows)], axis=0
    )
    gain_high = gain_rows.astype(jnp.bfloat16).astype(jnp.float32)
    rows_ref[...] = jnp.concatenate(
        [body, tail, gain_high, gain_rows - gain_high], axis=1
    ).astype(jnp.bfloat16)


def pack_rows(where, *arrays):
    fwd_act, fwd_routes, _, _, _, gain, router = arrays
    count, width = fwd_act.shape[1:]
    vmem = pl.BlockSpec(memory_space=pltpu.VMEM)
    return pl.pallas_call(
        pack_kernel,
        out_shape=[
            jax.ShapeDtypeStruct((2 * count, width + 3 * LANES), jnp.bfloat16),
            jax.ShapeDtypeStruct(gain.shape, gain.dtype),
            jax.ShapeDtypeStruct(router.shape, router.dtype),
        ],
        in_specs=[pl.BlockSpec(memory_space=pltpu.SMEM)]
        + [pl.BlockSpec(memory_space=pltpu.HBM)] * 7,
        out_specs=[vmem] * 3,
        scratch_shapes=[
            pltpu.VMEM((count, width), jnp.bfloat16),
            pltpu.VMEM((count, width), jnp.bfloat16),
            pltpu.VMEM(fwd_routes.shape[1:], jnp.int32),
            pltpu.SemaphoreType.DMA((5,)),
        ],
        compiler_params=pltpu.CompilerParams(vmem_limit_bytes=4 * 1024 * 1024),
        name="pack",
    )(where, *[in_hbm(x) for x in arrays])


def fetch_kernel(weights, held_ref, sem):
    copy = pltpu.make_async_copy(weights, held_ref, sem)
    copy.start()
    copy.wait()


def fetched(weights):
    return pl.pallas_call(
        fetch_kernel,
        out_shape=jax.ShapeDtypeStruct(weights.shape, weights.dtype),
        in_specs=[pl.BlockSpec(memory_space=pltpu.HBM)],
        out_specs=pl.BlockSpec(memory_space=pltpu.VMEM),
        scratch_shapes=[pltpu.SemaphoreType.DMA],
        compiler_params=pltpu.CompilerParams(vmem_limit_bytes=4 * 1024 * 1024),
        cost_estimate=pl.CostEstimate(
            flops=0, bytes_accessed=2 * weights.size * weights.dtype.itemsize, transcendentals=0
        ),
        name="fetch",
    )(in_hbm(weights))


def run_experts(where, near, far, across, gain_row, router, gate_mat, up_mat, down_mat):
    width = gate_mat.shape[0]
    rows = SQUARE // 2 * 16
    vmem = pl.BlockSpec(memory_space=pltpu.VMEM)
    return pl.pallas_call(
        expert_kernel,
        out_shape=[jax.ShapeDtypeStruct((rows, width), jnp.bfloat16)] * 2,
        in_specs=[pl.BlockSpec(memory_space=pltpu.SMEM)] + [vmem] * 8,
        out_specs=[vmem] * 2,
        compiler_params=pltpu.CompilerParams(vmem_limit_bytes=32 * 1024 * 1024),
        name="experts",
    )(where, near, far, across, gain_row, router, gate_mat, up_mat, down_mat)


def added(*blocks):
    return sum(block.astype(jnp.float32) for block in blocks)


def paired_plan(
    fwd_act, fwd_routes, bwd_saved, bwd_grad, bwd_routes, norm_gain, router, w_gate, w_up, w_down
):
    section = lax.axis_index("section")
    first = section == 0
    where = jnp.stack([section, lax.axis_index("expert")]).astype(jnp.int32)

    own_rows, gain_row, router_rows = pack_rows(
        where, fwd_act, fwd_routes, bwd_saved, bwd_grad, bwd_routes, norm_gain, router.T
    )
    across = swapped(own_rows, SECTION)
    along = swapped(own_rows, HALF)
    gate_mat, up_mat = fetched(w_gate[0]), fetched(w_up[0])
    used = norm_gain.shape[1] + LANES
    forward = jnp.where(first, along[:8, :used], across[:8, :used])
    backward = jnp.where(first, across[:, :used], along[:, :used])
    mine = jnp.concatenate([forward, backward], axis=0)
    mine, gate_mat, up_mat = lax.optimization_barrier((mine, gate_mat, up_mat))
    down_mat = fetched(lax.optimization_barrier((w_down[0], mine))[0])
    near = jnp.concatenate([mine] + [swapped(mine, k) for k in (2, 4, 6)], axis=0)
    near, down_mat = lax.optimization_barrier((near, down_mat))
    far = swapped(near, CORE)

    kept, sent = run_experts(where, near, far, across, gain_row, router_rows, gate_mat, up_mat, down_mat)

    chip = added(kept, swapped(sent, CORE)).astype(jnp.bfloat16)
    total = added(
        chip[0:16], swapped(chip[16:32], 2), swapped(chip[32:48], 4), swapped(chip[48:64], 6)
    )
    total = total.astype(jnp.bfloat16)
    leaving = jnp.where(first, total[:8], total[8:])
    staying = jnp.where(first, total[8:], total[:8])
    result = added(staying, swapped(leaving, SECTION + HALF)).astype(jnp.bfloat16)
    nothing = jnp.zeros_like(result)
    fwd_next = jnp.where(first, nothing, result)[None]
    grad_prev = jnp.where(first, result, nothing)[None]
    return (fwd_next, grad_prev)


def per_device(fwd_act, fwd_routes, *rest):
    sections, devices = lax.axis_size("section"), lax.axis_size("expert")
    tokens, top_count = fwd_routes.shape[1:]
    router = rest[4]
    paired = sections == 2 and devices == 2 * SQUARE and router.shape == (16 * LANES, devices)
    paired = paired and tokens == 8 and top_count == TOP_COUNT
    plan = paired_plan if paired else routed_plan
    return plan(fwd_act, fwd_routes, *rest)


def solution(mesh):
    in_specs = (
        P("section", "expert", None),
        P("section", "expert", None),
        P("section", "expert", None),
        P("section", "expert", None),
        P("section", "expert", None),
        P("section", None),
        P(),
        P("expert", None, None),
        P("expert", None, None),
        P("expert", None, None),
    )
    out_specs = (P("section", "expert", None), P("section", "expert", None))
    return jax.shard_map(
        per_device, mesh=mesh, in_specs=in_specs, out_specs=out_specs, check_vma=False
    )
```

```python
import functools
import jax
import jax.numpy as jnp
from jax import lax
from jax.experimental import pallas as pl
from jax.experimental.pallas import tpu as pltpu
from jax.sharding import PartitionSpec as P

EPSILON = 1e-06


def shifted(block, axis, distance):
    devices = range(lax.axis_size(axis))
    route = [(i - distance, i) for i in devices if i - distance in devices]
    return lax.ppermute(block, axis, route)


def normalize(acts_in, gain_row):
    values = acts_in.astype(jnp.float32)
    factor = lax.rsqrt(jnp.mean(values * values, axis=-1, keepdims=True) + EPSILON)
    unit_rows = values * factor
    return ((unit_rows * gain_row).astype(jnp.bfloat16), unit_rows, factor)


def gate_values(normed, router, routes):
    logits = jnp.dot(normed, router, preferred_element_type=jnp.float32)
    chosen = jnp.take_along_axis(logits, routes, axis=1)
    raised = jnp.exp(chosen)
    return raised / jnp.sum(raised, axis=-1, keepdims=True)


def expert_forward(rows_in, gate_mat, up_mat, down_mat):
    pre_gate = jnp.dot(rows_in, gate_mat, preferred_element_type=jnp.float32)
    pre_up = jnp.dot(rows_in, up_mat, preferred_element_type=jnp.float32)
    sigma = jax.nn.sigmoid(pre_gate)
    hidden = (pre_gate * sigma * pre_up).astype(jnp.bfloat16)
    return jnp.dot(hidden, down_mat, preferred_element_type=jnp.float32).astype(jnp.bfloat16)


def expert_backward(rows_in, grads_in, gate_mat, up_mat, down_mat):
    pre_gate = jnp.dot(rows_in, gate_mat, preferred_element_type=jnp.float32)
    pre_up = jnp.dot(rows_in, up_mat, preferred_element_type=jnp.float32)
    sigma = jax.nn.sigmoid(pre_gate)
    silu_val = pre_gate * sigma
    hidden = (silu_val * pre_up).astype(jnp.bfloat16)
    expert_out = jnp.dot(hidden, down_mat, preferred_element_type=jnp.float32).astype(jnp.bfloat16)
    dgate = jnp.sum(grads_in.astype(jnp.float32) * expert_out.astype(jnp.float32), axis=-1).astype(
        jnp.bfloat16
    )
    contract = (((1,), (1,)), ((), ()))
    d_hidden = lax.dot_general(grads_in, down_mat, contract, preferred_element_type=jnp.float32)
    d_up = (d_hidden * silu_val).astype(jnp.bfloat16)
    d_pre = (d_hidden * pre_up * sigma * (1.0 + pre_gate * (1.0 - sigma))).astype(jnp.bfloat16)
    d_rows = lax.dot_general(d_pre, gate_mat, contract, preferred_element_type=jnp.float32)
    d_rows = d_rows + lax.dot_general(d_up, up_mat, contract, preferred_element_type=jnp.float32)
    return (d_rows.astype(jnp.bfloat16), dgate)


def input_gradient(gates, dgate, pair_grads, routes, router, unit_rows, factor, gain_row, grads_in):
    d_normed = jnp.sum(gates[:, :, None] * pair_grads, axis=1)
    d_chosen = gates * (dgate - jnp.sum(gates * dgate, axis=-1, keepdims=True))
    labels = jnp.arange(router.shape[1], dtype=jnp.int32)
    hits = (routes[:, :, None] == labels[None, None, :]).astype(jnp.float32)
    d_logits = jnp.sum(hits * d_chosen[:, :, None], axis=1)
    d_normed = d_normed + lax.dot_general(
        d_logits,
        router.astype(jnp.float32),
        (((1,), (1,)), ((), ())),
        precision=lax.Precision.HIGHEST,
    )
    d_unit = d_normed * gain_row
    result = factor * (d_unit - unit_rows * jnp.mean(d_unit * unit_rows, axis=-1, keepdims=True))
    return (result + grads_in.astype(jnp.float32)).astype(jnp.bfloat16)


def placement(routes, expert_count, capacity):
    flat_ids = routes.reshape(-1)
    labels = jnp.arange(expert_count, dtype=jnp.int32)
    onehot = (flat_ids[:, None] == labels[None, :]).astype(jnp.int32)
    before = jnp.cumsum(onehot, axis=0) - onehot
    slot_ids = jnp.sum(before * onehot, axis=1)
    target = flat_ids * capacity + slot_ids
    slot_labels = jnp.arange(expert_count * capacity, dtype=jnp.int32)
    select = (slot_labels[:, None] == target[None, :]).astype(jnp.bfloat16)
    spread = jnp.sum(
        select.reshape(expert_count * capacity, routes.shape[0], routes.shape[1]), axis=2
    )
    return (target, spread)


def dispatch(spread, rows_in, expert_count, capacity):
    placed = jnp.dot(spread, rows_in, preferred_element_type=jnp.float32).astype(jnp.bfloat16)
    return placed.reshape(expert_count, capacity, rows_in.shape[1])


def routed_plan(
    fwd_act, fwd_routes, bwd_saved, bwd_grad, bwd_routes, norm_gain, router, w_gate, w_up, w_down
):
    tok_count = fwd_act.shape[1]
    top_count = fwd_routes.shape[2]
    model_width = fwd_act.shape[2]
    expert_count = router.shape[1]
    capacity = min(tok_count, max(2, 2 * tok_count * top_count // expert_count))
    gain_row = norm_gain[0]
    gate_mat = w_gate[0]
    up_mat = w_up[0]
    down_mat = w_down[0]
    acts_f = fwd_act[0]
    routes_f = fwd_routes[0]
    normed_f, unused_unit, unused_factor = normalize(acts_f, gain_row)
    gates_f = gate_values(normed_f, router, routes_f)
    target_f, spread_f = placement(routes_f, expert_count, capacity)
    send_f = dispatch(spread_f, normed_f, expert_count, capacity)
    saved_b = bwd_saved[0]
    grads_b = bwd_grad[0]
    routes_b = bwd_routes[0]
    normed_b, unit_b, factor_b = normalize(saved_b, gain_row)
    gates_b = gate_values(normed_b, router, routes_b)
    target_b, spread_b = placement(routes_b, expert_count, capacity)
    send_x = dispatch(spread_b, normed_b, expert_count, capacity)
    send_g = dispatch(spread_b, grads_b, expert_count, capacity)
    rows_in = lax.all_to_all(send_f, "expert", split_axis=0, concat_axis=0, tiled=True)
    sources = rows_in.shape[0]
    slots = rows_in.shape[1]
    result = expert_forward(rows_in.reshape(-1, model_width), gate_mat, up_mat, down_mat)
    back_f = lax.all_to_all(
        result.reshape(sources, slots, model_width),
        "expert",
        split_axis=0,
        concat_axis=0,
        tiled=True,
    )
    rows_in = lax.all_to_all(send_x, "expert", split_axis=0, concat_axis=0, tiled=True)
    grads_in = lax.all_to_all(send_g, "expert", split_axis=0, concat_axis=0, tiled=True)
    sources = rows_in.shape[0]
    slots = rows_in.shape[1]
    d_rows, d_gates = expert_backward(
        rows_in.reshape(-1, model_width),
        grads_in.reshape(-1, model_width),
        gate_mat,
        up_mat,
        down_mat,
    )
    back_rows = lax.all_to_all(
        d_rows.reshape(sources, slots, model_width),
        "expert",
        split_axis=0,
        concat_axis=0,
        tiled=True,
    )
    back_gates = lax.all_to_all(
        d_gates.reshape(sources, slots), "expert", split_axis=0, concat_axis=0, tiled=True
    )
    picked_f = jnp.take(back_f.reshape(expert_count * capacity, model_width), target_f, axis=0)
    picked_f = picked_f.reshape(tok_count, top_count, model_width).astype(jnp.float32)
    layer_out = (
        acts_f.astype(jnp.float32) + jnp.sum(gates_f[:, :, None] * picked_f, axis=1)
    ).astype(jnp.bfloat16)
    fwd_next = shifted(layer_out[None], "section", 1)
    pair_grads = jnp.take(back_rows.reshape(expert_count * capacity, model_width), target_b, axis=0)
    pair_grads = pair_grads.reshape(tok_count, top_count, model_width).astype(jnp.float32)
    dgate = (
        jnp.take(back_gates.reshape(-1), target_b, axis=0)
        .reshape(tok_count, top_count)
        .astype(jnp.float32)
    )
    d_input = input_gradient(
        gates_b, dgate, pair_grads, routes_b, router, unit_b, factor_b, gain_row, grads_b
    )
    grad_prev = shifted(d_input[None], "section", -1)
    return (fwd_next, grad_prev)


AXES = ("section", "expert")
SQUARE = 8
CORE, HALF, SECTION = 1, 8, 16
LANES = 128
TOP_COUNT = 8
VMEM = pl.BlockSpec(memory_space=pltpu.VMEM)
SMEM = pl.BlockSpec(memory_space=pltpu.SMEM)
HBM = pl.BlockSpec(memory_space=pltpu.HBM)
MIB = 1024 * 1024


def swapped(block, distance):
    count = lax.axis_size(AXES)
    return lax.ppermute(block, AXES, [(i, i ^ distance) for i in range(count)])


def in_hbm(array):
    return pltpu.with_memory_space_constraint(array, pltpu.HBM)


def root_factor(values):
    return lax.rsqrt(jnp.mean(values * values, axis=-1, keepdims=True) + EPSILON)


def in_first_section():
    return lax.axis_index("section") == 0


def pack_kernel(
    fwd_act, fwd_routes, bwd_saved, bwd_grad, bwd_routes, gain, router,
    along_ref, acts_ref, gain_ref, router_ref, grads_ref, routes_ref, sems,
):
    first_section = in_first_section()
    grad_copy = pltpu.make_async_copy(bwd_grad.at[0], grads_ref, sems.at[0])
    gain_copy = pltpu.make_async_copy(gain, gain_ref, sems.at[1])
    router_copy = pltpu.make_async_copy(router, router_ref, sems.at[4])

    @pl.when(first_section)
    def _():
        pltpu.make_async_copy(fwd_act.at[0], acts_ref, sems.at[2]).start()
        pltpu.make_async_copy(fwd_routes.at[0], routes_ref, sems.at[3]).start()

    @pl.when(jnp.logical_not(first_section))
    def _():
        pltpu.make_async_copy(bwd_saved.at[0], acts_ref, sems.at[2]).start()
        pltpu.make_async_copy(bwd_routes.at[0], routes_ref, sems.at[3]).start()

    gain_copy.start()
    grad_copy.start()
    router_copy.start()
    pltpu.make_async_copy(fwd_act.at[0], acts_ref, sems.at[2]).wait()
    gain_copy.wait()
    acts = acts_ref[...].astype(jnp.float32)
    normed = acts * root_factor(acts) * gain_ref[...]
    pltpu.make_async_copy(fwd_routes.at[0], routes_ref, sems.at[3]).wait()
    grad_copy.wait()
    routes = routes_ref[...].astype(jnp.float32)
    routes = jnp.concatenate([routes, jnp.zeros((8, LANES - TOP_COUNT), jnp.float32)], axis=1)
    blank = jnp.zeros((8, LANES), jnp.float32)
    grads = grads_ref[...].astype(jnp.float32)
    along_ref[...] = jnp.concatenate(
        [jnp.concatenate([normed, routes], axis=1), jnp.concatenate([grads, blank], axis=1)],
        axis=0,
    ).astype(jnp.bfloat16)
    router_copy.wait()


def pack_rows(*arrays):
    fwd_act, fwd_routes, _, _, _, gain, router = arrays
    count, width = fwd_act.shape[1:]
    return pl.pallas_call(
        pack_kernel,
        out_shape=[
            jax.ShapeDtypeStruct((2 * count, width + LANES), jnp.bfloat16),
            jax.ShapeDtypeStruct((count, width), jnp.bfloat16),
            jax.ShapeDtypeStruct(gain.shape, gain.dtype),
            jax.ShapeDtypeStruct(router.shape, router.dtype),
        ],
        in_specs=[HBM] * 7,
        out_specs=[VMEM] * 4,
        scratch_shapes=[
            pltpu.VMEM((count, width), jnp.bfloat16),
            pltpu.VMEM(fwd_routes.shape[1:], jnp.int32),
            pltpu.SemaphoreType.DMA((5,)),
        ],
        compiler_params=pltpu.CompilerParams(vmem_limit_bytes=4 * MIB),
        name="pack",
    )(*[in_hbm(x) for x in arrays])


def widen_kernel(along_ref, acts_ref, gain_ref, across_ref):
    rows = along_ref[...].astype(jnp.float32)
    acts = acts_ref[...].astype(jnp.float32)
    gain_row = gain_ref[...]
    width = gain_row.shape[1]
    gain_rows = jnp.concatenate(
        [gain_row[:, LANES * k : LANES * k + LANES] for k in range(16)], axis=0
    )
    gain_high = gain_rows.astype(jnp.bfloat16).astype(jnp.float32)
    gain_low = gain_rows - gain_high
    blank = jnp.zeros((8, LANES), jnp.float32)
    across_ref[...] = jnp.concatenate(
        [
            jnp.concatenate([rows[0:8], gain_low[:8]], axis=1),
            jnp.concatenate([rows[8:16, :width], gain_high[:8], gain_low[8:]], axis=1),
            jnp.concatenate([acts, gain_high[8:], blank], axis=1),
        ],
        axis=0,
    ).astype(jnp.bfloat16)


def in_vmem(body, name, out_shape, *arrays):
    return pl.pallas_call(
        body,
        out_shape=out_shape,
        in_specs=[VMEM] * len(arrays),
        out_specs=[VMEM] * len(out_shape),
        compiler_params=pltpu.CompilerParams(vmem_limit_bytes=4 * MIB),
        name=name,
    )(*arrays)


def merge_kernel(along_ref, across_ref, mine_ref):
    first_section = in_first_section()
    used = mine_ref.shape[1]
    along = along_ref[...].astype(jnp.float32)
    across = across_ref[...].astype(jnp.float32)[:, :used]
    mine_ref[...] = jnp.concatenate(
        [
            jnp.where(first_section, along[:8], across[:8]),
            jnp.where(first_section, across[:16], along),
        ],
        axis=0,
    ).astype(jnp.bfloat16)


def leave_kernel(a_ref, b_ref, c_ref, d_ref, leaving_ref, staying_ref):
    first_section = in_first_section()
    total = a_ref[...].astype(jnp.float32) + b_ref[...].astype(jnp.float32)
    total = total + c_ref[...].astype(jnp.float32) + d_ref[...].astype(jnp.float32)
    leaving_ref[...] = jnp.where(first_section, total[:8], total[8:]).astype(jnp.bfloat16)
    staying_ref[...] = jnp.where(first_section, total[8:], total[:8])


def finish_kernel(
    staying_ref, other_ref, scale_ref, towards_ref, back_ref, rest_ref, fwd_hbm, grad_hbm,
    result_ref, nothing_ref, sems,
):
    first_section = in_first_section()
    nothing_ref[...] = jnp.zeros_like(nothing_ref)

    @pl.when(first_section)
    def _():
        pltpu.make_async_copy(nothing_ref, fwd_hbm.at[0], sems.at[0]).start()

    @pl.when(jnp.logical_not(first_section))
    def _():
        pltpu.make_async_copy(nothing_ref, grad_hbm.at[0], sems.at[0]).start()

    sums = staying_ref[...] + other_ref[...].astype(jnp.float32)
    mean = jnp.mean(sums * towards_ref[...], axis=-1, keepdims=True)
    result = sums * scale_ref[...] + rest_ref[...] - back_ref[...] * mean
    result_ref[...] = result.astype(jnp.bfloat16)

    @pl.when(first_section)
    def _():
        pltpu.make_async_copy(result_ref, grad_hbm.at[0], sems.at[1]).start()

    @pl.when(jnp.logical_not(first_section))
    def _():
        pltpu.make_async_copy(result_ref, fwd_hbm.at[0], sems.at[1]).start()

    pltpu.make_async_copy(nothing_ref, fwd_hbm.at[0], sems.at[0]).wait()
    pltpu.make_async_copy(result_ref, grad_hbm.at[0], sems.at[1]).wait()


def finish(*arrays):
    count, width = arrays[0].shape
    return pl.pallas_call(
        finish_kernel,
        out_shape=[jax.ShapeDtypeStruct((1, count, width), jnp.bfloat16)] * 2,
        in_specs=[VMEM] * len(arrays),
        out_specs=[HBM] * 2,
        scratch_shapes=[
            pltpu.VMEM((count, width), jnp.bfloat16),
            pltpu.VMEM((count, width), jnp.bfloat16),
            pltpu.SemaphoreType.DMA((2,)),
        ],
        compiler_params=pltpu.CompilerParams(vmem_limit_bytes=4 * MIB),
        name="finish",
    )(*arrays)


def fetch_kernel(*refs, parts):
    count = len(parts)
    weights, held_refs, turned_refs = refs[:count], refs[count : 2 * count], refs[2 * count : 3 * count]
    sems = refs[-1]
    step = 256
    waiting = []
    for (first, rows), source, held, turned in zip(parts, weights, held_refs, turned_refs):
        for k in range(rows // step):
            copy = pltpu.make_async_copy(
                source.at[pl.ds(first + k * step, step)],
                held.at[pl.ds(k * step, step)],
                sems.at[len(waiting)],
            )
            copy.start()
            waiting.append((copy, held, turned, k * step))
    for copy, held, turned, start in waiting:
        copy.wait()
        turned[:, start : start + step] = held[start : start + step, :].T


def fetched(*parts):
    weights = [w for w, _, _ in parts]
    sizes = tuple((first, rows) for _, first, rows in parts)
    moved = sum(rows * w.shape[1] for w, _, rows in parts)
    held = [jax.ShapeDtypeStruct((rows, w.shape[1]), w.dtype) for w, _, rows in parts]
    turned = [jax.ShapeDtypeStruct((w.shape[1], rows), w.dtype) for w, _, rows in parts]
    outs = pl.pallas_call(
        functools.partial(fetch_kernel, parts=sizes),
        out_shape=held + turned,
        in_specs=[HBM] * len(parts),
        out_specs=[VMEM] * (2 * len(parts)),
        scratch_shapes=[pltpu.SemaphoreType.DMA((sum(rows for _, rows in sizes) // 256,))],
        compiler_params=pltpu.CompilerParams(vmem_limit_bytes=8 * MIB),
        cost_estimate=pl.CostEstimate(flops=0, bytes_accessed=4 * moved, transcendentals=0),
        name="fetch",
    )(*[in_hbm(w) for w in weights])
    return tuple(zip(outs[: len(parts)], outs[len(parts) :]))


def expert_kernel(
    near_ref, far_ref, router_ref, gate_ref, gate_turned_ref,
    up_ref, up_turned_ref, up_rest_ref, up_rest_turned_ref, down_ref, down_turned_ref,
    kept_ref, sent_ref,
):
    width, hidden_count = gate_ref.shape
    step = 256
    split = up_ref.shape[0]
    own_expert = lax.axis_index("expert")

    pairs = near_ref.shape[0] * 2 // 3
    tops = jnp.concatenate([near_ref[:pairs], far_ref[:pairs]], axis=0)
    grads = jnp.concatenate([near_ref[pairs:, :width], far_ref[pairs:, :width]], axis=0)
    routes = tops[:, width:].astype(jnp.float32)
    normed = tops[:, :width]

    def forward(rows):
        return jnp.concatenate([rows[16 * k : 16 * k + 8] for k in range(SQUARE)], axis=0)

    def backward(rows):
        return jnp.concatenate([rows[16 * k + 8 : 16 * k + 16] for k in range(SQUARE)], axis=0)

    router = router_ref[...]
    contract = (((1,), (1,)), ((), ()))
    logits = lax.dot_general(normed, router, contract, preferred_element_type=jnp.float32)
    labels = lax.broadcasted_iota(jnp.int32, logits.shape, 1)
    labels_real = labels.astype(jnp.float32)
    chosen = routes[:, 0:1] == labels_real
    for k in range(1, TOP_COUNT):
        chosen = jnp.logical_or(chosen, routes[:, k : k + 1] == labels_real)
    raised = jnp.where(chosen, jnp.exp(logits), 0.0)
    gates = raised / jnp.sum(raised, axis=-1, keepdims=True)
    own = jnp.where(labels == own_expert, 1.0, 0.0)
    gate_own = jnp.sum(own * gates, axis=-1, keepdims=True)
    gate_f, gate_b = forward(gate_own), backward(gate_own)

    hiddens, d_pres, d_ups = [], [], []
    dgate = 0.0
    for piece in range(hidden_count // step):
        cols = slice(piece * step, piece * step + step)
        pre_gate = jnp.dot(normed, gate_ref[:, cols], preferred_element_type=jnp.float32)
        pre_up = jnp.dot(normed[:, :split], up_ref[:, cols], preferred_element_type=jnp.float32)
        pre_up = pre_up + jnp.dot(
            normed[:, split:], up_rest_ref[:, cols], preferred_element_type=jnp.float32
        )
        d_hidden = jnp.dot(grads, down_turned_ref[:, cols], preferred_element_type=jnp.float32)
        sigma = jax.nn.sigmoid(pre_gate)
        silu_val = pre_gate * sigma
        hidden = silu_val * pre_up
        hiddens.append((forward(hidden) * gate_f).astype(jnp.bfloat16))
        dgate = dgate + jnp.sum(backward(hidden) * d_hidden, axis=-1, keepdims=True)
        d_hidden = d_hidden * gate_b
        d_ups.append((d_hidden * backward(silu_val)).astype(jnp.bfloat16))
        sigma_b = backward(sigma)
        slope = sigma_b * (1.0 + backward(pre_gate) * (1.0 - sigma_b))
        d_pres.append((d_hidden * backward(pre_up) * slope).astype(jnp.bfloat16))

    hidden = jnp.concatenate(hiddens, axis=1)
    d_pre = jnp.concatenate(d_pres, axis=1)
    d_up = jnp.concatenate(d_ups, axis=1)
    out_f = jnp.dot(hidden, down_ref[...], preferred_element_type=jnp.float32)
    d_normed = jnp.concatenate(
        [
            jnp.dot(d_up, mat[...], preferred_element_type=jnp.float32)
            for mat in (up_turned_ref, up_rest_turned_ref)
        ],
        axis=1,
    )
    d_normed = d_normed + jnp.dot(d_pre, gate_turned_ref[...], preferred_element_type=jnp.float32)
    spread = gate_b * dgate * (backward(own) - backward(gates))
    spread_high = spread.astype(jnp.bfloat16)
    spread_low = (spread - spread_high.astype(jnp.float32)).astype(jnp.bfloat16)
    d_normed = d_normed + jnp.dot(spread_high, router, preferred_element_type=jnp.float32)
    d_normed = d_normed + jnp.dot(spread_low, router, preferred_element_type=jnp.float32)

    parts = []
    for k in range(SQUARE):
        parts.append(out_f[8 * k : 8 * k + 8])
        parts.append(d_normed[8 * k : 8 * k + 8])
    kept_ref[...] = jnp.concatenate(parts[:SQUARE], axis=0).astype(jnp.bfloat16)
    sent_ref[...] = jnp.concatenate(parts[SQUARE:], axis=0).astype(jnp.bfloat16)


def run_experts(near, far, router, *weights):
    width = router.shape[1]
    rows = SQUARE // 2 * 16
    return pl.pallas_call(
        expert_kernel,
        out_shape=[jax.ShapeDtypeStruct((rows, width), jnp.bfloat16)] * 2,
        in_specs=[VMEM] * (3 + len(weights)),
        out_specs=[VMEM] * 2,
        compiler_params=pltpu.CompilerParams(vmem_limit_bytes=24 * MIB),
        name="experts",
    )(near, far, router, *weights)


def ending_kernel(across_ref, scale_ref, along_ref, back_ref, rest_ref):
    first_section = in_first_section()
    packed = across_ref[...].astype(jnp.float32)
    width = scale_ref.shape[1]
    grads = packed[8:16, :width]
    acts = packed[16:24, :width]
    gain_rows = packed[8:24, width : width + LANES] + packed[0:16, width + LANES :]
    gain_row = jnp.concatenate([gain_rows[k : k + 1] for k in range(16)], axis=1)
    factor = root_factor(acts)
    unit = acts * factor
    scale_ref[...] = jnp.where(first_section, factor * gain_row, 1.0)
    along_ref[...] = jnp.where(first_section, unit * gain_row, 0.0)
    back_ref[...] = jnp.where(first_section, unit * factor, 0.0)
    rest_ref[...] = jnp.where(first_section, grads, acts)


def added(*blocks):
    return sum(block.astype(jnp.float32) for block in blocks).astype(jnp.bfloat16)


def paired_plan(
    fwd_act, fwd_routes, bwd_saved, bwd_grad, bwd_routes, norm_gain, router, w_gate, w_up, w_down
):
    count, width = fwd_act.shape[1:]
    used = width + LANES
    along, acts, gain_row, router_rows = pack_rows(
        fwd_act, fwd_routes, bwd_saved, bwd_grad, bwd_routes, norm_gain, router.T
    )
    wide = jax.ShapeDtypeStruct((3 * count, used + LANES), jnp.bfloat16)
    across = in_vmem(widen_kernel, "widen", [wide], along, acts, gain_row)[0]
    across = swapped(across, SECTION)
    along = swapped(along, HALF)
    upper = width // 2
    gate_mats, up_mats = fetched((w_gate[0], 0, width), (w_up[0], 0, upper))
    along, gate_mats, up_mats = lax.optimization_barrier((along, gate_mats, up_mats))
    rows = jax.ShapeDtypeStruct((3 * count, used), jnp.bfloat16)
    mine = in_vmem(merge_kernel, "merge", [rows], along, across)[0]
    down_hbm, up_hbm, _ = lax.optimization_barrier((w_down[0], w_up[0], mine))
    rest_mats, down_mats = fetched((up_hbm, upper, width - upper), (down_hbm, 0, down_hbm.shape[0]))
    real = jax.ShapeDtypeStruct((count, width), jnp.float32)
    ending = in_vmem(ending_kernel, "endings", [real] * 4, across)
    blocks = [mine] + [swapped(mine, k) for k in (2, 4, 6)]
    near = jnp.concatenate([b[:16] for b in blocks] + [b[16:] for b in blocks], axis=0)
    near, rest_mats, down_mats, ending = lax.optimization_barrier(
        (near, rest_mats, down_mats, ending)
    )
    far = swapped(near, CORE)

    kept, sent = run_experts(
        near, far, router_rows, *gate_mats, *up_mats, *rest_mats, *down_mats
    )

    chip = added(kept, swapped(sent, CORE))
    pieces = [chip[0:16]] + [swapped(chip[8 * k : 8 * k + 16], k) for k in (2, 4, 6)]
    small = jax.ShapeDtypeStruct((count, width), jnp.bfloat16)
    leaving, staying = in_vmem(leave_kernel, "leave", [small, real], *pieces)
    other = swapped(leaving, SECTION + HALF)
    return tuple(finish(staying, other, *ending))


def per_device(fwd_act, fwd_routes, *rest):
    sections, devices = lax.axis_size("section"), lax.axis_size("expert")
    tokens, top_count = fwd_routes.shape[1:]
    router = rest[4]
    paired = sections == 2 and devices == 2 * SQUARE and router.shape == (16 * LANES, devices)
    paired = paired and tokens == 8 and top_count == TOP_COUNT
    plan = paired_plan if paired else routed_plan
    return plan(fwd_act, fwd_routes, *rest)


def solution(mesh):
    in_specs = (
        P("section", "expert", None),
        P("section", "expert", None),
        P("section", "expert", None),
        P("section", "expert", None),
        P("section", "expert", None),
        P("section", None),
        P(),
        P("expert", None, None),
        P("expert", None, None),
        P("expert", None, None),
    )
    out_specs = (P("section", "expert", None), P("section", "expert", None))
    return jax.shard_map(
        per_device, mesh=mesh, in_specs=in_specs, out_specs=out_specs, check_vma=False
    )
```

```python
import functools
import jax
import jax.numpy as jnp
from jax import lax
from jax.experimental import pallas as pl
from jax.experimental.pallas import tpu as pltpu
from jax.sharding import PartitionSpec as P

EPSILON = 1e-06


def shifted(block, axis, distance):
    devices = range(lax.axis_size(axis))
    route = [(i - distance, i) for i in devices if i - distance in devices]
    return lax.ppermute(block, axis, route)


def normalize(acts_in, gain_row):
    values = acts_in.astype(jnp.float32)
    factor = lax.rsqrt(jnp.mean(values * values, axis=-1, keepdims=True) + EPSILON)
    unit_rows = values * factor
    return ((unit_rows * gain_row).astype(jnp.bfloat16), unit_rows, factor)


def gate_values(normed, router, routes):
    logits = jnp.dot(normed, router, preferred_element_type=jnp.float32)
    chosen = jnp.take_along_axis(logits, routes, axis=1)
    raised = jnp.exp(chosen)
    return raised / jnp.sum(raised, axis=-1, keepdims=True)


def expert_forward(rows_in, gate_mat, up_mat, down_mat):
    pre_gate = jnp.dot(rows_in, gate_mat, preferred_element_type=jnp.float32)
    pre_up = jnp.dot(rows_in, up_mat, preferred_element_type=jnp.float32)
    sigma = jax.nn.sigmoid(pre_gate)
    hidden = (pre_gate * sigma * pre_up).astype(jnp.bfloat16)
    return jnp.dot(hidden, down_mat, preferred_element_type=jnp.float32).astype(jnp.bfloat16)


def expert_backward(rows_in, grads_in, gate_mat, up_mat, down_mat):
    pre_gate = jnp.dot(rows_in, gate_mat, preferred_element_type=jnp.float32)
    pre_up = jnp.dot(rows_in, up_mat, preferred_element_type=jnp.float32)
    sigma = jax.nn.sigmoid(pre_gate)
    silu_val = pre_gate * sigma
    hidden = (silu_val * pre_up).astype(jnp.bfloat16)
    expert_out = jnp.dot(hidden, down_mat, preferred_element_type=jnp.float32).astype(jnp.bfloat16)
    dgate = jnp.sum(grads_in.astype(jnp.float32) * expert_out.astype(jnp.float32), axis=-1).astype(
        jnp.bfloat16
    )
    contract = (((1,), (1,)), ((), ()))
    d_hidden = lax.dot_general(grads_in, down_mat, contract, preferred_element_type=jnp.float32)
    d_up = (d_hidden * silu_val).astype(jnp.bfloat16)
    d_pre = (d_hidden * pre_up * sigma * (1.0 + pre_gate * (1.0 - sigma))).astype(jnp.bfloat16)
    d_rows = lax.dot_general(d_pre, gate_mat, contract, preferred_element_type=jnp.float32)
    d_rows = d_rows + lax.dot_general(d_up, up_mat, contract, preferred_element_type=jnp.float32)
    return (d_rows.astype(jnp.bfloat16), dgate)


def input_gradient(gates, dgate, pair_grads, routes, router, unit_rows, factor, gain_row, grads_in):
    d_normed = jnp.sum(gates[:, :, None] * pair_grads, axis=1)
    d_chosen = gates * (dgate - jnp.sum(gates * dgate, axis=-1, keepdims=True))
    labels = jnp.arange(router.shape[1], dtype=jnp.int32)
    hits = (routes[:, :, None] == labels[None, None, :]).astype(jnp.float32)
    d_logits = jnp.sum(hits * d_chosen[:, :, None], axis=1)
    d_normed = d_normed + lax.dot_general(
        d_logits,
        router.astype(jnp.float32),
        (((1,), (1,)), ((), ())),
        precision=lax.Precision.HIGHEST,
    )
    d_unit = d_normed * gain_row
    result = factor * (d_unit - unit_rows * jnp.mean(d_unit * unit_rows, axis=-1, keepdims=True))
    return (result + grads_in.astype(jnp.float32)).astype(jnp.bfloat16)


def placement(routes, expert_count, capacity):
    flat_ids = routes.reshape(-1)
    labels = jnp.arange(expert_count, dtype=jnp.int32)
    onehot = (flat_ids[:, None] == labels[None, :]).astype(jnp.int32)
    before = jnp.cumsum(onehot, axis=0) - onehot
    slot_ids = jnp.sum(before * onehot, axis=1)
    target = flat_ids * capacity + slot_ids
    slot_labels = jnp.arange(expert_count * capacity, dtype=jnp.int32)
    select = (slot_labels[:, None] == target[None, :]).astype(jnp.bfloat16)
    spread = jnp.sum(
        select.reshape(expert_count * capacity, routes.shape[0], routes.shape[1]), axis=2
    )
    return (target, spread)


def dispatch(spread, rows_in, expert_count, capacity):
    placed = jnp.dot(spread, rows_in, preferred_element_type=jnp.float32).astype(jnp.bfloat16)
    return placed.reshape(expert_count, capacity, rows_in.shape[1])


def routed_plan(
    fwd_act, fwd_routes, bwd_saved, bwd_grad, bwd_routes, norm_gain, router, w_gate, w_up, w_down
):
    tok_count = fwd_act.shape[1]
    top_count = fwd_routes.shape[2]
    model_width = fwd_act.shape[2]
    expert_count = router.shape[1]
    capacity = min(tok_count, max(2, 2 * tok_count * top_count // expert_count))
    gain_row = norm_gain[0]
    gate_mat = w_gate[0]
    up_mat = w_up[0]
    down_mat = w_down[0]
    acts_f = fwd_act[0]
    routes_f = fwd_routes[0]
    normed_f, unused_unit, unused_factor = normalize(acts_f, gain_row)
    gates_f = gate_values(normed_f, router, routes_f)
    target_f, spread_f = placement(routes_f, expert_count, capacity)
    send_f = dispatch(spread_f, normed_f, expert_count, capacity)
    saved_b = bwd_saved[0]
    grads_b = bwd_grad[0]
    routes_b = bwd_routes[0]
    normed_b, unit_b, factor_b = normalize(saved_b, gain_row)
    gates_b = gate_values(normed_b, router, routes_b)
    target_b, spread_b = placement(routes_b, expert_count, capacity)
    send_x = dispatch(spread_b, normed_b, expert_count, capacity)
    send_g = dispatch(spread_b, grads_b, expert_count, capacity)
    rows_in = lax.all_to_all(send_f, "expert", split_axis=0, concat_axis=0, tiled=True)
    sources = rows_in.shape[0]
    slots = rows_in.shape[1]
    result = expert_forward(rows_in.reshape(-1, model_width), gate_mat, up_mat, down_mat)
    back_f = lax.all_to_all(
        result.reshape(sources, slots, model_width),
        "expert",
        split_axis=0,
        concat_axis=0,
        tiled=True,
    )
    rows_in = lax.all_to_all(send_x, "expert", split_axis=0, concat_axis=0, tiled=True)
    grads_in = lax.all_to_all(send_g, "expert", split_axis=0, concat_axis=0, tiled=True)
    sources = rows_in.shape[0]
    slots = rows_in.shape[1]
    d_rows, d_gates = expert_backward(
        rows_in.reshape(-1, model_width),
        grads_in.reshape(-1, model_width),
        gate_mat,
        up_mat,
        down_mat,
    )
    back_rows = lax.all_to_all(
        d_rows.reshape(sources, slots, model_width),
        "expert",
        split_axis=0,
        concat_axis=0,
        tiled=True,
    )
    back_gates = lax.all_to_all(
        d_gates.reshape(sources, slots), "expert", split_axis=0, concat_axis=0, tiled=True
    )
    picked_f = jnp.take(back_f.reshape(expert_count * capacity, model_width), target_f, axis=0)
    picked_f = picked_f.reshape(tok_count, top_count, model_width).astype(jnp.float32)
    layer_out = (
        acts_f.astype(jnp.float32) + jnp.sum(gates_f[:, :, None] * picked_f, axis=1)
    ).astype(jnp.bfloat16)
    fwd_next = shifted(layer_out[None], "section", 1)
    pair_grads = jnp.take(back_rows.reshape(expert_count * capacity, model_width), target_b, axis=0)
    pair_grads = pair_grads.reshape(tok_count, top_count, model_width).astype(jnp.float32)
    dgate = (
        jnp.take(back_gates.reshape(-1), target_b, axis=0)
        .reshape(tok_count, top_count)
        .astype(jnp.float32)
    )
    d_input = input_gradient(
        gates_b, dgate, pair_grads, routes_b, router, unit_b, factor_b, gain_row, grads_b
    )
    grad_prev = shifted(d_input[None], "section", -1)
    return (fwd_next, grad_prev)


AXES = ("section", "expert")
SQUARE = 8
CORE, HALF, SECTION = 1, 8, 16
EARLY = 2
LANES = 128
SQUARE_CHIPS = ((2, 2), (4, 4), (6, 6))
TOP_COUNT = 8
VMEM = pl.BlockSpec(memory_space=pltpu.VMEM)
SMEM = pl.BlockSpec(memory_space=pltpu.SMEM)
HBM = pl.BlockSpec(memory_space=pltpu.HBM)
MIB = 1024 * 1024


def swapped(block, even, odd=None):
    distances = (even, even if odd is None else odd)
    count = lax.axis_size(AXES)
    return lax.ppermute(block, AXES, [(i, i ^ distances[i & CORE]) for i in range(count)])


def in_hbm(array):
    return pltpu.with_memory_space_constraint(array, pltpu.HBM)


def root_factor(values):
    return lax.rsqrt(jnp.mean(values * values, axis=-1, keepdims=True) + EPSILON)


def in_first_section():
    return lax.axis_index("section") == 0


def pack_kernel(
    fwd_act, fwd_routes, bwd_saved, bwd_grad, bwd_routes, gain, router,
    across_ref, along_ref, acts_ref, gain_ref, router_ref, grads_ref, routes_ref, sems,
):
    first_section = in_first_section()
    grad_copy = pltpu.make_async_copy(bwd_grad.at[0], grads_ref, sems.at[0])
    gain_copy = pltpu.make_async_copy(gain, gain_ref, sems.at[1])
    router_copy = pltpu.make_async_copy(router, router_ref, sems.at[4])

    @pl.when(first_section)
    def _():
        pltpu.make_async_copy(fwd_act.at[0], acts_ref, sems.at[2]).start()
        pltpu.make_async_copy(fwd_routes.at[0], routes_ref, sems.at[3]).start()

    @pl.when(jnp.logical_not(first_section))
    def _():
        pltpu.make_async_copy(bwd_saved.at[0], acts_ref, sems.at[2]).start()
        pltpu.make_async_copy(bwd_routes.at[0], routes_ref, sems.at[3]).start()

    gain_copy.start()
    grad_copy.start()
    router_copy.start()
    pltpu.make_async_copy(fwd_act.at[0], acts_ref, sems.at[2]).wait()
    gain_copy.wait()
    acts = acts_ref[...].astype(jnp.float32)
    normed = acts * root_factor(acts) * gain_ref[...]
    pltpu.make_async_copy(fwd_routes.at[0], routes_ref, sems.at[3]).wait()
    grad_copy.wait()
    routes = routes_ref[...].astype(jnp.float32)
    routes = jnp.concatenate(
        [routes, jnp.zeros((routes.shape[0], LANES - TOP_COUNT), jnp.float32)], axis=1
    )
    rows = jnp.concatenate(
        [normed, grads_ref[...].astype(jnp.float32), routes], axis=1
    ).astype(jnp.bfloat16)
    across_ref[...] = rows
    along_ref[...] = jnp.concatenate([rows, rows[:, -LANES:]], axis=1)
    router_copy.wait()


def pack_rows(*arrays):
    fwd_act, fwd_routes, _, _, _, gain, router = arrays
    count, width = fwd_act.shape[1:]
    return pl.pallas_call(
        pack_kernel,
        out_shape=[
            jax.ShapeDtypeStruct((count, 2 * width + LANES), jnp.bfloat16),
            jax.ShapeDtypeStruct((count, 2 * width + 2 * LANES), jnp.bfloat16),
            jax.ShapeDtypeStruct((count, width), jnp.bfloat16),
            jax.ShapeDtypeStruct(gain.shape, gain.dtype),
            jax.ShapeDtypeStruct(router.shape, router.dtype),
        ],
        in_specs=[HBM] * 7,
        out_specs=[VMEM] * 5,
        scratch_shapes=[
            pltpu.VMEM((count, width), jnp.bfloat16),
            pltpu.VMEM(fwd_routes.shape[1:], jnp.int32),
            pltpu.SemaphoreType.DMA((5,)),
        ],
        compiler_params=pltpu.CompilerParams(vmem_limit_bytes=4 * MIB),
        name="pack",
    )(*[in_hbm(x) for x in arrays])


def widen_kernel(acts_ref, gain_ref, raw_ref):
    gain_row = gain_ref[...]
    count = acts_ref.shape[0]
    pieces = [gain_row[:, k : k + LANES] for k in range(0, gain_row.shape[1], LANES)]
    gain_rows = jnp.concatenate(
        [jnp.concatenate(pieces[k : k + count], axis=0) for k in range(0, len(pieces), count)],
        axis=1,
    )
    gain_high = gain_rows.astype(jnp.bfloat16).astype(jnp.float32)
    raw_ref[...] = jnp.concatenate(
        [acts_ref[...].astype(jnp.float32), gain_high, gain_rows - gain_high], axis=1
    ).astype(jnp.bfloat16)


def in_vmem(body, name, out_shape, *arrays):
    return pl.pallas_call(
        body,
        out_shape=out_shape,
        in_specs=[VMEM] * len(arrays),
        out_specs=[VMEM] * len(out_shape),
        compiler_params=pltpu.CompilerParams(vmem_limit_bytes=4 * MIB),
        name=name,
    )(*arrays)


def merge_kernel(along_ref, across_ref, mine_ref):
    first_section = in_first_section()
    used = across_ref.shape[1]
    width = (used - LANES) // 2
    along = along_ref[...].astype(jnp.float32)[:, :used]
    across = across_ref[...].astype(jnp.float32)
    forward = jnp.where(first_section, along, across)
    backward = jnp.where(first_section, across, along)
    routes = jnp.concatenate(
        [forward[:, 2 * width : 2 * width + TOP_COUNT], backward[:, 2 * width : -TOP_COUNT]], axis=1
    )
    mine_ref[...] = jnp.concatenate(
        [forward[:, :width], backward[:, : 2 * width], routes], axis=1
    ).astype(jnp.bfloat16)


def leave_kernel(a_ref, b_ref, c_ref, d_ref, leaving_ref, staying_ref):
    first_section = in_first_section()
    width = leaving_ref.shape[1]
    total = a_ref[...].astype(jnp.float32) + b_ref[...].astype(jnp.float32)
    total = total + c_ref[...].astype(jnp.float32) + d_ref[...].astype(jnp.float32)
    forward, backward = total[:, :width], total[:, width:]
    leaving_ref[...] = jnp.where(first_section, forward, backward).astype(jnp.bfloat16)
    staying_ref[...] = jnp.where(first_section, backward, forward)


def finish_kernel(
    staying_ref, other_ref, scale_ref, towards_ref, back_ref, rest_ref, fwd_hbm, grad_hbm,
    result_ref, nothing_ref, sems,
):
    first_section = in_first_section()
    nothing_ref[...] = jnp.zeros_like(nothing_ref)

    @pl.when(first_section)
    def _():
        pltpu.make_async_copy(nothing_ref, fwd_hbm.at[0], sems.at[0]).start()

    @pl.when(jnp.logical_not(first_section))
    def _():
        pltpu.make_async_copy(nothing_ref, grad_hbm.at[0], sems.at[0]).start()

    sums = staying_ref[...] + other_ref[...].astype(jnp.float32)
    mean = jnp.mean(sums * towards_ref[...], axis=-1, keepdims=True)
    result = sums * scale_ref[...] + rest_ref[...] - back_ref[...] * mean
    result_ref[...] = result.astype(jnp.bfloat16)

    @pl.when(first_section)
    def _():
        pltpu.make_async_copy(result_ref, grad_hbm.at[0], sems.at[1]).start()

    @pl.when(jnp.logical_not(first_section))
    def _():
        pltpu.make_async_copy(result_ref, fwd_hbm.at[0], sems.at[1]).start()

    pltpu.make_async_copy(nothing_ref, fwd_hbm.at[0], sems.at[0]).wait()
    pltpu.make_async_copy(result_ref, grad_hbm.at[0], sems.at[1]).wait()


def finish(*arrays):
    count, width = arrays[0].shape
    return pl.pallas_call(
        finish_kernel,
        out_shape=[jax.ShapeDtypeStruct((1, count, width), jnp.bfloat16)] * 2,
        in_specs=[VMEM] * len(arrays),
        out_specs=[HBM] * 2,
        scratch_shapes=[
            pltpu.VMEM((count, width), jnp.bfloat16),
            pltpu.VMEM((count, width), jnp.bfloat16),
            pltpu.SemaphoreType.DMA((2,)),
        ],
        compiler_params=pltpu.CompilerParams(vmem_limit_bytes=4 * MIB),
        name="finish",
    )(*arrays)


def fetch_kernel(*refs, parts):
    count = len(parts)
    weights, held_refs, turned_refs = refs[:count], refs[count : 2 * count], refs[2 * count : 3 * count]
    sems = refs[-1]
    step = 256
    waiting = []
    for (first, rows), source, held, turned in zip(parts, weights, held_refs, turned_refs):
        for k in range(rows // step):
            copy = pltpu.make_async_copy(
                source.at[pl.ds(first + k * step, step)],
                held.at[pl.ds(k * step, step)],
                sems.at[len(waiting)],
            )
            copy.start()
            waiting.append((copy, held, turned, k * step))
    for copy, held, turned, start in waiting:
        copy.wait()
        turned[:, start : start + step] = held[start : start + step, :].T


def fetched(*parts):
    weights = [w for w, _, _ in parts]
    sizes = tuple((first, rows) for _, first, rows in parts)
    moved = sum(rows * w.shape[1] for w, _, rows in parts)
    held = [jax.ShapeDtypeStruct((rows, w.shape[1]), w.dtype) for w, _, rows in parts]
    turned = [jax.ShapeDtypeStruct((w.shape[1], rows), w.dtype) for w, _, rows in parts]
    outs = pl.pallas_call(
        functools.partial(fetch_kernel, parts=sizes),
        out_shape=held + turned,
        in_specs=[HBM] * len(parts),
        out_specs=[VMEM] * (2 * len(parts)),
        scratch_shapes=[pltpu.SemaphoreType.DMA((sum(rows for _, rows in sizes) // 256,))],
        compiler_params=pltpu.CompilerParams(vmem_limit_bytes=8 * MIB),
        cost_estimate=pl.CostEstimate(flops=0, bytes_accessed=4 * moved, transcendentals=0),
        name="fetch",
    )(*[in_hbm(w) for w in weights])
    return tuple(zip(outs[: len(parts)], outs[len(parts) :]))


def expert_kernel(
    near_ref, next_ref, far_ref, last_ref, router_ref,
    gate_ref, gate_turned_ref, down_ref, down_turned_ref, *refs,
):
    up_refs, up_turned_refs, (kept_ref, sent_ref) = refs[:-2:2], refs[1:-2:2], refs[-2:]
    width, hidden_count = gate_ref.shape
    step = 256
    own_expert = lax.axis_index("expert")

    def both(first, last):
        blocks = (near_ref, next_ref, far_ref, last_ref)
        return jnp.concatenate([block[:, first:last] for block in blocks], axis=0)

    normed = jnp.concatenate([both(0, width), both(width, 2 * width)], axis=0)
    grads = both(2 * width, 3 * width)
    routes = both(3 * width, 3 * width + LANES).astype(jnp.float32)
    routes = jnp.concatenate([routes[:, :TOP_COUNT], routes[:, TOP_COUNT : 2 * TOP_COUNT]], axis=0)
    half = grads.shape[0]

    router = router_ref[...]
    contract = (((1,), (1,)), ((), ()))
    logits = lax.dot_general(normed, router, contract, preferred_element_type=jnp.float32)
    labels = lax.broadcasted_iota(jnp.int32, logits.shape, 1)
    labels_real = labels.astype(jnp.float32)
    chosen = routes[:, 0:1] == labels_real
    for k in range(1, TOP_COUNT):
        chosen = jnp.logical_or(chosen, routes[:, k : k + 1] == labels_real)
    raised = jnp.where(chosen, jnp.exp(logits), 0.0)
    gates = raised / jnp.sum(raised, axis=-1, keepdims=True)
    own = jnp.where(labels == own_expert, 1.0, 0.0)
    gate_own = jnp.sum(own * gates, axis=-1, keepdims=True)
    gate_f, gate_b = gate_own[:half], gate_own[half:]

    hiddens, d_pres, d_ups = [], [], []
    dgate = 0.0
    for piece in range(hidden_count // step):
        cols = slice(piece * step, piece * step + step)
        pre_gate = jnp.dot(normed, gate_ref[:, cols], preferred_element_type=jnp.float32)
        pre_up, start = 0.0, 0
        for ref in up_refs:
            rows = normed[:, start : start + ref.shape[0]]
            pre_up = pre_up + jnp.dot(rows, ref[:, cols], preferred_element_type=jnp.float32)
            start += ref.shape[0]
        d_hidden = jnp.dot(grads, down_turned_ref[:, cols], preferred_element_type=jnp.float32)
        sigma = jax.nn.sigmoid(pre_gate)
        silu_val = pre_gate * sigma
        hidden = silu_val * pre_up
        hiddens.append((hidden[:half] * gate_f).astype(jnp.bfloat16))
        dgate = dgate + jnp.sum(hidden[half:] * d_hidden, axis=-1, keepdims=True)
        d_hidden = d_hidden * gate_b
        d_ups.append((d_hidden * silu_val[half:]).astype(jnp.bfloat16))
        sigma_b = sigma[half:]
        slope = sigma_b * (1.0 + pre_gate[half:] * (1.0 - sigma_b))
        d_pres.append((d_hidden * pre_up[half:] * slope).astype(jnp.bfloat16))

    hidden = jnp.concatenate(hiddens, axis=1)
    d_pre = jnp.concatenate(d_pres, axis=1)
    d_up = jnp.concatenate(d_ups, axis=1)
    out_f = jnp.dot(hidden, down_ref[...], preferred_element_type=jnp.float32)
    d_normed = jnp.concatenate(
        [
            jnp.dot(d_up, mat[...], preferred_element_type=jnp.float32)
            for mat in up_turned_refs
        ],
        axis=1,
    )
    d_normed = d_normed + jnp.dot(d_pre, gate_turned_ref[...], preferred_element_type=jnp.float32)
    spread = gate_b * dgate * (own[half:] - gates[half:])
    spread_high = spread.astype(jnp.bfloat16)
    spread_low = (spread - spread_high.astype(jnp.float32)).astype(jnp.bfloat16)
    d_normed = d_normed + jnp.dot(spread_high, router, preferred_element_type=jnp.float32)
    d_normed = d_normed + jnp.dot(spread_low, router, preferred_element_type=jnp.float32)

    quarter = half // 2
    for ref, rows in ((kept_ref, slice(0, quarter)), (sent_ref, slice(quarter, half))):
        ref[...] = jnp.concatenate([out_f[rows], d_normed[rows]], axis=1).astype(jnp.bfloat16)


def run_experts(blocks, router, *weights):
    width = router.shape[1]
    return pl.pallas_call(
        expert_kernel,
        out_shape=[jax.ShapeDtypeStruct((2 * blocks[0].shape[0], 2 * width), jnp.bfloat16)] * 2,
        in_specs=[VMEM] * (1 + len(blocks) + len(weights)),
        out_specs=[VMEM] * 2,
        compiler_params=pltpu.CompilerParams(vmem_limit_bytes=24 * MIB),
        name="experts",
    )(*blocks, router, *weights)


def ending_kernel(across_ref, raw_ref, scale_ref, along_ref, back_ref, rest_ref):
    first_section = in_first_section()
    count, width = scale_ref.shape
    grads = across_ref[...].astype(jnp.float32)[:, width : 2 * width]
    raw = raw_ref[...].astype(jnp.float32)
    acts, gain_rows = raw[:, :width], raw[:, width:]
    spread = width // count
    gain_rows = gain_rows[:, :spread] + gain_rows[:, spread:]
    gain_row = jnp.concatenate(
        [
            gain_rows[row : row + 1, k : k + LANES]
            for k in range(0, spread, LANES)
            for row in range(count)
        ],
        axis=1,
    )
    factor = root_factor(acts)
    unit = acts * factor
    scale_ref[...] = jnp.where(first_section, factor * gain_row, 1.0)
    along_ref[...] = jnp.where(first_section, unit * gain_row, 0.0)
    back_ref[...] = jnp.where(first_section, unit * factor, 0.0)
    rest_ref[...] = jnp.where(first_section, grads, acts)


def added(*blocks):
    return sum(block.astype(jnp.float32) for block in blocks).astype(jnp.bfloat16)


def paired_plan(
    fwd_act, fwd_routes, bwd_saved, bwd_grad, bwd_routes, norm_gain, router, w_gate, w_up, w_down
):
    count, width = fwd_act.shape[1:]
    across, along, acts, gain_row, router_rows = pack_rows(
        fwd_act, fwd_routes, bwd_saved, bwd_grad, bwd_routes, norm_gain, router.T
    )
    across = swapped(across, SECTION)
    along = swapped(along, HALF)
    cuts = (width // 2, width)
    gate_hbm, up_hbm, down_hbm = w_gate[0], w_up[0], w_down[0]
    gate_mats, *ups = fetched((gate_hbm, 0, width), (up_hbm, 0, cuts[0]))
    along, gate_mats, ups = lax.optimization_barrier((along, gate_mats, ups))
    rows = jax.ShapeDtypeStruct((count, 3 * width + LANES), jnp.bfloat16)
    mine = in_vmem(merge_kernel, "merge", [rows], along, across)[0]
    down_hbm, up_hbm, _ = lax.optimization_barrier((down_hbm, up_hbm, mine))
    down_mats, *more = fetched(
        (down_hbm, 0, down_hbm.shape[0]), (up_hbm, cuts[0], cuts[1] - cuts[0])
    )
    ups = ups + more
    received = [swapped(mine, *k) for k in SQUARE_CHIPS]
    early = jnp.concatenate([mine, received[EARLY]], axis=0)
    late = jnp.concatenate([b for i, b in enumerate(received) if i != EARLY], axis=0)
    late, ups, down_mats = lax.optimization_barrier((late, ups, down_mats))
    blocks = [early, late, swapped(early, CORE), swapped(late, CORE)]

    weights = [m for mats in [gate_mats, down_mats] + ups for m in mats]
    kept, sent = run_experts(blocks, router_rows, *weights)

    chip = added(kept, swapped(sent, CORE))
    acts, chip = lax.optimization_barrier((acts, chip))
    real = jax.ShapeDtypeStruct((count, width), jnp.float32)
    wide = jax.ShapeDtypeStruct((count, width + 2 * (width // count)), jnp.bfloat16)
    raw = swapped(in_vmem(widen_kernel, "widen", [wide], acts, gain_row)[0], SECTION)
    pieces = [chip[:count]]
    order = [EARLY] + [i for i in range(len(SQUARE_CHIPS)) if i != EARLY]
    places = [order.index(i) + 1 for i in range(len(SQUARE_CHIPS))]
    pieces += [
        swapped(chip[i * count : (i + 1) * count], *k) for i, k in zip(places, SQUARE_CHIPS)
    ]
    ending = in_vmem(ending_kernel, "endings", [real] * 4, across, raw)
    small = jax.ShapeDtypeStruct((count, width), jnp.bfloat16)
    leaving, staying = in_vmem(leave_kernel, "leave", [small, real], *pieces)
    other = swapped(leaving, SECTION + HALF)
    return tuple(finish(staying, other, *ending))


def per_device(fwd_act, fwd_routes, *rest):
    sections, devices = lax.axis_size("section"), lax.axis_size("expert")
    tokens, top_count = fwd_routes.shape[1:]
    router = rest[4]
    paired = sections == 2 and devices == 2 * SQUARE and router.shape == (16 * LANES, devices)
    paired = paired and tokens == 8 and top_count == TOP_COUNT
    plan = paired_plan if paired else routed_plan
    return plan(fwd_act, fwd_routes, *rest)


def solution(mesh):
    in_specs = (
        P("section", "expert", None),
        P("section", "expert", None),
        P("section", "expert", None),
        P("section", "expert", None),
        P("section", "expert", None),
        P("section", None),
        P(),
        P("expert", None, None),
        P("expert", None, None),
        P("expert", None, None),
    )
    out_specs = (P("section", "expert", None), P("section", "expert", None))
    return jax.shard_map(
        per_device, mesh=mesh, in_specs=in_specs, out_specs=out_specs, check_vma=False
    )
```

```python
import functools
import jax
import jax.numpy as jnp
from jax import lax
from jax.experimental import pallas as pl
from jax.experimental.pallas import tpu as pltpu
from jax.sharding import PartitionSpec as P

EPSILON = 1e-06


def shifted(block, axis, distance):
    devices = range(lax.axis_size(axis))
    route = [(i - distance, i) for i in devices if i - distance in devices]
    return lax.ppermute(block, axis, route)


def normalize(acts_in, gain_row):
    values = acts_in.astype(jnp.float32)
    factor = lax.rsqrt(jnp.mean(values * values, axis=-1, keepdims=True) + EPSILON)
    unit_rows = values * factor
    return ((unit_rows * gain_row).astype(jnp.bfloat16), unit_rows, factor)


def gate_values(normed, router, routes):
    logits = jnp.dot(normed, router, preferred_element_type=jnp.float32)
    chosen = jnp.take_along_axis(logits, routes, axis=1)
    raised = jnp.exp(chosen)
    return raised / jnp.sum(raised, axis=-1, keepdims=True)


def expert_forward(rows_in, gate_mat, up_mat, down_mat):
    pre_gate = jnp.dot(rows_in, gate_mat, preferred_element_type=jnp.float32)
    pre_up = jnp.dot(rows_in, up_mat, preferred_element_type=jnp.float32)
    sigma = jax.nn.sigmoid(pre_gate)
    hidden = (pre_gate * sigma * pre_up).astype(jnp.bfloat16)
    return jnp.dot(hidden, down_mat, preferred_element_type=jnp.float32).astype(jnp.bfloat16)


def expert_backward(rows_in, grads_in, gate_mat, up_mat, down_mat):
    pre_gate = jnp.dot(rows_in, gate_mat, preferred_element_type=jnp.float32)
    pre_up = jnp.dot(rows_in, up_mat, preferred_element_type=jnp.float32)
    sigma = jax.nn.sigmoid(pre_gate)
    silu_val = pre_gate * sigma
    hidden = (silu_val * pre_up).astype(jnp.bfloat16)
    expert_out = jnp.dot(hidden, down_mat, preferred_element_type=jnp.float32).astype(jnp.bfloat16)
    dgate = jnp.sum(grads_in.astype(jnp.float32) * expert_out.astype(jnp.float32), axis=-1).astype(
        jnp.bfloat16
    )
    contract = (((1,), (1,)), ((), ()))
    d_hidden = lax.dot_general(grads_in, down_mat, contract, preferred_element_type=jnp.float32)
    d_up = (d_hidden * silu_val).astype(jnp.bfloat16)
    d_pre = (d_hidden * pre_up * sigma * (1.0 + pre_gate * (1.0 - sigma))).astype(jnp.bfloat16)
    d_rows = lax.dot_general(d_pre, gate_mat, contract, preferred_element_type=jnp.float32)
    d_rows = d_rows + lax.dot_general(d_up, up_mat, contract, preferred_element_type=jnp.float32)
    return (d_rows.astype(jnp.bfloat16), dgate)


def input_gradient(gates, dgate, pair_grads, routes, router, unit_rows, factor, gain_row, grads_in):
    d_normed = jnp.sum(gates[:, :, None] * pair_grads, axis=1)
    d_chosen = gates * (dgate - jnp.sum(gates * dgate, axis=-1, keepdims=True))
    labels = jnp.arange(router.shape[1], dtype=jnp.int32)
    hits = (routes[:, :, None] == labels[None, None, :]).astype(jnp.float32)
    d_logits = jnp.sum(hits * d_chosen[:, :, None], axis=1)
    d_normed = d_normed + lax.dot_general(
        d_logits,
        router.astype(jnp.float32),
        (((1,), (1,)), ((), ())),
        precision=lax.Precision.HIGHEST,
    )
    d_unit = d_normed * gain_row
    result = factor * (d_unit - unit_rows * jnp.mean(d_unit * unit_rows, axis=-1, keepdims=True))
    return (result + grads_in.astype(jnp.float32)).astype(jnp.bfloat16)


def placement(routes, expert_count, capacity):
    flat_ids = routes.reshape(-1)
    labels = jnp.arange(expert_count, dtype=jnp.int32)
    onehot = (flat_ids[:, None] == labels[None, :]).astype(jnp.int32)
    before = jnp.cumsum(onehot, axis=0) - onehot
    slot_ids = jnp.sum(before * onehot, axis=1)
    target = flat_ids * capacity + slot_ids
    slot_labels = jnp.arange(expert_count * capacity, dtype=jnp.int32)
    select = (slot_labels[:, None] == target[None, :]).astype(jnp.bfloat16)
    spread = jnp.sum(
        select.reshape(expert_count * capacity, routes.shape[0], routes.shape[1]), axis=2
    )
    return (target, spread)


def dispatch(spread, rows_in, expert_count, capacity):
    placed = jnp.dot(spread, rows_in, preferred_element_type=jnp.float32).astype(jnp.bfloat16)
    return placed.reshape(expert_count, capacity, rows_in.shape[1])


def routed_plan(
    fwd_act, fwd_routes, bwd_saved, bwd_grad, bwd_routes, norm_gain, router, w_gate, w_up, w_down
):
    tok_count = fwd_act.shape[1]
    top_count = fwd_routes.shape[2]
    model_width = fwd_act.shape[2]
    expert_count = router.shape[1]
    capacity = min(tok_count, max(2, 2 * tok_count * top_count // expert_count))
    gain_row = norm_gain[0]
    gate_mat = w_gate[0]
    up_mat = w_up[0]
    down_mat = w_down[0]
    acts_f = fwd_act[0]
    routes_f = fwd_routes[0]
    normed_f, unused_unit, unused_factor = normalize(acts_f, gain_row)
    gates_f = gate_values(normed_f, router, routes_f)
    target_f, spread_f = placement(routes_f, expert_count, capacity)
    send_f = dispatch(spread_f, normed_f, expert_count, capacity)
    saved_b = bwd_saved[0]
    grads_b = bwd_grad[0]
    routes_b = bwd_routes[0]
    normed_b, unit_b, factor_b = normalize(saved_b, gain_row)
    gates_b = gate_values(normed_b, router, routes_b)
    target_b, spread_b = placement(routes_b, expert_count, capacity)
    send_x = dispatch(spread_b, normed_b, expert_count, capacity)
    send_g = dispatch(spread_b, grads_b, expert_count, capacity)
    rows_in = lax.all_to_all(send_f, "expert", split_axis=0, concat_axis=0, tiled=True)
    sources = rows_in.shape[0]
    slots = rows_in.shape[1]
    result = expert_forward(rows_in.reshape(-1, model_width), gate_mat, up_mat, down_mat)
    back_f = lax.all_to_all(
        result.reshape(sources, slots, model_width),
        "expert",
        split_axis=0,
        concat_axis=0,
        tiled=True,
    )
    rows_in = lax.all_to_all(send_x, "expert", split_axis=0, concat_axis=0, tiled=True)
    grads_in = lax.all_to_all(send_g, "expert", split_axis=0, concat_axis=0, tiled=True)
    sources = rows_in.shape[0]
    slots = rows_in.shape[1]
    d_rows, d_gates = expert_backward(
        rows_in.reshape(-1, model_width),
        grads_in.reshape(-1, model_width),
        gate_mat,
        up_mat,
        down_mat,
    )
    back_rows = lax.all_to_all(
        d_rows.reshape(sources, slots, model_width),
        "expert",
        split_axis=0,
        concat_axis=0,
        tiled=True,
    )
    back_gates = lax.all_to_all(
        d_gates.reshape(sources, slots), "expert", split_axis=0, concat_axis=0, tiled=True
    )
    picked_f = jnp.take(back_f.reshape(expert_count * capacity, model_width), target_f, axis=0)
    picked_f = picked_f.reshape(tok_count, top_count, model_width).astype(jnp.float32)
    layer_out = (
        acts_f.astype(jnp.float32) + jnp.sum(gates_f[:, :, None] * picked_f, axis=1)
    ).astype(jnp.bfloat16)
    fwd_next = shifted(layer_out[None], "section", 1)
    pair_grads = jnp.take(back_rows.reshape(expert_count * capacity, model_width), target_b, axis=0)
    pair_grads = pair_grads.reshape(tok_count, top_count, model_width).astype(jnp.float32)
    dgate = (
        jnp.take(back_gates.reshape(-1), target_b, axis=0)
        .reshape(tok_count, top_count)
        .astype(jnp.float32)
    )
    d_input = input_gradient(
        gates_b, dgate, pair_grads, routes_b, router, unit_b, factor_b, gain_row, grads_b
    )
    grad_prev = shifted(d_input[None], "section", -1)
    return (fwd_next, grad_prev)


AXES = ("section", "expert")
SQUARE = 8
CORE, HALF, SECTION = 1, 8, 16
EARLY = 2
LANES = 128
SQUARE_CHIPS = ((2, 2), (4, 4), (6, 6))
TOP_COUNT = 8
VMEM = pl.BlockSpec(memory_space=pltpu.VMEM)
SMEM = pl.BlockSpec(memory_space=pltpu.SMEM)
HBM = pl.BlockSpec(memory_space=pltpu.HBM)
MIB = 1024 * 1024


def swapped(block, even, odd=None):
    distances = (even, even if odd is None else odd)
    count = lax.axis_size(AXES)
    return lax.ppermute(block, AXES, [(i, i ^ distances[i & CORE]) for i in range(count)])


def in_hbm(array):
    return pltpu.with_memory_space_constraint(array, pltpu.HBM)


def root_factor(values):
    return lax.rsqrt(jnp.mean(values * values, axis=-1, keepdims=True) + EPSILON)


def in_first_section():
    return lax.axis_index("section") == 0


def pack_kernel(
    fwd_act, fwd_routes, bwd_saved, bwd_grad, bwd_routes, gain, router,
    across_ref, along_ref, acts_ref, gain_ref, router_ref, grads_ref, routes_ref, sems,
):
    first_section = in_first_section()
    grad_copy = pltpu.make_async_copy(bwd_grad.at[0], grads_ref, sems.at[0])
    gain_copy = pltpu.make_async_copy(gain, gain_ref, sems.at[1])
    router_copy = pltpu.make_async_copy(router, router_ref, sems.at[4])

    @pl.when(first_section)
    def _():
        pltpu.make_async_copy(fwd_act.at[0], acts_ref, sems.at[2]).start()
        pltpu.make_async_copy(fwd_routes.at[0], routes_ref, sems.at[3]).start()

    @pl.when(jnp.logical_not(first_section))
    def _():
        pltpu.make_async_copy(bwd_saved.at[0], acts_ref, sems.at[2]).start()
        pltpu.make_async_copy(bwd_routes.at[0], routes_ref, sems.at[3]).start()

    gain_copy.start()
    grad_copy.start()
    router_copy.start()
    pltpu.make_async_copy(fwd_act.at[0], acts_ref, sems.at[2]).wait()
    gain_copy.wait()
    acts = acts_ref[...].astype(jnp.float32)
    normed = acts * root_factor(acts) * gain_ref[...]
    pltpu.make_async_copy(fwd_routes.at[0], routes_ref, sems.at[3]).wait()
    grad_copy.wait()
    routes = routes_ref[...].astype(jnp.float32)
    routes = jnp.concatenate(
        [routes, jnp.zeros((routes.shape[0], LANES - TOP_COUNT), jnp.float32)], axis=1
    )
    rows = jnp.concatenate(
        [normed, grads_ref[...].astype(jnp.float32), routes], axis=1
    ).astype(jnp.bfloat16)
    across_ref[...] = rows
    along_ref[...] = jnp.concatenate([rows, rows[:, -LANES:]], axis=1)
    router_copy.wait()


def pack_rows(*arrays):
    fwd_act, fwd_routes, _, _, _, gain, router = arrays
    count, width = fwd_act.shape[1:]
    return pl.pallas_call(
        pack_kernel,
        out_shape=[
            jax.ShapeDtypeStruct((count, 2 * width + LANES), jnp.bfloat16),
            jax.ShapeDtypeStruct((count, 2 * width + 2 * LANES), jnp.bfloat16),
            jax.ShapeDtypeStruct((count, width), jnp.bfloat16),
            jax.ShapeDtypeStruct(gain.shape, gain.dtype),
            jax.ShapeDtypeStruct(router.shape, router.dtype),
        ],
        in_specs=[HBM] * 7,
        out_specs=[VMEM] * 5,
        scratch_shapes=[
            pltpu.VMEM((count, width), jnp.bfloat16),
            pltpu.VMEM(fwd_routes.shape[1:], jnp.int32),
            pltpu.SemaphoreType.DMA((5,)),
        ],
        compiler_params=pltpu.CompilerParams(vmem_limit_bytes=4 * MIB),
        name="pack",
    )(*[in_hbm(x) for x in arrays])


def widen_kernel(acts_ref, gain_ref, raw_ref):
    gain_row = gain_ref[...]
    count = acts_ref.shape[0]
    pieces = [gain_row[:, k : k + LANES] for k in range(0, gain_row.shape[1], LANES)]
    gain_rows = jnp.concatenate(
        [jnp.concatenate(pieces[k : k + count], axis=0) for k in range(0, len(pieces), count)],
        axis=1,
    )
    gain_high = gain_rows.astype(jnp.bfloat16).astype(jnp.float32)
    raw_ref[...] = jnp.concatenate(
        [acts_ref[...].astype(jnp.float32), gain_high, gain_rows - gain_high], axis=1
    ).astype(jnp.bfloat16)


def in_vmem(body, name, out_shape, *arrays):
    return pl.pallas_call(
        body,
        out_shape=out_shape,
        in_specs=[VMEM] * len(arrays),
        out_specs=[VMEM] * len(out_shape),
        compiler_params=pltpu.CompilerParams(vmem_limit_bytes=4 * MIB),
        name=name,
    )(*arrays)


def merge_kernel(along_ref, across_ref, mine_ref):
    first_section = in_first_section()
    used = across_ref.shape[1]
    width = (used - LANES) // 2
    along = along_ref[...].astype(jnp.float32)[:, :used]
    across = across_ref[...].astype(jnp.float32)
    forward = jnp.where(first_section, along, across)
    backward = jnp.where(first_section, across, along)
    routes = jnp.concatenate(
        [forward[:, 2 * width : 2 * width + TOP_COUNT], backward[:, 2 * width : -TOP_COUNT]], axis=1
    )
    mine_ref[...] = jnp.concatenate(
        [forward[:, :width], backward[:, : 2 * width], routes], axis=1
    ).astype(jnp.bfloat16)


def leave_kernel(a_ref, b_ref, c_ref, d_ref, leaving_ref, staying_ref):
    first_section = in_first_section()
    width = leaving_ref.shape[1]
    total = a_ref[...].astype(jnp.float32) + b_ref[...].astype(jnp.float32)
    total = total + c_ref[...].astype(jnp.float32) + d_ref[...].astype(jnp.float32)
    forward, backward = total[:, :width], total[:, width:]
    leaving_ref[...] = jnp.where(first_section, forward, backward).astype(jnp.bfloat16)
    staying_ref[...] = jnp.where(first_section, backward, forward)


def finish_kernel(
    staying_ref, other_ref, scale_ref, towards_ref, back_ref, rest_ref, fwd_hbm, grad_hbm,
    result_ref, nothing_ref, sems,
):
    first_section = in_first_section()
    nothing_ref[...] = jnp.zeros_like(nothing_ref)

    @pl.when(first_section)
    def _():
        pltpu.make_async_copy(nothing_ref, fwd_hbm.at[0], sems.at[0]).start()

    @pl.when(jnp.logical_not(first_section))
    def _():
        pltpu.make_async_copy(nothing_ref, grad_hbm.at[0], sems.at[0]).start()

    sums = staying_ref[...] + other_ref[...].astype(jnp.float32)
    mean = jnp.mean(sums * towards_ref[...], axis=-1, keepdims=True)
    result = sums * scale_ref[...] + rest_ref[...] - back_ref[...] * mean
    result_ref[...] = result.astype(jnp.bfloat16)

    @pl.when(first_section)
    def _():
        pltpu.make_async_copy(result_ref, grad_hbm.at[0], sems.at[1]).start()

    @pl.when(jnp.logical_not(first_section))
    def _():
        pltpu.make_async_copy(result_ref, fwd_hbm.at[0], sems.at[1]).start()

    pltpu.make_async_copy(nothing_ref, fwd_hbm.at[0], sems.at[0]).wait()
    pltpu.make_async_copy(result_ref, grad_hbm.at[0], sems.at[1]).wait()


def finish(*arrays):
    count, width = arrays[0].shape
    return pl.pallas_call(
        finish_kernel,
        out_shape=[jax.ShapeDtypeStruct((1, count, width), jnp.bfloat16)] * 2,
        in_specs=[VMEM] * len(arrays),
        out_specs=[HBM] * 2,
        scratch_shapes=[
            pltpu.VMEM((count, width), jnp.bfloat16),
            pltpu.VMEM((count, width), jnp.bfloat16),
            pltpu.SemaphoreType.DMA((2,)),
        ],
        compiler_params=pltpu.CompilerParams(vmem_limit_bytes=4 * MIB),
        name="finish",
    )(*arrays)


def fetch_kernel(*refs, parts):
    count = len(parts)
    weights, held_refs, turned_refs = refs[:count], refs[count : 2 * count], refs[2 * count : 3 * count]
    sems = refs[-1]
    step = 256
    waiting = []
    for (first, rows), source, held, turned in zip(parts, weights, held_refs, turned_refs):
        for k in range(rows // step):
            copy = pltpu.make_async_copy(
                source.at[pl.ds(first + k * step, step)],
                held.at[pl.ds(k * step, step)],
                sems.at[len(waiting)],
            )
            copy.start()
            waiting.append((copy, held, turned, k * step))
    for copy, held, turned, start in waiting:
        copy.wait()
        turned[:, start : start + step] = held[start : start + step, :].T


def fetched(*parts):
    weights = [w for w, _, _ in parts]
    sizes = tuple((first, rows) for _, first, rows in parts)
    moved = sum(rows * w.shape[1] for w, _, rows in parts)
    held = [jax.ShapeDtypeStruct((rows, w.shape[1]), w.dtype) for w, _, rows in parts]
    turned = [jax.ShapeDtypeStruct((w.shape[1], rows), w.dtype) for w, _, rows in parts]
    outs = pl.pallas_call(
        functools.partial(fetch_kernel, parts=sizes),
        out_shape=held + turned,
        in_specs=[HBM] * len(parts),
        out_specs=[VMEM] * (2 * len(parts)),
        scratch_shapes=[pltpu.SemaphoreType.DMA((sum(rows for _, rows in sizes) // 256,))],
        compiler_params=pltpu.CompilerParams(vmem_limit_bytes=8 * MIB),
        cost_estimate=pl.CostEstimate(flops=0, bytes_accessed=4 * moved, transcendentals=0),
        name="fetch",
    )(*[in_hbm(w) for w in weights])
    return tuple(zip(outs[: len(parts)], outs[len(parts) :]))


def expert_kernel(
    near_ref, next_ref, far_ref, last_ref, router_ref,
    gate_ref, gate_turned_ref, down_ref, down_turned_ref, *refs,
):
    up_refs, up_turned_refs, out_refs = refs[:-4:2], refs[1:-4:2], refs[-4:]
    width, hidden_count = gate_ref.shape
    step = 256
    own_expert = lax.axis_index("expert")

    def both(first, last):
        blocks = (near_ref, next_ref, far_ref, last_ref)
        return jnp.concatenate([block[:, first:last] for block in blocks], axis=0)

    normed = jnp.concatenate([both(0, width), both(width, 2 * width)], axis=0)
    grads = both(2 * width, 3 * width)
    routes = both(3 * width, 3 * width + LANES).astype(jnp.float32)
    routes = jnp.concatenate([routes[:, :TOP_COUNT], routes[:, TOP_COUNT : 2 * TOP_COUNT]], axis=0)
    half = grads.shape[0]

    router = router_ref[...]
    contract = (((1,), (1,)), ((), ()))
    logits = lax.dot_general(normed, router, contract, preferred_element_type=jnp.float32)
    labels = lax.broadcasted_iota(jnp.int32, logits.shape, 1)
    labels_real = labels.astype(jnp.float32)
    chosen = routes[:, 0:1] == labels_real
    for k in range(1, TOP_COUNT):
        chosen = jnp.logical_or(chosen, routes[:, k : k + 1] == labels_real)
    raised = jnp.where(chosen, jnp.exp(logits), 0.0)
    gates = raised / jnp.sum(raised, axis=-1, keepdims=True)
    own = jnp.where(labels == own_expert, 1.0, 0.0)
    gate_own = jnp.sum(own * gates, axis=-1, keepdims=True)
    gate_f, gate_b = gate_own[:half], gate_own[half:]

    hiddens, d_pres, d_ups = [], [], []
    dgate = 0.0
    for piece in range(hidden_count // step):
        cols = slice(piece * step, piece * step + step)
        pre_gate = jnp.dot(normed, gate_ref[:, cols], preferred_element_type=jnp.float32)
        pre_up, start = 0.0, 0
        for ref in up_refs:
            rows = normed[:, start : start + ref.shape[0]]
            pre_up = pre_up + jnp.dot(rows, ref[:, cols], preferred_element_type=jnp.float32)
            start += ref.shape[0]
        d_hidden = jnp.dot(grads, down_turned_ref[:, cols], preferred_element_type=jnp.float32)
        sigma = jax.nn.sigmoid(pre_gate)
        silu_val = pre_gate * sigma
        hidden = silu_val * pre_up
        hiddens.append((hidden[:half] * gate_f).astype(jnp.bfloat16))
        dgate = dgate + jnp.sum(hidden[half:] * d_hidden, axis=-1, keepdims=True)
        d_hidden = d_hidden * gate_b
        d_ups.append((d_hidden * silu_val[half:]).astype(jnp.bfloat16))
        sigma_b = sigma[half:]
        slope = sigma_b * (1.0 + pre_gate[half:] * (1.0 - sigma_b))
        d_pres.append((d_hidden * pre_up[half:] * slope).astype(jnp.bfloat16))

    hidden = jnp.concatenate(hiddens, axis=1)
    d_pre = jnp.concatenate(d_pres, axis=1)
    d_up = jnp.concatenate(d_ups, axis=1)
    out_f = jnp.dot(hidden, down_ref[...], preferred_element_type=jnp.float32)
    d_normed = jnp.concatenate(
        [
            jnp.dot(d_up, mat[...], preferred_element_type=jnp.float32)
            for mat in up_turned_refs
        ],
        axis=1,
    )
    d_normed = d_normed + jnp.dot(d_pre, gate_turned_ref[...], preferred_element_type=jnp.float32)
    spread = gate_b * dgate * (own[half:] - gates[half:])
    spread_high = spread.astype(jnp.bfloat16)
    spread_low = (spread - spread_high.astype(jnp.float32)).astype(jnp.bfloat16)
    d_normed = d_normed + jnp.dot(spread_high, router, preferred_element_type=jnp.float32)
    d_normed = d_normed + jnp.dot(spread_low, router, preferred_element_type=jnp.float32)

    count = half // len(out_refs)
    for k, ref in enumerate(out_refs):
        rows = slice(k * count, (k + 1) * count)
        ref[...] = jnp.concatenate([out_f[rows], d_normed[rows]], axis=1).astype(jnp.bfloat16)


def run_experts(blocks, router, *weights):
    width = router.shape[1]
    return pl.pallas_call(
        expert_kernel,
        out_shape=[jax.ShapeDtypeStruct((b.shape[0], 2 * width), jnp.bfloat16) for b in blocks],
        in_specs=[VMEM] * (1 + len(blocks) + len(weights)),
        out_specs=[VMEM] * len(blocks),
        compiler_params=pltpu.CompilerParams(vmem_limit_bytes=24 * MIB),
        name="experts",
    )(*blocks, router, *weights)


def ending_kernel(across_ref, raw_ref, scale_ref, along_ref, back_ref, rest_ref):
    first_section = in_first_section()
    count, width = scale_ref.shape
    grads = across_ref[...].astype(jnp.float32)[:, width : 2 * width]
    raw = raw_ref[...].astype(jnp.float32)
    acts, gain_rows = raw[:, :width], raw[:, width:]
    spread = width // count
    gain_rows = gain_rows[:, :spread] + gain_rows[:, spread:]
    gain_row = jnp.concatenate(
        [
            gain_rows[row : row + 1, k : k + LANES]
            for k in range(0, spread, LANES)
            for row in range(count)
        ],
        axis=1,
    )
    factor = root_factor(acts)
    unit = acts * factor
    scale_ref[...] = jnp.where(first_section, factor * gain_row, 1.0)
    along_ref[...] = jnp.where(first_section, unit * gain_row, 0.0)
    back_ref[...] = jnp.where(first_section, unit * factor, 0.0)
    rest_ref[...] = jnp.where(first_section, grads, acts)


def added(*blocks):
    return sum(block.astype(jnp.float32) for block in blocks).astype(jnp.bfloat16)


def paired_plan(
    fwd_act, fwd_routes, bwd_saved, bwd_grad, bwd_routes, norm_gain, router, w_gate, w_up, w_down
):
    count, width = fwd_act.shape[1:]
    across, along, acts, gain_row, router_rows = pack_rows(
        fwd_act, fwd_routes, bwd_saved, bwd_grad, bwd_routes, norm_gain, router.T
    )
    across = swapped(across, SECTION)
    along = swapped(along, HALF)
    cuts = (width // 2, width)
    gate_hbm, up_hbm, down_hbm = w_gate[0], w_up[0], w_down[0]
    gate_mats, *ups = fetched((gate_hbm, 0, width), (up_hbm, 0, cuts[0]))
    along, gate_mats, ups = lax.optimization_barrier((along, gate_mats, ups))
    rows = jax.ShapeDtypeStruct((count, 3 * width + LANES), jnp.bfloat16)
    mine = in_vmem(merge_kernel, "merge", [rows], along, across)[0]
    down_hbm, up_hbm, _ = lax.optimization_barrier((down_hbm, up_hbm, mine))
    down_mats, *more = fetched(
        (down_hbm, 0, down_hbm.shape[0]), (up_hbm, cuts[0], cuts[1] - cuts[0])
    )
    ups = ups + more
    received = [swapped(mine, *k) for k in SQUARE_CHIPS]
    early = jnp.concatenate([mine, received[EARLY]], axis=0)
    late = jnp.concatenate([b for i, b in enumerate(received) if i != EARLY], axis=0)
    late, ups, down_mats = lax.optimization_barrier((late, ups, down_mats))
    blocks = [early, late, swapped(early, CORE), swapped(late, CORE)]

    weights = [m for mats in [gate_mats, down_mats] + ups for m in mats]
    kept = run_experts(blocks, router_rows, *weights)
    chips = [added(block, swapped(sent, CORE)) for block, sent in zip(kept[:2], kept[2:])]
    acts, last_chip = lax.optimization_barrier((acts, chips[1]))
    chips = [chips[0], last_chip]
    real = jax.ShapeDtypeStruct((count, width), jnp.float32)
    wide = jax.ShapeDtypeStruct((count, width + 2 * (width // count)), jnp.bfloat16)
    raw = swapped(in_vmem(widen_kernel, "widen", [wide], acts, gain_row)[0], SECTION)
    pieces = [chips[0][:count]]
    order = [EARLY] + [i for i in range(len(SQUARE_CHIPS)) if i != EARLY]
    for i, distances in enumerate(SQUARE_CHIPS):
        chip, place = divmod(order.index(i) + 1, 2)
        pieces.append(swapped(chips[chip][place * count : (place + 1) * count], *distances))
    ending = in_vmem(ending_kernel, "endings", [real] * 4, across, raw)
    small = jax.ShapeDtypeStruct((count, width), jnp.bfloat16)
    leaving, staying = in_vmem(leave_kernel, "leave", [small, real], *pieces)
    other = swapped(leaving, SECTION + HALF)
    return tuple(finish(staying, other, *ending))


def per_device(fwd_act, fwd_routes, *rest):
    sections, devices = lax.axis_size("section"), lax.axis_size("expert")
    tokens, top_count = fwd_routes.shape[1:]
    router = rest[4]
    paired = sections == 2 and devices == 2 * SQUARE and router.shape == (16 * LANES, devices)
    paired = paired and tokens == 8 and top_count == TOP_COUNT
    plan = paired_plan if paired else routed_plan
    return plan(fwd_act, fwd_routes, *rest)


def solution(mesh):
    in_specs = (
        P("section", "expert", None),
        P("section", "expert", None),
        P("section", "expert", None),
        P("section", "expert", None),
        P("section", "expert", None),
        P("section", None),
        P(),
        P("expert", None, None),
        P("expert", None, None),
        P("expert", None, None),
    )
    out_specs = (P("section", "expert", None), P("section", "expert", None))
    return jax.shard_map(
        per_device, mesh=mesh, in_specs=in_specs, out_specs=out_specs, check_vma=False
    )
```

```python
import functools
import jax
import jax.numpy as jnp
from jax import lax
from jax.experimental import pallas as pl
from jax.experimental.pallas import tpu as pltpu
from jax.sharding import PartitionSpec as P

EPSILON = 1e-06


def shifted(block, axis, distance):
    devices = range(lax.axis_size(axis))
    route = [(i - distance, i) for i in devices if i - distance in devices]
    return lax.ppermute(block, axis, route)


def normalize(acts_in, gain_row):
    values = acts_in.astype(jnp.float32)
    factor = lax.rsqrt(jnp.mean(values * values, axis=-1, keepdims=True) + EPSILON)
    unit_rows = values * factor
    return ((unit_rows * gain_row).astype(jnp.bfloat16), unit_rows, factor)


def gate_values(normed, router, routes):
    logits = jnp.dot(normed, router, preferred_element_type=jnp.float32)
    chosen = jnp.take_along_axis(logits, routes, axis=1)
    raised = jnp.exp(chosen)
    return raised / jnp.sum(raised, axis=-1, keepdims=True)


def expert_forward(rows_in, gate_mat, up_mat, down_mat):
    pre_gate = jnp.dot(rows_in, gate_mat, preferred_element_type=jnp.float32)
    pre_up = jnp.dot(rows_in, up_mat, preferred_element_type=jnp.float32)
    sigma = jax.nn.sigmoid(pre_gate)
    hidden = (pre_gate * sigma * pre_up).astype(jnp.bfloat16)
    return jnp.dot(hidden, down_mat, preferred_element_type=jnp.float32).astype(jnp.bfloat16)


def expert_backward(rows_in, grads_in, gate_mat, up_mat, down_mat):
    pre_gate = jnp.dot(rows_in, gate_mat, preferred_element_type=jnp.float32)
    pre_up = jnp.dot(rows_in, up_mat, preferred_element_type=jnp.float32)
    sigma = jax.nn.sigmoid(pre_gate)
    silu_val = pre_gate * sigma
    hidden = (silu_val * pre_up).astype(jnp.bfloat16)
    expert_out = jnp.dot(hidden, down_mat, preferred_element_type=jnp.float32).astype(jnp.bfloat16)
    dgate = jnp.sum(grads_in.astype(jnp.float32) * expert_out.astype(jnp.float32), axis=-1).astype(
        jnp.bfloat16
    )
    contract = (((1,), (1,)), ((), ()))
    d_hidden = lax.dot_general(grads_in, down_mat, contract, preferred_element_type=jnp.float32)
    d_up = (d_hidden * silu_val).astype(jnp.bfloat16)
    d_pre = (d_hidden * pre_up * sigma * (1.0 + pre_gate * (1.0 - sigma))).astype(jnp.bfloat16)
    d_rows = lax.dot_general(d_pre, gate_mat, contract, preferred_element_type=jnp.float32)
    d_rows = d_rows + lax.dot_general(d_up, up_mat, contract, preferred_element_type=jnp.float32)
    return (d_rows.astype(jnp.bfloat16), dgate)


def input_gradient(gates, dgate, pair_grads, routes, router, unit_rows, factor, gain_row, grads_in):
    d_normed = jnp.sum(gates[:, :, None] * pair_grads, axis=1)
    d_chosen = gates * (dgate - jnp.sum(gates * dgate, axis=-1, keepdims=True))
    labels = jnp.arange(router.shape[1], dtype=jnp.int32)
    hits = (routes[:, :, None] == labels[None, None, :]).astype(jnp.float32)
    d_logits = jnp.sum(hits * d_chosen[:, :, None], axis=1)
    d_normed = d_normed + lax.dot_general(
        d_logits,
        router.astype(jnp.float32),
        (((1,), (1,)), ((), ())),
        precision=lax.Precision.HIGHEST,
    )
    d_unit = d_normed * gain_row
    result = factor * (d_unit - unit_rows * jnp.mean(d_unit * unit_rows, axis=-1, keepdims=True))
    return (result + grads_in.astype(jnp.float32)).astype(jnp.bfloat16)


def placement(routes, expert_count, capacity):
    flat_ids = routes.reshape(-1)
    labels = jnp.arange(expert_count, dtype=jnp.int32)
    onehot = (flat_ids[:, None] == labels[None, :]).astype(jnp.int32)
    before = jnp.cumsum(onehot, axis=0) - onehot
    slot_ids = jnp.sum(before * onehot, axis=1)
    target = flat_ids * capacity + slot_ids
    slot_labels = jnp.arange(expert_count * capacity, dtype=jnp.int32)
    select = (slot_labels[:, None] == target[None, :]).astype(jnp.bfloat16)
    spread = jnp.sum(
        select.reshape(expert_count * capacity, routes.shape[0], routes.shape[1]), axis=2
    )
    return (target, spread)


def dispatch(spread, rows_in, expert_count, capacity):
    placed = jnp.dot(spread, rows_in, preferred_element_type=jnp.float32).astype(jnp.bfloat16)
    return placed.reshape(expert_count, capacity, rows_in.shape[1])


def routed_plan(
    fwd_act, fwd_routes, bwd_saved, bwd_grad, bwd_routes, norm_gain, router, w_gate, w_up, w_down
):
    tok_count = fwd_act.shape[1]
    top_count = fwd_routes.shape[2]
    model_width = fwd_act.shape[2]
    expert_count = router.shape[1]
    capacity = min(tok_count, max(2, 2 * tok_count * top_count // expert_count))
    gain_row = norm_gain[0]
    gate_mat = w_gate[0]
    up_mat = w_up[0]
    down_mat = w_down[0]
    acts_f = fwd_act[0]
    routes_f = fwd_routes[0]
    normed_f, unused_unit, unused_factor = normalize(acts_f, gain_row)
    gates_f = gate_values(normed_f, router, routes_f)
    target_f, spread_f = placement(routes_f, expert_count, capacity)
    send_f = dispatch(spread_f, normed_f, expert_count, capacity)
    saved_b = bwd_saved[0]
    grads_b = bwd_grad[0]
    routes_b = bwd_routes[0]
    normed_b, unit_b, factor_b = normalize(saved_b, gain_row)
    gates_b = gate_values(normed_b, router, routes_b)
    target_b, spread_b = placement(routes_b, expert_count, capacity)
    send_x = dispatch(spread_b, normed_b, expert_count, capacity)
    send_g = dispatch(spread_b, grads_b, expert_count, capacity)
    rows_in = lax.all_to_all(send_f, "expert", split_axis=0, concat_axis=0, tiled=True)
    sources = rows_in.shape[0]
    slots = rows_in.shape[1]
    result = expert_forward(rows_in.reshape(-1, model_width), gate_mat, up_mat, down_mat)
    back_f = lax.all_to_all(
        result.reshape(sources, slots, model_width),
        "expert",
        split_axis=0,
        concat_axis=0,
        tiled=True,
    )
    rows_in = lax.all_to_all(send_x, "expert", split_axis=0, concat_axis=0, tiled=True)
    grads_in = lax.all_to_all(send_g, "expert", split_axis=0, concat_axis=0, tiled=True)
    sources = rows_in.shape[0]
    slots = rows_in.shape[1]
    d_rows, d_gates = expert_backward(
        rows_in.reshape(-1, model_width),
        grads_in.reshape(-1, model_width),
        gate_mat,
        up_mat,
        down_mat,
    )
    back_rows = lax.all_to_all(
        d_rows.reshape(sources, slots, model_width),
        "expert",
        split_axis=0,
        concat_axis=0,
        tiled=True,
    )
    back_gates = lax.all_to_all(
        d_gates.reshape(sources, slots), "expert", split_axis=0, concat_axis=0, tiled=True
    )
    picked_f = jnp.take(back_f.reshape(expert_count * capacity, model_width), target_f, axis=0)
    picked_f = picked_f.reshape(tok_count, top_count, model_width).astype(jnp.float32)
    layer_out = (
        acts_f.astype(jnp.float32) + jnp.sum(gates_f[:, :, None] * picked_f, axis=1)
    ).astype(jnp.bfloat16)
    fwd_next = shifted(layer_out[None], "section", 1)
    pair_grads = jnp.take(back_rows.reshape(expert_count * capacity, model_width), target_b, axis=0)
    pair_grads = pair_grads.reshape(tok_count, top_count, model_width).astype(jnp.float32)
    dgate = (
        jnp.take(back_gates.reshape(-1), target_b, axis=0)
        .reshape(tok_count, top_count)
        .astype(jnp.float32)
    )
    d_input = input_gradient(
        gates_b, dgate, pair_grads, routes_b, router, unit_b, factor_b, gain_row, grads_b
    )
    grad_prev = shifted(d_input[None], "section", -1)
    return (fwd_next, grad_prev)


AXES = ("section", "expert")
SQUARE = 8
CORE, HALF, SECTION = 1, 9, 16
EARLY = 2
LANES = 128
SQUARE_CHIPS = (3, 5, 7)
TOP_COUNT = 8
VMEM = pl.BlockSpec(memory_space=pltpu.VMEM)
SMEM = pl.BlockSpec(memory_space=pltpu.SMEM)
HBM = pl.BlockSpec(memory_space=pltpu.HBM)
MIB = 1024 * 1024


def swapped(block, distance):
    count = lax.axis_size(AXES)
    return lax.ppermute(block, AXES, [(i, i ^ distance) for i in range(count)])


def in_hbm(array):
    return pltpu.with_memory_space_constraint(array, pltpu.HBM)


def root_factor(values):
    return lax.rsqrt(jnp.mean(values * values, axis=-1, keepdims=True) + EPSILON)


def in_first_section():
    return lax.axis_index("section") == 0


def pack_kernel(
    fwd_act, fwd_routes, bwd_saved, bwd_grad, bwd_routes, gain, router,
    across_ref, along_ref, acts_ref, gain_ref, router_ref, grads_ref, routes_ref, sems,
):
    first_section = in_first_section()
    grad_copy = pltpu.make_async_copy(bwd_grad.at[0], grads_ref, sems.at[0])
    gain_copy = pltpu.make_async_copy(gain, gain_ref, sems.at[1])
    router_copy = pltpu.make_async_copy(router, router_ref, sems.at[4])

    @pl.when(first_section)
    def _():
        pltpu.make_async_copy(fwd_act.at[0], acts_ref, sems.at[2]).start()
        pltpu.make_async_copy(fwd_routes.at[0], routes_ref, sems.at[3]).start()

    @pl.when(jnp.logical_not(first_section))
    def _():
        pltpu.make_async_copy(bwd_saved.at[0], acts_ref, sems.at[2]).start()
        pltpu.make_async_copy(bwd_routes.at[0], routes_ref, sems.at[3]).start()

    gain_copy.start()
    grad_copy.start()
    router_copy.start()
    pltpu.make_async_copy(fwd_act.at[0], acts_ref, sems.at[2]).wait()
    gain_copy.wait()
    acts = acts_ref[...].astype(jnp.float32)
    normed = acts * root_factor(acts) * gain_ref[...]
    pltpu.make_async_copy(fwd_routes.at[0], routes_ref, sems.at[3]).wait()
    grad_copy.wait()
    routes = routes_ref[...].astype(jnp.float32)
    blank = jnp.zeros_like(routes)
    routes = jnp.concatenate(
        [
            jnp.where(first_section, routes, blank),
            jnp.where(first_section, blank, routes),
            jnp.zeros((routes.shape[0], LANES - 2 * TOP_COUNT), jnp.float32),
        ],
        axis=1,
    )
    rows = jnp.concatenate(
        [normed, grads_ref[...].astype(jnp.float32), routes], axis=1
    ).astype(jnp.bfloat16)
    across_ref[...] = rows
    along_ref[...] = jnp.concatenate([rows, rows[:, -LANES:]], axis=1)
    router_copy.wait()


def pack_rows(*arrays):
    fwd_act, fwd_routes, _, _, _, gain, router = arrays
    count, width = fwd_act.shape[1:]
    return pl.pallas_call(
        pack_kernel,
        out_shape=[
            jax.ShapeDtypeStruct((count, 2 * width + LANES), jnp.bfloat16),
            jax.ShapeDtypeStruct((count, 2 * width + 2 * LANES), jnp.bfloat16),
            jax.ShapeDtypeStruct((count, width), jnp.bfloat16),
            jax.ShapeDtypeStruct(gain.shape, gain.dtype),
            jax.ShapeDtypeStruct(router.shape, router.dtype),
        ],
        in_specs=[HBM] * 7,
        out_specs=[VMEM] * 5,
        scratch_shapes=[
            pltpu.VMEM((count, width), jnp.bfloat16),
            pltpu.VMEM(fwd_routes.shape[1:], jnp.int32),
            pltpu.SemaphoreType.DMA((5,)),
        ],
        compiler_params=pltpu.CompilerParams(vmem_limit_bytes=4 * MIB),
        name="pack",
    )(*[in_hbm(x) for x in arrays])


def widen_kernel(acts_ref, gain_ref, raw_ref):
    gain_row = gain_ref[...]
    count = acts_ref.shape[0]
    pieces = [gain_row[:, k : k + LANES] for k in range(0, gain_row.shape[1], LANES)]
    gain_rows = jnp.concatenate(
        [jnp.concatenate(pieces[k : k + count], axis=0) for k in range(0, len(pieces), count)],
        axis=1,
    )
    gain_high = gain_rows.astype(jnp.bfloat16).astype(jnp.float32)
    raw_ref[...] = jnp.concatenate(
        [acts_ref[...].astype(jnp.float32), gain_high, gain_rows - gain_high], axis=1
    ).astype(jnp.bfloat16)


def in_vmem(body, name, out_shape, *arrays):
    return pl.pallas_call(
        body,
        out_shape=out_shape,
        in_specs=[VMEM] * len(arrays),
        out_specs=[VMEM] * len(out_shape),
        compiler_params=pltpu.CompilerParams(vmem_limit_bytes=4 * MIB),
        name=name,
    )(*arrays)


def merge_kernel(along_ref, across_ref, mine_ref):
    width = (across_ref.shape[1] - LANES) // 2
    first_section = in_first_section()

    def merge(forward_ref, backward_ref):
        mine_ref[:, :width] = forward_ref[:, :width]
        mine_ref[:, width : 3 * width] = backward_ref[:, : 2 * width]

    @pl.when(first_section)
    def _():
        merge(along_ref, across_ref)

    @pl.when(jnp.logical_not(first_section))
    def _():
        merge(across_ref, along_ref)

    tail = slice(2 * width, 2 * width + LANES)
    mine_ref[:, 3 * width :] = along_ref[:, tail] + across_ref[:, tail]


def leave_kernel(a_ref, b_ref, c_ref, d_ref, leaving_ref, staying_ref):
    first_section = in_first_section()
    width = leaving_ref.shape[1]
    total = a_ref[...].astype(jnp.float32) + b_ref[...].astype(jnp.float32)
    total = total + c_ref[...].astype(jnp.float32) + d_ref[...].astype(jnp.float32)
    forward, backward = total[:, :width], total[:, width:]
    leaving_ref[...] = jnp.where(first_section, forward, backward).astype(jnp.bfloat16)
    staying_ref[...] = jnp.where(first_section, backward, forward)


def finish_kernel(
    staying_ref, other_ref, scale_ref, towards_ref, back_ref, rest_ref, fwd_hbm, grad_hbm,
    result_ref, nothing_ref, sems,
):
    first_section = in_first_section()
    nothing_ref[...] = jnp.zeros_like(nothing_ref)

    @pl.when(first_section)
    def _():
        pltpu.make_async_copy(nothing_ref, fwd_hbm.at[0], sems.at[0]).start()

    @pl.when(jnp.logical_not(first_section))
    def _():
        pltpu.make_async_copy(nothing_ref, grad_hbm.at[0], sems.at[0]).start()

    sums = staying_ref[...] + other_ref[...].astype(jnp.float32)
    mean = jnp.mean(sums * towards_ref[...], axis=-1, keepdims=True)
    result = sums * scale_ref[...] + rest_ref[...] - back_ref[...] * mean
    result_ref[...] = result.astype(jnp.bfloat16)

    @pl.when(first_section)
    def _():
        pltpu.make_async_copy(result_ref, grad_hbm.at[0], sems.at[1]).start()

    @pl.when(jnp.logical_not(first_section))
    def _():
        pltpu.make_async_copy(result_ref, fwd_hbm.at[0], sems.at[1]).start()

    pltpu.make_async_copy(nothing_ref, fwd_hbm.at[0], sems.at[0]).wait()
    pltpu.make_async_copy(result_ref, grad_hbm.at[0], sems.at[1]).wait()


def finish(*arrays):
    count, width = arrays[0].shape
    return pl.pallas_call(
        finish_kernel,
        out_shape=[jax.ShapeDtypeStruct((1, count, width), jnp.bfloat16)] * 2,
        in_specs=[VMEM] * len(arrays),
        out_specs=[HBM] * 2,
        scratch_shapes=[
            pltpu.VMEM((count, width), jnp.bfloat16),
            pltpu.VMEM((count, width), jnp.bfloat16),
            pltpu.SemaphoreType.DMA((2,)),
        ],
        compiler_params=pltpu.CompilerParams(vmem_limit_bytes=4 * MIB),
        name="finish",
    )(*arrays)


def fetch_kernel(*refs, parts):
    count = len(parts)
    weights, held_refs, turned_refs = refs[:count], refs[count : 2 * count], refs[2 * count : 3 * count]
    sems = refs[-1]
    step = 256
    waiting = []
    for (first, rows), source, held, turned in zip(parts, weights, held_refs, turned_refs):
        for k in range(rows // step):
            copy = pltpu.make_async_copy(
                source.at[pl.ds(first + k * step, step)],
                held.at[pl.ds(k * step, step)],
                sems.at[len(waiting)],
            )
            copy.start()
            waiting.append((copy, held, turned, k * step))
    for copy, held, turned, start in waiting:
        copy.wait()
        turned[:, start : start + step] = held[start : start + step, :].T


def fetched(*parts):
    weights = [w for w, _, _ in parts]
    sizes = tuple((first, rows) for _, first, rows in parts)
    moved = sum(rows * w.shape[1] for w, _, rows in parts)
    held = [jax.ShapeDtypeStruct((rows, w.shape[1]), w.dtype) for w, _, rows in parts]
    turned = [jax.ShapeDtypeStruct((w.shape[1], rows), w.dtype) for w, _, rows in parts]
    outs = pl.pallas_call(
        functools.partial(fetch_kernel, parts=sizes),
        out_shape=held + turned,
        in_specs=[HBM] * len(parts),
        out_specs=[VMEM] * (2 * len(parts)),
        scratch_shapes=[pltpu.SemaphoreType.DMA((sum(rows for _, rows in sizes) // 256,))],
        compiler_params=pltpu.CompilerParams(vmem_limit_bytes=8 * MIB),
        cost_estimate=pl.CostEstimate(flops=0, bytes_accessed=4 * moved, transcendentals=0),
        name="fetch",
    )(*[in_hbm(w) for w in weights])
    return tuple(zip(outs[: len(parts)], outs[len(parts) :]))


def expert_kernel(
    near_ref, next_ref, far_ref, last_ref, router_ref,
    gate_ref, gate_turned_ref, down_ref, down_turned_ref, *refs,
):
    up_refs, up_turned_refs, out_refs = refs[:-4:2], refs[1:-4:2], refs[-4:]
    width, hidden_count = gate_ref.shape
    step = 256
    own_expert = lax.axis_index("expert")

    def both(first, last):
        blocks = (near_ref, next_ref, far_ref, last_ref)
        return jnp.concatenate([block[:, first:last] for block in blocks], axis=0)

    normed = jnp.concatenate([both(0, width), both(width, 2 * width)], axis=0)
    grads = both(2 * width, 3 * width)
    routes = both(3 * width, 3 * width + LANES).astype(jnp.float32)
    routes = jnp.concatenate([routes[:, :TOP_COUNT], routes[:, TOP_COUNT : 2 * TOP_COUNT]], axis=0)
    half = grads.shape[0]

    router = router_ref[...]
    contract = (((1,), (1,)), ((), ()))
    logits = lax.dot_general(normed, router, contract, preferred_element_type=jnp.float32)
    labels = lax.broadcasted_iota(jnp.int32, logits.shape, 1)
    labels_real = labels.astype(jnp.float32)
    chosen = routes[:, 0:1] == labels_real
    for k in range(1, TOP_COUNT):
        chosen = jnp.logical_or(chosen, routes[:, k : k + 1] == labels_real)
    raised = jnp.where(chosen, jnp.exp(logits), 0.0)
    gates = raised / jnp.sum(raised, axis=-1, keepdims=True)
    own = jnp.where(labels == own_expert, 1.0, 0.0)
    gate_own = jnp.sum(own * gates, axis=-1, keepdims=True)
    gate_f, gate_b = gate_own[:half], gate_own[half:]

    hiddens, d_pres, d_ups = [], [], []
    dgate = 0.0
    for piece in range(hidden_count // step):
        cols = slice(piece * step, piece * step + step)
        pre_gate = jnp.dot(normed, gate_ref[:, cols], preferred_element_type=jnp.float32)
        pre_up, start = 0.0, 0
        for ref in up_refs:
            rows = normed[:, start : start + ref.shape[0]]
            pre_up = pre_up + jnp.dot(rows, ref[:, cols], preferred_element_type=jnp.float32)
            start += ref.shape[0]
        d_hidden = jnp.dot(grads, down_turned_ref[:, cols], preferred_element_type=jnp.float32)
        sigma = jax.nn.sigmoid(pre_gate)
        silu_val = pre_gate * sigma
        hidden = silu_val * pre_up
        hiddens.append((hidden[:half] * gate_f).astype(jnp.bfloat16))
        dgate = dgate + jnp.sum(hidden[half:] * d_hidden, axis=-1, keepdims=True)
        d_hidden = d_hidden * gate_b
        d_ups.append((d_hidden * silu_val[half:]).astype(jnp.bfloat16))
        sigma_b = sigma[half:]
        slope = sigma_b * (1.0 + pre_gate[half:] * (1.0 - sigma_b))
        d_pres.append((d_hidden * pre_up[half:] * slope).astype(jnp.bfloat16))

    hidden = jnp.concatenate(hiddens, axis=1)
    d_pre = jnp.concatenate(d_pres, axis=1)
    d_up = jnp.concatenate(d_ups, axis=1)
    out_f = jnp.dot(hidden, down_ref[...], preferred_element_type=jnp.float32)
    d_normed = jnp.concatenate(
        [
            jnp.dot(d_up, mat[...], preferred_element_type=jnp.float32)
            for mat in up_turned_refs
        ],
        axis=1,
    )
    d_normed = d_normed + jnp.dot(d_pre, gate_turned_ref[...], preferred_element_type=jnp.float32)
    spread = gate_b * dgate * (own[half:] - gates[half:])
    spread_high = spread.astype(jnp.bfloat16)
    spread_low = (spread - spread_high.astype(jnp.float32)).astype(jnp.bfloat16)
    d_normed = d_normed + jnp.dot(
        jnp.concatenate([spread_high, spread_low], axis=1),
        jnp.concatenate([router, router], axis=0),
        preferred_element_type=jnp.float32,
    )

    count = half // len(out_refs)
    for k, ref in enumerate(out_refs):
        rows = slice(k * count, (k + 1) * count)
        ref[...] = jnp.concatenate([out_f[rows], d_normed[rows]], axis=1).astype(jnp.bfloat16)


def run_experts(blocks, router, *weights):
    width = router.shape[1]
    return pl.pallas_call(
        expert_kernel,
        out_shape=[jax.ShapeDtypeStruct((b.shape[0], 2 * width), jnp.bfloat16) for b in blocks],
        in_specs=[VMEM] * (1 + len(blocks) + len(weights)),
        out_specs=[VMEM] * len(blocks),
        compiler_params=pltpu.CompilerParams(vmem_limit_bytes=24 * MIB),
        name="experts",
    )(*blocks, router, *weights)


def ending_kernel(across_ref, raw_ref, scale_ref, along_ref, back_ref, rest_ref):
    first_section = in_first_section()
    count, width = scale_ref.shape
    grads = across_ref[...].astype(jnp.float32)[:, width : 2 * width]
    raw = raw_ref[...].astype(jnp.float32)
    acts, gain_rows = raw[:, :width], raw[:, width:]
    spread = width // count
    gain_rows = gain_rows[:, :spread] + gain_rows[:, spread:]
    gain_row = jnp.concatenate(
        [
            gain_rows[row : row + 1, k : k + LANES]
            for k in range(0, spread, LANES)
            for row in range(count)
        ],
        axis=1,
    )
    factor = root_factor(acts)
    unit = acts * factor
    scale_ref[...] = jnp.where(first_section, factor * gain_row, 1.0)
    along_ref[...] = jnp.where(first_section, unit * gain_row, 0.0)
    back_ref[...] = jnp.where(first_section, unit * factor, 0.0)
    rest_ref[...] = jnp.where(first_section, grads, acts)


def added(*blocks):
    return sum(block.astype(jnp.float32) for block in blocks).astype(jnp.bfloat16)


def paired_plan(
    fwd_act, fwd_routes, bwd_saved, bwd_grad, bwd_routes, norm_gain, router, w_gate, w_up, w_down
):
    count, width = fwd_act.shape[1:]
    across, along, acts, gain_row, router_rows = pack_rows(
        fwd_act, fwd_routes, bwd_saved, bwd_grad, bwd_routes, norm_gain, router.T
    )
    across = swapped(across, SECTION)
    along = swapped(along, HALF)
    cuts = (width // 2, width)
    gate_hbm, up_hbm, down_hbm = w_gate[0], w_up[0], w_down[0]
    gate_mats, *ups = fetched((gate_hbm, 0, width), (up_hbm, 0, cuts[0]))
    along, gate_mats, ups = lax.optimization_barrier((along, gate_mats, ups))
    rows = jax.ShapeDtypeStruct((count, 3 * width + LANES), jnp.bfloat16)
    mine = in_vmem(merge_kernel, "merge", [rows], along, across)[0]
    down_hbm, up_hbm, _ = lax.optimization_barrier((down_hbm, up_hbm, mine))
    down_mats, *more = fetched(
        (down_hbm, 0, down_hbm.shape[0]), (up_hbm, cuts[0], cuts[1] - cuts[0])
    )
    ups = ups + more
    received = [swapped(mine, k) for k in SQUARE_CHIPS]
    early = jnp.concatenate([mine, received[EARLY]], axis=0)
    late = jnp.concatenate([b for i, b in enumerate(received) if i != EARLY], axis=0)
    late, ups, down_mats = lax.optimization_barrier((late, ups, down_mats))
    blocks = [early, late, swapped(early, CORE), swapped(late, CORE)]

    weights = [m for mats in [gate_mats, down_mats] + ups for m in mats]
    kept = run_experts(blocks, router_rows, *weights)
    chips = [added(block, swapped(sent, CORE)) for block, sent in zip(kept[:2], kept[2:])]
    acts, last_chip = lax.optimization_barrier((acts, chips[1]))
    chips = [chips[0], last_chip]
    real = jax.ShapeDtypeStruct((count, width), jnp.float32)
    wide = jax.ShapeDtypeStruct((count, width + 2 * (width // count)), jnp.bfloat16)
    raw = swapped(in_vmem(widen_kernel, "widen", [wide], acts, gain_row)[0], SECTION)
    pieces = [chips[0][:count]]
    order = [EARLY] + [i for i in range(len(SQUARE_CHIPS)) if i != EARLY]
    for i, distance in enumerate(SQUARE_CHIPS):
        chip, place = divmod(order.index(i) + 1, 2)
        pieces.append(swapped(chips[chip][place * count : (place + 1) * count], distance))
    ending = in_vmem(ending_kernel, "endings", [real] * 4, across, raw)
    small = jax.ShapeDtypeStruct((count, width), jnp.bfloat16)
    leaving, staying = in_vmem(leave_kernel, "leave", [small, real], *pieces)
    other = swapped(leaving, SECTION + HALF)
    return tuple(finish(staying, other, *ending))


def per_device(fwd_act, fwd_routes, *rest):
    sections, devices = lax.axis_size("section"), lax.axis_size("expert")
    tokens, top_count = fwd_routes.shape[1:]
    router = rest[4]
    paired = sections == 2 and devices == 2 * SQUARE and router.shape == (16 * LANES, devices)
    paired = paired and tokens == 8 and top_count == TOP_COUNT
    plan = paired_plan if paired else routed_plan
    return plan(fwd_act, fwd_routes, *rest)


def solution(mesh):
    in_specs = (
        P("section", "expert", None),
        P("section", "expert", None),
        P("section", "expert", None),
        P("section", "expert", None),
        P("section", "expert", None),
        P("section", None),
        P(),
        P("expert", None, None),
        P("expert", None, None),
        P("expert", None, None),
    )
    out_specs = (P("section", "expert", None), P("section", "expert", None))
    return jax.shard_map(
        per_device, mesh=mesh, in_specs=in_specs, out_specs=out_specs, check_vma=False
    )
```

```python
import functools
import jax
import jax.numpy as jnp
from jax import lax
from jax.experimental import pallas as pl
from jax.experimental.pallas import tpu as pltpu
from jax.sharding import PartitionSpec as P

EPSILON = 1e-06


def shifted(block, axis, distance):
    devices = range(lax.axis_size(axis))
    route = [(i - distance, i) for i in devices if i - distance in devices]
    return lax.ppermute(block, axis, route)


def normalize(acts_in, gain_row):
    values = acts_in.astype(jnp.float32)
    factor = lax.rsqrt(jnp.mean(values * values, axis=-1, keepdims=True) + EPSILON)
    unit_rows = values * factor
    return ((unit_rows * gain_row).astype(jnp.bfloat16), unit_rows, factor)


def gate_values(normed, router, routes):
    logits = jnp.dot(normed, router, preferred_element_type=jnp.float32)
    chosen = jnp.take_along_axis(logits, routes, axis=1)
    raised = jnp.exp(chosen)
    return raised / jnp.sum(raised, axis=-1, keepdims=True)


def expert_forward(rows_in, gate_mat, up_mat, down_mat):
    pre_gate = jnp.dot(rows_in, gate_mat, preferred_element_type=jnp.float32)
    pre_up = jnp.dot(rows_in, up_mat, preferred_element_type=jnp.float32)
    sigma = jax.nn.sigmoid(pre_gate)
    hidden = (pre_gate * sigma * pre_up).astype(jnp.bfloat16)
    return jnp.dot(hidden, down_mat, preferred_element_type=jnp.float32).astype(jnp.bfloat16)


def expert_backward(rows_in, grads_in, gate_mat, up_mat, down_mat):
    pre_gate = jnp.dot(rows_in, gate_mat, preferred_element_type=jnp.float32)
    pre_up = jnp.dot(rows_in, up_mat, preferred_element_type=jnp.float32)
    sigma = jax.nn.sigmoid(pre_gate)
    silu_val = pre_gate * sigma
    hidden = (silu_val * pre_up).astype(jnp.bfloat16)
    expert_out = jnp.dot(hidden, down_mat, preferred_element_type=jnp.float32).astype(jnp.bfloat16)
    dgate = jnp.sum(grads_in.astype(jnp.float32) * expert_out.astype(jnp.float32), axis=-1).astype(
        jnp.bfloat16
    )
    contract = (((1,), (1,)), ((), ()))
    d_hidden = lax.dot_general(grads_in, down_mat, contract, preferred_element_type=jnp.float32)
    d_up = (d_hidden * silu_val).astype(jnp.bfloat16)
    d_pre = (d_hidden * pre_up * sigma * (1.0 + pre_gate * (1.0 - sigma))).astype(jnp.bfloat16)
    d_rows = lax.dot_general(d_pre, gate_mat, contract, preferred_element_type=jnp.float32)
    d_rows = d_rows + lax.dot_general(d_up, up_mat, contract, preferred_element_type=jnp.float32)
    return (d_rows.astype(jnp.bfloat16), dgate)


def input_gradient(gates, dgate, pair_grads, routes, router, unit_rows, factor, gain_row, grads_in):
    d_normed = jnp.sum(gates[:, :, None] * pair_grads, axis=1)
    d_chosen = gates * (dgate - jnp.sum(gates * dgate, axis=-1, keepdims=True))
    labels = jnp.arange(router.shape[1], dtype=jnp.int32)
    hits = (routes[:, :, None] == labels[None, None, :]).astype(jnp.float32)
    d_logits = jnp.sum(hits * d_chosen[:, :, None], axis=1)
    d_normed = d_normed + lax.dot_general(
        d_logits,
        router.astype(jnp.float32),
        (((1,), (1,)), ((), ())),
        precision=lax.Precision.HIGHEST,
    )
    d_unit = d_normed * gain_row
    result = factor * (d_unit - unit_rows * jnp.mean(d_unit * unit_rows, axis=-1, keepdims=True))
    return (result + grads_in.astype(jnp.float32)).astype(jnp.bfloat16)


def placement(routes, expert_count, capacity):
    flat_ids = routes.reshape(-1)
    labels = jnp.arange(expert_count, dtype=jnp.int32)
    onehot = (flat_ids[:, None] == labels[None, :]).astype(jnp.int32)
    before = jnp.cumsum(onehot, axis=0) - onehot
    slot_ids = jnp.sum(before * onehot, axis=1)
    target = flat_ids * capacity + slot_ids
    slot_labels = jnp.arange(expert_count * capacity, dtype=jnp.int32)
    select = (slot_labels[:, None] == target[None, :]).astype(jnp.bfloat16)
    spread = jnp.sum(
        select.reshape(expert_count * capacity, routes.shape[0], routes.shape[1]), axis=2
    )
    return (target, spread)


def dispatch(spread, rows_in, expert_count, capacity):
    placed = jnp.dot(spread, rows_in, preferred_element_type=jnp.float32).astype(jnp.bfloat16)
    return placed.reshape(expert_count, capacity, rows_in.shape[1])


def routed_plan(
    fwd_act, fwd_routes, bwd_saved, bwd_grad, bwd_routes, norm_gain, router, w_gate, w_up, w_down
):
    tok_count = fwd_act.shape[1]
    top_count = fwd_routes.shape[2]
    model_width = fwd_act.shape[2]
    expert_count = router.shape[1]
    capacity = min(tok_count, max(2, 2 * tok_count * top_count // expert_count))
    gain_row = norm_gain[0]
    gate_mat = w_gate[0]
    up_mat = w_up[0]
    down_mat = w_down[0]
    acts_f = fwd_act[0]
    routes_f = fwd_routes[0]
    normed_f, unused_unit, unused_factor = normalize(acts_f, gain_row)
    gates_f = gate_values(normed_f, router, routes_f)
    target_f, spread_f = placement(routes_f, expert_count, capacity)
    send_f = dispatch(spread_f, normed_f, expert_count, capacity)
    saved_b = bwd_saved[0]
    grads_b = bwd_grad[0]
    routes_b = bwd_routes[0]
    normed_b, unit_b, factor_b = normalize(saved_b, gain_row)
    gates_b = gate_values(normed_b, router, routes_b)
    target_b, spread_b = placement(routes_b, expert_count, capacity)
    send_x = dispatch(spread_b, normed_b, expert_count, capacity)
    send_g = dispatch(spread_b, grads_b, expert_count, capacity)
    rows_in = lax.all_to_all(send_f, "expert", split_axis=0, concat_axis=0, tiled=True)
    sources = rows_in.shape[0]
    slots = rows_in.shape[1]
    result = expert_forward(rows_in.reshape(-1, model_width), gate_mat, up_mat, down_mat)
    back_f = lax.all_to_all(
        result.reshape(sources, slots, model_width),
        "expert",
        split_axis=0,
        concat_axis=0,
        tiled=True,
    )
    rows_in = lax.all_to_all(send_x, "expert", split_axis=0, concat_axis=0, tiled=True)
    grads_in = lax.all_to_all(send_g, "expert", split_axis=0, concat_axis=0, tiled=True)
    sources = rows_in.shape[0]
    slots = rows_in.shape[1]
    d_rows, d_gates = expert_backward(
        rows_in.reshape(-1, model_width),
        grads_in.reshape(-1, model_width),
        gate_mat,
        up_mat,
        down_mat,
    )
    back_rows = lax.all_to_all(
        d_rows.reshape(sources, slots, model_width),
        "expert",
        split_axis=0,
        concat_axis=0,
        tiled=True,
    )
    back_gates = lax.all_to_all(
        d_gates.reshape(sources, slots), "expert", split_axis=0, concat_axis=0, tiled=True
    )
    picked_f = jnp.take(back_f.reshape(expert_count * capacity, model_width), target_f, axis=0)
    picked_f = picked_f.reshape(tok_count, top_count, model_width).astype(jnp.float32)
    layer_out = (
        acts_f.astype(jnp.float32) + jnp.sum(gates_f[:, :, None] * picked_f, axis=1)
    ).astype(jnp.bfloat16)
    fwd_next = shifted(layer_out[None], "section", 1)
    pair_grads = jnp.take(back_rows.reshape(expert_count * capacity, model_width), target_b, axis=0)
    pair_grads = pair_grads.reshape(tok_count, top_count, model_width).astype(jnp.float32)
    dgate = (
        jnp.take(back_gates.reshape(-1), target_b, axis=0)
        .reshape(tok_count, top_count)
        .astype(jnp.float32)
    )
    d_input = input_gradient(
        gates_b, dgate, pair_grads, routes_b, router, unit_b, factor_b, gain_row, grads_b
    )
    grad_prev = shifted(d_input[None], "section", -1)
    return (fwd_next, grad_prev)


AXES = ("section", "expert")
SQUARE = 8
CORE, HALF, SECTION = 1, 9, 16
EARLY = 2
LANES = 128
SQUARE_CHIPS = (3, 5, 7)
TOP_COUNT = 8
VMEM = pl.BlockSpec(memory_space=pltpu.VMEM)
SMEM = pl.BlockSpec(memory_space=pltpu.SMEM)
HBM = pl.BlockSpec(memory_space=pltpu.HBM)
MIB = 1024 * 1024


def swapped(block, distance):
    count = lax.axis_size(AXES)
    return lax.ppermute(block, AXES, [(i, i ^ distance) for i in range(count)])


def in_hbm(array):
    return pltpu.with_memory_space_constraint(array, pltpu.HBM)


def root_factor(values):
    return lax.rsqrt(jnp.mean(values * values, axis=-1, keepdims=True) + EPSILON)


def in_first_section():
    return lax.axis_index("section") == 0


def pack_kernel(
    fwd_act, fwd_routes, bwd_saved, bwd_grad, bwd_routes, gain, router,
    rows_ref, acts_ref, gain_ref, router_ref, grads_ref, routes_ref, sems,
):
    first_section = in_first_section()
    grad_copy = pltpu.make_async_copy(bwd_grad.at[0], grads_ref, sems.at[0])
    gain_copy = pltpu.make_async_copy(gain, gain_ref, sems.at[1])
    router_copy = pltpu.make_async_copy(router, router_ref, sems.at[4])

    @pl.when(first_section)
    def _():
        pltpu.make_async_copy(fwd_act.at[0], acts_ref, sems.at[2]).start()
        pltpu.make_async_copy(fwd_routes.at[0], routes_ref, sems.at[3]).start()

    @pl.when(jnp.logical_not(first_section))
    def _():
        pltpu.make_async_copy(bwd_saved.at[0], acts_ref, sems.at[2]).start()
        pltpu.make_async_copy(bwd_routes.at[0], routes_ref, sems.at[3]).start()

    gain_copy.start()
    grad_copy.start()
    router_copy.start()
    pltpu.make_async_copy(fwd_act.at[0], acts_ref, sems.at[2]).wait()
    gain_copy.wait()
    acts = acts_ref[...].astype(jnp.float32)
    normed = acts * root_factor(acts) * gain_ref[...]
    pltpu.make_async_copy(fwd_routes.at[0], routes_ref, sems.at[3]).wait()
    grad_copy.wait()
    routes = routes_ref[...].astype(jnp.float32)
    blank = jnp.zeros_like(routes)
    routes = jnp.concatenate(
        [
            jnp.where(first_section, routes, blank),
            jnp.where(first_section, blank, routes),
            jnp.zeros((routes.shape[0], LANES - 2 * TOP_COUNT), jnp.float32),
        ],
        axis=1,
    )
    rows_ref[...] = jnp.concatenate(
        [normed, grads_ref[...].astype(jnp.float32), routes], axis=1
    ).astype(jnp.bfloat16)
    router_copy.wait()


def pack_rows(*arrays):
    fwd_act, fwd_routes, _, _, _, gain, router = arrays
    count, width = fwd_act.shape[1:]
    return pl.pallas_call(
        pack_kernel,
        out_shape=[
            jax.ShapeDtypeStruct((count, 2 * width + LANES), jnp.bfloat16),
            jax.ShapeDtypeStruct((count, width), jnp.bfloat16),
            jax.ShapeDtypeStruct(gain.shape, gain.dtype),
            jax.ShapeDtypeStruct(router.shape, router.dtype),
        ],
        in_specs=[HBM] * 7,
        out_specs=[VMEM] * 4,
        scratch_shapes=[
            pltpu.VMEM((count, width), jnp.bfloat16),
            pltpu.VMEM(fwd_routes.shape[1:], jnp.int32),
            pltpu.SemaphoreType.DMA((5,)),
        ],
        compiler_params=pltpu.CompilerParams(vmem_limit_bytes=4 * MIB),
        name="pack",
    )(*[in_hbm(x) for x in arrays])


def widen_kernel(acts_ref, gain_ref, raw_ref):
    gain_row = gain_ref[...]
    count = acts_ref.shape[0]
    pieces = [gain_row[:, k : k + LANES] for k in range(0, gain_row.shape[1], LANES)]
    gain_rows = jnp.concatenate(
        [jnp.concatenate(pieces[k : k + count], axis=0) for k in range(0, len(pieces), count)],
        axis=1,
    )
    gain_high = gain_rows.astype(jnp.bfloat16).astype(jnp.float32)
    raw_ref[...] = jnp.concatenate(
        [acts_ref[...].astype(jnp.float32), gain_high, gain_rows - gain_high], axis=1
    ).astype(jnp.bfloat16)


def in_vmem(body, name, out_shape, *arrays):
    return pl.pallas_call(
        body,
        out_shape=out_shape,
        in_specs=[VMEM] * len(arrays),
        out_specs=[VMEM] * len(out_shape),
        compiler_params=pltpu.CompilerParams(vmem_limit_bytes=4 * MIB),
        name=name,
    )(*arrays)


def merge_kernel(along_ref, across_ref, mine_ref):
    width = (across_ref.shape[1] - LANES) // 2
    first_section = in_first_section()

    def merge(forward_ref, backward_ref):
        mine_ref[:, :width] = forward_ref[:, :width]
        mine_ref[:, width : 3 * width] = backward_ref[:, : 2 * width]

    @pl.when(first_section)
    def _():
        merge(along_ref, across_ref)

    @pl.when(jnp.logical_not(first_section))
    def _():
        merge(across_ref, along_ref)

    tail = slice(2 * width, 2 * width + LANES)
    mine_ref[:, 3 * width :] = along_ref[:, tail] + across_ref[:, tail]


def leave_kernel(a_ref, b_ref, c_ref, d_ref, leaving_ref, staying_ref):
    first_section = in_first_section()
    width = leaving_ref.shape[1]
    total = a_ref[...].astype(jnp.float32) + b_ref[...].astype(jnp.float32)
    total = total + c_ref[...].astype(jnp.float32) + d_ref[...].astype(jnp.float32)
    forward, backward = total[:, :width], total[:, width:]
    leaving_ref[...] = jnp.where(first_section, forward, backward).astype(jnp.bfloat16)
    staying_ref[...] = jnp.where(first_section, backward, forward)


def finish_kernel(
    staying_ref, other_ref, scale_ref, towards_ref, back_ref, rest_ref, fwd_hbm, grad_hbm,
    result_ref, nothing_ref, sems,
):
    first_section = in_first_section()
    nothing_ref[...] = jnp.zeros_like(nothing_ref)

    @pl.when(first_section)
    def _():
        pltpu.make_async_copy(nothing_ref, fwd_hbm.at[0], sems.at[0]).start()

    @pl.when(jnp.logical_not(first_section))
    def _():
        pltpu.make_async_copy(nothing_ref, grad_hbm.at[0], sems.at[0]).start()

    sums = staying_ref[...] + other_ref[...].astype(jnp.float32)
    mean = jnp.mean(sums * towards_ref[...], axis=-1, keepdims=True)
    result = sums * scale_ref[...] + rest_ref[...] - back_ref[...] * mean
    result_ref[...] = result.astype(jnp.bfloat16)

    @pl.when(first_section)
    def _():
        pltpu.make_async_copy(result_ref, grad_hbm.at[0], sems.at[1]).start()

    @pl.when(jnp.logical_not(first_section))
    def _():
        pltpu.make_async_copy(result_ref, fwd_hbm.at[0], sems.at[1]).start()

    pltpu.make_async_copy(nothing_ref, fwd_hbm.at[0], sems.at[0]).wait()
    pltpu.make_async_copy(result_ref, grad_hbm.at[0], sems.at[1]).wait()


def finish(*arrays):
    count, width = arrays[0].shape
    return pl.pallas_call(
        finish_kernel,
        out_shape=[jax.ShapeDtypeStruct((1, count, width), jnp.bfloat16)] * 2,
        in_specs=[VMEM] * len(arrays),
        out_specs=[HBM] * 2,
        scratch_shapes=[
            pltpu.VMEM((count, width), jnp.bfloat16),
            pltpu.VMEM((count, width), jnp.bfloat16),
            pltpu.SemaphoreType.DMA((2,)),
        ],
        compiler_params=pltpu.CompilerParams(vmem_limit_bytes=4 * MIB),
        name="finish",
    )(*arrays)


def fetch_kernel(*refs, parts):
    count = len(parts)
    weights, held_refs, turned_refs = refs[:count], refs[count : 2 * count], refs[2 * count : 3 * count]
    sems = refs[-1]
    step = 256
    waiting = []
    for (first, rows), source, held, turned in zip(parts, weights, held_refs, turned_refs):
        for k in range(rows // step):
            copy = pltpu.make_async_copy(
                source.at[pl.ds(first + k * step, step)],
                held.at[pl.ds(k * step, step)],
                sems.at[len(waiting)],
            )
            copy.start()
            waiting.append((copy, held, turned, k * step))
    for copy, held, turned, start in waiting:
        copy.wait()
        turned[:, start : start + step] = held[start : start + step, :].T


def fetched(*parts):
    weights = [w for w, _, _ in parts]
    sizes = tuple((first, rows) for _, first, rows in parts)
    moved = sum(rows * w.shape[1] for w, _, rows in parts)
    held = [jax.ShapeDtypeStruct((rows, w.shape[1]), w.dtype) for w, _, rows in parts]
    turned = [jax.ShapeDtypeStruct((w.shape[1], rows), w.dtype) for w, _, rows in parts]
    outs = pl.pallas_call(
        functools.partial(fetch_kernel, parts=sizes),
        out_shape=held + turned,
        in_specs=[HBM] * len(parts),
        out_specs=[VMEM] * (2 * len(parts)),
        scratch_shapes=[pltpu.SemaphoreType.DMA((sum(rows for _, rows in sizes) // 256,))],
        compiler_params=pltpu.CompilerParams(vmem_limit_bytes=8 * MIB),
        cost_estimate=pl.CostEstimate(flops=0, bytes_accessed=4 * moved, transcendentals=0),
        name="fetch",
    )(*[in_hbm(w) for w in weights])
    return tuple(zip(outs[: len(parts)], outs[len(parts) :]))


def expert_kernel(
    near_ref, next_ref, far_ref, last_ref, router_ref,
    gate_ref, gate_turned_ref, down_ref, down_turned_ref, *refs,
):
    up_refs, up_turned_refs, out_refs = refs[:-4:2], refs[1:-4:2], refs[-4:]
    width, hidden_count = gate_ref.shape
    step = 256
    own_expert = lax.axis_index("expert")

    def both(first, last):
        blocks = (near_ref, next_ref, far_ref, last_ref)
        return jnp.concatenate([block[:, first:last] for block in blocks], axis=0)

    normed = jnp.concatenate([both(0, width), both(width, 2 * width)], axis=0)
    grads = both(2 * width, 3 * width)
    routes = both(3 * width, 3 * width + LANES).astype(jnp.float32)
    routes = jnp.concatenate([routes[:, :TOP_COUNT], routes[:, TOP_COUNT : 2 * TOP_COUNT]], axis=0)
    half = grads.shape[0]

    router = router_ref[...]
    contract = (((1,), (1,)), ((), ()))
    logits = lax.dot_general(normed, router, contract, preferred_element_type=jnp.float32)
    labels = lax.broadcasted_iota(jnp.int32, logits.shape, 1)
    labels_real = labels.astype(jnp.float32)
    chosen = routes[:, 0:1] == labels_real
    for k in range(1, TOP_COUNT):
        chosen = jnp.logical_or(chosen, routes[:, k : k + 1] == labels_real)
    raised = jnp.where(chosen, jnp.exp(logits), 0.0)
    gates = raised / jnp.sum(raised, axis=-1, keepdims=True)
    own = jnp.where(labels == own_expert, 1.0, 0.0)
    gate_own = jnp.sum(own * gates, axis=-1, keepdims=True)
    gate_f, gate_b = gate_own[:half], gate_own[half:]

    hiddens, d_pres, d_ups = [], [], []
    dgate = 0.0
    for piece in range(hidden_count // step):
        cols = slice(piece * step, piece * step + step)
        pre_gate = jnp.dot(normed, gate_ref[:, cols], preferred_element_type=jnp.float32)
        pre_up, start = 0.0, 0
        for ref in up_refs:
            rows = normed[:, start : start + ref.shape[0]]
            pre_up = pre_up + jnp.dot(rows, ref[:, cols], preferred_element_type=jnp.float32)
            start += ref.shape[0]
        d_hidden = jnp.dot(grads, down_turned_ref[:, cols], preferred_element_type=jnp.float32)
        sigma = jax.nn.sigmoid(pre_gate)
        silu_val = pre_gate * sigma
        hidden = silu_val * pre_up
        hiddens.append((hidden[:half] * gate_f).astype(jnp.bfloat16))
        dgate = dgate + jnp.sum(hidden[half:] * d_hidden, axis=-1, keepdims=True)
        d_hidden = d_hidden * gate_b
        d_ups.append((d_hidden * silu_val[half:]).astype(jnp.bfloat16))
        sigma_b = sigma[half:]
        slope = sigma_b * (1.0 + pre_gate[half:] * (1.0 - sigma_b))
        d_pres.append((d_hidden * pre_up[half:] * slope).astype(jnp.bfloat16))

    hidden = jnp.concatenate(hiddens, axis=1)
    d_pre = jnp.concatenate(d_pres, axis=1)
    d_up = jnp.concatenate(d_ups, axis=1)
    out_f = jnp.dot(hidden, down_ref[...], preferred_element_type=jnp.float32)
    d_normed = jnp.concatenate(
        [
            jnp.dot(d_up, mat[...], preferred_element_type=jnp.float32)
            for mat in up_turned_refs
        ],
        axis=1,
    )
    d_normed = d_normed + jnp.dot(d_pre, gate_turned_ref[...], preferred_element_type=jnp.float32)
    spread = gate_b * dgate * (own[half:] - gates[half:])
    spread_high = spread.astype(jnp.bfloat16)
    spread_low = (spread - spread_high.astype(jnp.float32)).astype(jnp.bfloat16)
    d_normed = d_normed + jnp.dot(
        jnp.concatenate([spread_high, spread_low], axis=1),
        jnp.concatenate([router, router], axis=0),
        preferred_element_type=jnp.float32,
    )

    count = half // len(out_refs)
    for k, ref in enumerate(out_refs):
        rows = slice(k * count, (k + 1) * count)
        ref[...] = jnp.concatenate([out_f[rows], d_normed[rows]], axis=1).astype(jnp.bfloat16)


def run_experts(blocks, router, *weights):
    width = router.shape[1]
    return pl.pallas_call(
        expert_kernel,
        out_shape=[jax.ShapeDtypeStruct((b.shape[0], 2 * width), jnp.bfloat16) for b in blocks],
        in_specs=[VMEM] * (1 + len(blocks) + len(weights)),
        out_specs=[VMEM] * len(blocks),
        compiler_params=pltpu.CompilerParams(vmem_limit_bytes=24 * MIB),
        name="experts",
    )(*blocks, router, *weights)


def ending_kernel(across_ref, raw_ref, scale_ref, along_ref, back_ref, rest_ref):
    first_section = in_first_section()
    count, width = scale_ref.shape
    grads = across_ref[...].astype(jnp.float32)[:, width : 2 * width]
    raw = raw_ref[...].astype(jnp.float32)
    acts, gain_rows = raw[:, :width], raw[:, width:]
    spread = width // count
    gain_rows = gain_rows[:, :spread] + gain_rows[:, spread:]
    gain_row = jnp.concatenate(
        [
            gain_rows[row : row + 1, k : k + LANES]
            for k in range(0, spread, LANES)
            for row in range(count)
        ],
        axis=1,
    )
    factor = root_factor(acts)
    unit = acts * factor
    scale_ref[...] = jnp.where(first_section, factor * gain_row, 1.0)
    along_ref[...] = jnp.where(first_section, unit * gain_row, 0.0)
    back_ref[...] = jnp.where(first_section, unit * factor, 0.0)
    rest_ref[...] = jnp.where(first_section, grads, acts)


def added(*blocks):
    return sum(block.astype(jnp.float32) for block in blocks).astype(jnp.bfloat16)


def paired_plan(
    fwd_act, fwd_routes, bwd_saved, bwd_grad, bwd_routes, norm_gain, router, w_gate, w_up, w_down
):
    count, width = fwd_act.shape[1:]
    own, acts, gain_row, router_rows = pack_rows(
        fwd_act, fwd_routes, bwd_saved, bwd_grad, bwd_routes, norm_gain, router.T
    )
    across = swapped(own, SECTION)
    along = swapped(own, HALF)
    cuts = (width // 2, width)
    gate_hbm, up_hbm, down_hbm = w_gate[0], w_up[0], w_down[0]
    gate_mats, *ups = fetched((gate_hbm, 0, width), (up_hbm, 0, cuts[0]))
    along, gate_mats, ups = lax.optimization_barrier((along, gate_mats, ups))
    rows = jax.ShapeDtypeStruct((count, 3 * width + LANES), jnp.bfloat16)
    mine = in_vmem(merge_kernel, "merge", [rows], along, across)[0]
    down_hbm, up_hbm, _ = lax.optimization_barrier((down_hbm, up_hbm, mine))
    down_mats, *more = fetched(
        (down_hbm, 0, down_hbm.shape[0]), (up_hbm, cuts[0], cuts[1] - cuts[0])
    )
    ups = ups + more
    received = [swapped(mine, k) for k in SQUARE_CHIPS]
    early = jnp.concatenate([mine, received[EARLY]], axis=0)
    late = jnp.concatenate([b for i, b in enumerate(received) if i != EARLY], axis=0)
    early, ups, down_mats = lax.optimization_barrier((early, ups, down_mats))
    last = [swapped(b, CORE) for i, b in enumerate(received) if i != EARLY]
    blocks = [early, late, swapped(early, CORE), jnp.concatenate(last, axis=0)]

    weights = [m for mats in [gate_mats, down_mats] + ups for m in mats]
    kept = run_experts(blocks, router_rows, *weights)
    chips = [added(block, swapped(sent, CORE)) for block, sent in zip(kept[:2], kept[2:])]
    acts, last_chip = lax.optimization_barrier((acts, chips[1]))
    chips = [chips[0], last_chip]
    real = jax.ShapeDtypeStruct((count, width), jnp.float32)
    wide = jax.ShapeDtypeStruct((count, width + 2 * (width // count)), jnp.bfloat16)
    raw = swapped(in_vmem(widen_kernel, "widen", [wide], acts, gain_row)[0], SECTION)
    pieces = [chips[0][:count]]
    order = [EARLY] + [i for i in range(len(SQUARE_CHIPS)) if i != EARLY]
    for i, distance in enumerate(SQUARE_CHIPS):
        chip, place = divmod(order.index(i) + 1, 2)
        pieces.append(swapped(chips[chip][place * count : (place + 1) * count], distance))
    ending = in_vmem(ending_kernel, "endings", [real] * 4, across, raw)
    small = jax.ShapeDtypeStruct((count, width), jnp.bfloat16)
    leaving, staying = in_vmem(leave_kernel, "leave", [small, real], *pieces)
    other = swapped(leaving, SECTION + HALF)
    return tuple(finish(staying, other, *ending))


def per_device(fwd_act, fwd_routes, *rest):
    sections, devices = lax.axis_size("section"), lax.axis_size("expert")
    tokens, top_count = fwd_routes.shape[1:]
    router = rest[4]
    paired = sections == 2 and devices == 2 * SQUARE and router.shape == (16 * LANES, devices)
    paired = paired and tokens == 8 and top_count == TOP_COUNT
    plan = paired_plan if paired else routed_plan
    return plan(fwd_act, fwd_routes, *rest)


def solution(mesh):
    in_specs = (
        P("section", "expert", None),
        P("section", "expert", None),
        P("section", "expert", None),
        P("section", "expert", None),
        P("section", "expert", None),
        P("section", None),
        P(),
        P("expert", None, None),
        P("expert", None, None),
        P("expert", None, None),
    )
    out_specs = (P("section", "expert", None), P("section", "expert", None))
    return jax.shard_map(
        per_device, mesh=mesh, in_specs=in_specs, out_specs=out_specs, check_vma=False
    )
```

```python
import functools
import jax
import jax.numpy as jnp
from jax import lax
from jax.experimental import pallas as pl
from jax.experimental.pallas import tpu as pltpu
from jax.sharding import PartitionSpec as P

EPSILON = 1e-06


def shifted(block, axis, distance):
    devices = range(lax.axis_size(axis))
    route = [(i - distance, i) for i in devices if i - distance in devices]
    return lax.ppermute(block, axis, route)


def normalize(acts_in, gain_row):
    values = acts_in.astype(jnp.float32)
    factor = lax.rsqrt(jnp.mean(values * values, axis=-1, keepdims=True) + EPSILON)
    unit_rows = values * factor
    return ((unit_rows * gain_row).astype(jnp.bfloat16), unit_rows, factor)


def gate_values(normed, router, routes):
    logits = jnp.dot(normed, router, preferred_element_type=jnp.float32)
    chosen = jnp.take_along_axis(logits, routes, axis=1)
    raised = jnp.exp(chosen)
    return raised / jnp.sum(raised, axis=-1, keepdims=True)


def expert_forward(rows_in, gate_mat, up_mat, down_mat):
    pre_gate = jnp.dot(rows_in, gate_mat, preferred_element_type=jnp.float32)
    pre_up = jnp.dot(rows_in, up_mat, preferred_element_type=jnp.float32)
    sigma = jax.nn.sigmoid(pre_gate)
    hidden = (pre_gate * sigma * pre_up).astype(jnp.bfloat16)
    return jnp.dot(hidden, down_mat, preferred_element_type=jnp.float32).astype(jnp.bfloat16)


def expert_backward(rows_in, grads_in, gate_mat, up_mat, down_mat):
    pre_gate = jnp.dot(rows_in, gate_mat, preferred_element_type=jnp.float32)
    pre_up = jnp.dot(rows_in, up_mat, preferred_element_type=jnp.float32)
    sigma = jax.nn.sigmoid(pre_gate)
    silu_val = pre_gate * sigma
    hidden = (silu_val * pre_up).astype(jnp.bfloat16)
    expert_out = jnp.dot(hidden, down_mat, preferred_element_type=jnp.float32).astype(jnp.bfloat16)
    dgate = jnp.sum(grads_in.astype(jnp.float32) * expert_out.astype(jnp.float32), axis=-1).astype(
        jnp.bfloat16
    )
    contract = (((1,), (1,)), ((), ()))
    d_hidden = lax.dot_general(grads_in, down_mat, contract, preferred_element_type=jnp.float32)
    d_up = (d_hidden * silu_val).astype(jnp.bfloat16)
    d_pre = (d_hidden * pre_up * sigma * (1.0 + pre_gate * (1.0 - sigma))).astype(jnp.bfloat16)
    d_rows = lax.dot_general(d_pre, gate_mat, contract, preferred_element_type=jnp.float32)
    d_rows = d_rows + lax.dot_general(d_up, up_mat, contract, preferred_element_type=jnp.float32)
    return (d_rows.astype(jnp.bfloat16), dgate)


def input_gradient(gates, dgate, pair_grads, routes, router, unit_rows, factor, gain_row, grads_in):
    d_normed = jnp.sum(gates[:, :, None] * pair_grads, axis=1)
    d_chosen = gates * (dgate - jnp.sum(gates * dgate, axis=-1, keepdims=True))
    labels = jnp.arange(router.shape[1], dtype=jnp.int32)
    hits = (routes[:, :, None] == labels[None, None, :]).astype(jnp.float32)
    d_logits = jnp.sum(hits * d_chosen[:, :, None], axis=1)
    d_normed = d_normed + lax.dot_general(
        d_logits,
        router.astype(jnp.float32),
        (((1,), (1,)), ((), ())),
        precision=lax.Precision.HIGHEST,
    )
    d_unit = d_normed * gain_row
    result = factor * (d_unit - unit_rows * jnp.mean(d_unit * unit_rows, axis=-1, keepdims=True))
    return (result + grads_in.astype(jnp.float32)).astype(jnp.bfloat16)


def placement(routes, expert_count, capacity):
    flat_ids = routes.reshape(-1)
    labels = jnp.arange(expert_count, dtype=jnp.int32)
    onehot = (flat_ids[:, None] == labels[None, :]).astype(jnp.int32)
    before = jnp.cumsum(onehot, axis=0) - onehot
    slot_ids = jnp.sum(before * onehot, axis=1)
    target = flat_ids * capacity + slot_ids
    slot_labels = jnp.arange(expert_count * capacity, dtype=jnp.int32)
    select = (slot_labels[:, None] == target[None, :]).astype(jnp.bfloat16)
    spread = jnp.sum(
        select.reshape(expert_count * capacity, routes.shape[0], routes.shape[1]), axis=2
    )
    return (target, spread)


def dispatch(spread, rows_in, expert_count, capacity):
    placed = jnp.dot(spread, rows_in, preferred_element_type=jnp.float32).astype(jnp.bfloat16)
    return placed.reshape(expert_count, capacity, rows_in.shape[1])


def routed_plan(
    fwd_act, fwd_routes, bwd_saved, bwd_grad, bwd_routes, norm_gain, router, w_gate, w_up, w_down
):
    tok_count = fwd_act.shape[1]
    top_count = fwd_routes.shape[2]
    model_width = fwd_act.shape[2]
    expert_count = router.shape[1]
    capacity = min(tok_count, max(2, 2 * tok_count * top_count // expert_count))
    gain_row = norm_gain[0]
    gate_mat = w_gate[0]
    up_mat = w_up[0]
    down_mat = w_down[0]
    acts_f = fwd_act[0]
    routes_f = fwd_routes[0]
    normed_f, unused_unit, unused_factor = normalize(acts_f, gain_row)
    gates_f = gate_values(normed_f, router, routes_f)
    target_f, spread_f = placement(routes_f, expert_count, capacity)
    send_f = dispatch(spread_f, normed_f, expert_count, capacity)
    saved_b = bwd_saved[0]
    grads_b = bwd_grad[0]
    routes_b = bwd_routes[0]
    normed_b, unit_b, factor_b = normalize(saved_b, gain_row)
    gates_b = gate_values(normed_b, router, routes_b)
    target_b, spread_b = placement(routes_b, expert_count, capacity)
    send_x = dispatch(spread_b, normed_b, expert_count, capacity)
    send_g = dispatch(spread_b, grads_b, expert_count, capacity)
    rows_in = lax.all_to_all(send_f, "expert", split_axis=0, concat_axis=0, tiled=True)
    sources = rows_in.shape[0]
    slots = rows_in.shape[1]
    result = expert_forward(rows_in.reshape(-1, model_width), gate_mat, up_mat, down_mat)
    back_f = lax.all_to_all(
        result.reshape(sources, slots, model_width),
        "expert",
        split_axis=0,
        concat_axis=0,
        tiled=True,
    )
    rows_in = lax.all_to_all(send_x, "expert", split_axis=0, concat_axis=0, tiled=True)
    grads_in = lax.all_to_all(send_g, "expert", split_axis=0, concat_axis=0, tiled=True)
    sources = rows_in.shape[0]
    slots = rows_in.shape[1]
    d_rows, d_gates = expert_backward(
        rows_in.reshape(-1, model_width),
        grads_in.reshape(-1, model_width),
        gate_mat,
        up_mat,
        down_mat,
    )
    back_rows = lax.all_to_all(
        d_rows.reshape(sources, slots, model_width),
        "expert",
        split_axis=0,
        concat_axis=0,
        tiled=True,
    )
    back_gates = lax.all_to_all(
        d_gates.reshape(sources, slots), "expert", split_axis=0, concat_axis=0, tiled=True
    )
    picked_f = jnp.take(back_f.reshape(expert_count * capacity, model_width), target_f, axis=0)
    picked_f = picked_f.reshape(tok_count, top_count, model_width).astype(jnp.float32)
    layer_out = (
        acts_f.astype(jnp.float32) + jnp.sum(gates_f[:, :, None] * picked_f, axis=1)
    ).astype(jnp.bfloat16)
    fwd_next = shifted(layer_out[None], "section", 1)
    pair_grads = jnp.take(back_rows.reshape(expert_count * capacity, model_width), target_b, axis=0)
    pair_grads = pair_grads.reshape(tok_count, top_count, model_width).astype(jnp.float32)
    dgate = (
        jnp.take(back_gates.reshape(-1), target_b, axis=0)
        .reshape(tok_count, top_count)
        .astype(jnp.float32)
    )
    d_input = input_gradient(
        gates_b, dgate, pair_grads, routes_b, router, unit_b, factor_b, gain_row, grads_b
    )
    grad_prev = shifted(d_input[None], "section", -1)
    return (fwd_next, grad_prev)


AXES = ("section", "expert")
SQUARE = 8
CORE, HALF, SECTION = 1, 9, 16
EARLY = 2
LANES = 128
SQUARE_CHIPS = (3, 5, 7)
TOP_COUNT = 8
VMEM = pl.BlockSpec(memory_space=pltpu.VMEM)
SMEM = pl.BlockSpec(memory_space=pltpu.SMEM)
HBM = pl.BlockSpec(memory_space=pltpu.HBM)
MIB = 1024 * 1024


def swapped(block, distance):
    count = lax.axis_size(AXES)
    return lax.ppermute(block, AXES, [(i, i ^ distance) for i in range(count)])


def in_hbm(array):
    return pltpu.with_memory_space_constraint(array, pltpu.HBM)


def root_factor(values):
    return lax.rsqrt(jnp.mean(values * values, axis=-1, keepdims=True) + EPSILON)


def in_first_section():
    return lax.axis_index("section") == 0


def pack_kernel(
    fwd_act, fwd_routes, bwd_saved, bwd_grad, bwd_routes, gain, router,
    rows_ref, acts_ref, gain_ref, router_ref, grads_ref, routes_ref, sems,
):
    first_section = in_first_section()
    grad_copy = pltpu.make_async_copy(bwd_grad.at[0], grads_ref, sems.at[0])
    gain_copy = pltpu.make_async_copy(gain, gain_ref, sems.at[1])
    router_copy = pltpu.make_async_copy(router, router_ref, sems.at[4])

    @pl.when(first_section)
    def _():
        pltpu.make_async_copy(fwd_act.at[0], acts_ref, sems.at[2]).start()
        pltpu.make_async_copy(fwd_routes.at[0], routes_ref, sems.at[3]).start()

    @pl.when(jnp.logical_not(first_section))
    def _():
        pltpu.make_async_copy(bwd_saved.at[0], acts_ref, sems.at[2]).start()
        pltpu.make_async_copy(bwd_routes.at[0], routes_ref, sems.at[3]).start()

    gain_copy.start()
    grad_copy.start()
    router_copy.start()
    pltpu.make_async_copy(fwd_act.at[0], acts_ref, sems.at[2]).wait()
    gain_copy.wait()
    acts = acts_ref[...].astype(jnp.float32)
    normed = acts * root_factor(acts) * gain_ref[...]
    pltpu.make_async_copy(fwd_routes.at[0], routes_ref, sems.at[3]).wait()
    grad_copy.wait()
    routes = routes_ref[...].astype(jnp.float32)
    blank = jnp.zeros_like(routes)
    routes = jnp.concatenate(
        [
            jnp.where(first_section, routes, blank),
            jnp.where(first_section, blank, routes),
            jnp.zeros((routes.shape[0], LANES - 2 * TOP_COUNT), jnp.float32),
        ],
        axis=1,
    )
    rows_ref[...] = jnp.concatenate(
        [normed, grads_ref[...].astype(jnp.float32), routes], axis=1
    ).astype(jnp.bfloat16)
    router_copy.wait()


def pack_rows(*arrays):
    fwd_act, fwd_routes, _, _, _, gain, router = arrays
    count, width = fwd_act.shape[1:]
    return pl.pallas_call(
        pack_kernel,
        out_shape=[
            jax.ShapeDtypeStruct((count, 2 * width + LANES), jnp.bfloat16),
            jax.ShapeDtypeStruct((count, width), jnp.bfloat16),
            jax.ShapeDtypeStruct(gain.shape, gain.dtype),
            jax.ShapeDtypeStruct(router.shape, router.dtype),
        ],
        in_specs=[HBM] * 7,
        out_specs=[VMEM] * 4,
        scratch_shapes=[
            pltpu.VMEM((count, width), jnp.bfloat16),
            pltpu.VMEM(fwd_routes.shape[1:], jnp.int32),
            pltpu.SemaphoreType.DMA((5,)),
        ],
        compiler_params=pltpu.CompilerParams(vmem_limit_bytes=4 * MIB),
        name="pack",
    )(*[in_hbm(x) for x in arrays])


def widen_kernel(acts_ref, gain_ref, raw_ref):
    gain_row = gain_ref[...]
    count = acts_ref.shape[0]
    pieces = [gain_row[:, k : k + LANES] for k in range(0, gain_row.shape[1], LANES)]
    gain_rows = jnp.concatenate(
        [jnp.concatenate(pieces[k : k + count], axis=0) for k in range(0, len(pieces), count)],
        axis=1,
    )
    gain_high = gain_rows.astype(jnp.bfloat16).astype(jnp.float32)
    raw_ref[...] = jnp.concatenate(
        [acts_ref[...].astype(jnp.float32), gain_high, gain_rows - gain_high], axis=1
    ).astype(jnp.bfloat16)


def in_vmem(body, name, out_shape, *arrays):
    return pl.pallas_call(
        body,
        out_shape=out_shape,
        in_specs=[VMEM] * len(arrays),
        out_specs=[VMEM] * len(out_shape),
        compiler_params=pltpu.CompilerParams(vmem_limit_bytes=4 * MIB),
        name=name,
    )(*arrays)


def merge_kernel(along_ref, across_ref, mine_ref):
    width = (across_ref.shape[1] - LANES) // 2
    first_section = in_first_section()

    def merge(forward_ref, backward_ref):
        mine_ref[:, :width] = forward_ref[:, :width]
        mine_ref[:, width : 3 * width] = backward_ref[:, : 2 * width]

    @pl.when(first_section)
    def _():
        merge(along_ref, across_ref)

    @pl.when(jnp.logical_not(first_section))
    def _():
        merge(across_ref, along_ref)

    tail = slice(2 * width, 2 * width + LANES)
    mine_ref[:, 3 * width :] = along_ref[:, tail] + across_ref[:, tail]


def leave_kernel(a_ref, b_ref, c_ref, d_ref, leaving_ref, staying_ref):
    first_section = in_first_section()
    width = leaving_ref.shape[1]
    total = a_ref[...].astype(jnp.float32) + b_ref[...].astype(jnp.float32)
    total = total + c_ref[...].astype(jnp.float32) + d_ref[...].astype(jnp.float32)
    forward, backward = total[:, :width], total[:, width:]
    leaving_ref[...] = jnp.where(first_section, forward, backward).astype(jnp.bfloat16)
    staying_ref[...] = jnp.where(first_section, backward, forward)


def finish_kernel(
    staying_ref, other_ref, scale_ref, towards_ref, back_ref, rest_ref, fwd_hbm, grad_hbm,
    result_ref, nothing_ref, sems,
):
    first_section = in_first_section()
    nothing_ref[...] = jnp.zeros_like(nothing_ref)

    @pl.when(first_section)
    def _():
        pltpu.make_async_copy(nothing_ref, fwd_hbm.at[0], sems.at[0]).start()

    @pl.when(jnp.logical_not(first_section))
    def _():
        pltpu.make_async_copy(nothing_ref, grad_hbm.at[0], sems.at[0]).start()

    sums = staying_ref[...] + other_ref[...].astype(jnp.float32)
    mean = jnp.mean(sums * towards_ref[...], axis=-1, keepdims=True)
    result = sums * scale_ref[...] + rest_ref[...] - back_ref[...] * mean
    result_ref[...] = result.astype(jnp.bfloat16)

    @pl.when(first_section)
    def _():
        pltpu.make_async_copy(result_ref, grad_hbm.at[0], sems.at[1]).start()

    @pl.when(jnp.logical_not(first_section))
    def _():
        pltpu.make_async_copy(result_ref, fwd_hbm.at[0], sems.at[1]).start()

    pltpu.make_async_copy(nothing_ref, fwd_hbm.at[0], sems.at[0]).wait()
    pltpu.make_async_copy(result_ref, grad_hbm.at[0], sems.at[1]).wait()


def finish(*arrays):
    count, width = arrays[0].shape
    return pl.pallas_call(
        finish_kernel,
        out_shape=[jax.ShapeDtypeStruct((1, count, width), jnp.bfloat16)] * 2,
        in_specs=[VMEM] * len(arrays),
        out_specs=[HBM] * 2,
        scratch_shapes=[
            pltpu.VMEM((count, width), jnp.bfloat16),
            pltpu.VMEM((count, width), jnp.bfloat16),
            pltpu.SemaphoreType.DMA((2,)),
        ],
        compiler_params=pltpu.CompilerParams(vmem_limit_bytes=4 * MIB),
        name="finish",
    )(*arrays)


def fetch_kernel(*refs, parts):
    count = len(parts)
    weights, held_refs, turned_refs = refs[:count], refs[count : 2 * count], refs[2 * count : 3 * count]
    sems = refs[-1]
    step = 256
    waiting = []
    for (first, rows), source, held, turned in zip(parts, weights, held_refs, turned_refs):
        for k in range(rows // step):
            copy = pltpu.make_async_copy(
                source.at[pl.ds(first + k * step, step)],
                held.at[pl.ds(k * step, step)],
                sems.at[len(waiting)],
            )
            copy.start()
            waiting.append((copy, held, turned, k * step))
    for copy, held, turned, start in waiting:
        copy.wait()
        turned[:, start : start + step] = held[start : start + step, :].T


def fetched(*parts):
    weights = [w for w, _, _ in parts]
    sizes = tuple((first, rows) for _, first, rows in parts)
    moved = sum(rows * w.shape[1] for w, _, rows in parts)
    held = [jax.ShapeDtypeStruct((rows, w.shape[1]), w.dtype) for w, _, rows in parts]
    turned = [jax.ShapeDtypeStruct((w.shape[1], rows), w.dtype) for w, _, rows in parts]
    outs = pl.pallas_call(
        functools.partial(fetch_kernel, parts=sizes),
        out_shape=held + turned,
        in_specs=[HBM] * len(parts),
        out_specs=[VMEM] * (2 * len(parts)),
        scratch_shapes=[pltpu.SemaphoreType.DMA((sum(rows for _, rows in sizes) // 256,))],
        compiler_params=pltpu.CompilerParams(vmem_limit_bytes=8 * MIB),
        cost_estimate=pl.CostEstimate(flops=0, bytes_accessed=4 * moved, transcendentals=0),
        name="fetch",
    )(*[in_hbm(w) for w in weights])
    return tuple(zip(outs[: len(parts)], outs[len(parts) :]))


def expert_kernel(
    near_ref, next_ref, far_ref, last_ref, router_ref,
    gate_ref, gate_turned_ref, down_ref, down_turned_ref, *refs,
):
    up_refs, up_turned_refs, out_refs = refs[:-4:2], refs[1:-4:2], refs[-4:]
    width, hidden_count = gate_ref.shape
    step = 256
    own_expert = lax.axis_index("expert")

    def both(first, last):
        blocks = (near_ref, next_ref, far_ref, last_ref)
        return jnp.concatenate([block[:, first:last] for block in blocks], axis=0)

    normed = jnp.concatenate([both(0, width), both(width, 2 * width)], axis=0)
    grads = both(2 * width, 3 * width)
    routes = both(3 * width, 3 * width + LANES).astype(jnp.float32)
    routes = jnp.concatenate([routes[:, :TOP_COUNT], routes[:, TOP_COUNT : 2 * TOP_COUNT]], axis=0)
    half = grads.shape[0]

    router = router_ref[...]
    contract = (((1,), (1,)), ((), ()))
    logits = lax.dot_general(normed, router, contract, preferred_element_type=jnp.float32)
    labels = lax.broadcasted_iota(jnp.int32, logits.shape, 1)
    labels_real = labels.astype(jnp.float32)
    chosen = routes[:, 0:1] == labels_real
    for k in range(1, TOP_COUNT):
        chosen = jnp.logical_or(chosen, routes[:, k : k + 1] == labels_real)
    raised = jnp.where(chosen, jnp.exp(logits), 0.0)
    gates = raised / jnp.sum(raised, axis=-1, keepdims=True)
    own = jnp.where(labels == own_expert, 1.0, 0.0)
    gate_own = jnp.sum(own * gates, axis=-1, keepdims=True)
    gate_f, gate_b = gate_own[:half], gate_own[half:]

    hiddens, d_pres, d_ups = [], [], []
    dgate = 0.0
    for piece in range(hidden_count // step):
        cols = slice(piece * step, piece * step + step)
        pre_gate = jnp.dot(normed, gate_ref[:, cols], preferred_element_type=jnp.float32)
        pre_up, start = 0.0, 0
        for ref in up_refs:
            rows = normed[:, start : start + ref.shape[0]]
            pre_up = pre_up + jnp.dot(rows, ref[:, cols], preferred_element_type=jnp.float32)
            start += ref.shape[0]
        d_hidden = jnp.dot(grads, down_turned_ref[:, cols], preferred_element_type=jnp.float32)
        sigma = jax.nn.sigmoid(pre_gate)
        silu_val = pre_gate * sigma
        hidden = silu_val * pre_up
        hiddens.append((hidden[:half] * gate_f).astype(jnp.bfloat16))
        dgate = dgate + jnp.sum(hidden[half:] * d_hidden, axis=-1, keepdims=True)
        d_hidden = d_hidden * gate_b
        d_ups.append((d_hidden * silu_val[half:]).astype(jnp.bfloat16))
        sigma_b = sigma[half:]
        slope = sigma_b * (1.0 + pre_gate[half:] * (1.0 - sigma_b))
        d_pres.append((d_hidden * pre_up[half:] * slope).astype(jnp.bfloat16))

    hidden = jnp.concatenate(hiddens, axis=1)
    d_pre = jnp.concatenate(d_pres, axis=1)
    d_up = jnp.concatenate(d_ups, axis=1)
    spread = gate_b * dgate * (own[half:] - gates[half:])
    spread_high = spread.astype(jnp.bfloat16)
    spread_low = (spread - spread_high.astype(jnp.float32)).astype(jnp.bfloat16)
    spread = jnp.concatenate([spread_high, spread_low], axis=1)
    routers = jnp.concatenate([router, router], axis=0)
    count = half // len(out_refs)
    start = 0
    for turned in up_turned_refs:
        span = turned.shape[1]
        cols = slice(start, start + span)
        out_f = jnp.dot(hidden, down_ref[:, cols], preferred_element_type=jnp.float32)
        d_normed = jnp.dot(d_up, turned[...], preferred_element_type=jnp.float32)
        d_normed = d_normed + jnp.dot(
            d_pre, gate_turned_ref[:, cols], preferred_element_type=jnp.float32
        )
        d_normed = d_normed + jnp.dot(
            spread, routers[:, cols], preferred_element_type=jnp.float32
        )
        for k, ref in enumerate(out_refs):
            rows = slice(k * count, (k + 1) * count)
            ref[:, cols] = out_f[rows].astype(jnp.bfloat16)
            ref[:, width + start : width + start + span] = d_normed[rows].astype(jnp.bfloat16)
        start += span


def run_experts(blocks, router, *weights):
    width = router.shape[1]
    return pl.pallas_call(
        expert_kernel,
        out_shape=[jax.ShapeDtypeStruct((b.shape[0], 2 * width), jnp.bfloat16) for b in blocks],
        in_specs=[VMEM] * (1 + len(blocks) + len(weights)),
        out_specs=[VMEM] * len(blocks),
        compiler_params=pltpu.CompilerParams(vmem_limit_bytes=24 * MIB),
        name="experts",
    )(*blocks, router, *weights)


def ending_kernel(across_ref, raw_ref, scale_ref, along_ref, back_ref, rest_ref):
    first_section = in_first_section()
    count, width = scale_ref.shape
    grads = across_ref[...].astype(jnp.float32)[:, width : 2 * width]
    raw = raw_ref[...].astype(jnp.float32)
    acts, gain_rows = raw[:, :width], raw[:, width:]
    spread = width // count
    gain_rows = gain_rows[:, :spread] + gain_rows[:, spread:]
    gain_row = jnp.concatenate(
        [
            gain_rows[row : row + 1, k : k + LANES]
            for k in range(0, spread, LANES)
            for row in range(count)
        ],
        axis=1,
    )
    factor = root_factor(acts)
    unit = acts * factor
    scale_ref[...] = jnp.where(first_section, factor * gain_row, 1.0)
    along_ref[...] = jnp.where(first_section, unit * gain_row, 0.0)
    back_ref[...] = jnp.where(first_section, unit * factor, 0.0)
    rest_ref[...] = jnp.where(first_section, grads, acts)


def added(*blocks):
    return sum(block.astype(jnp.float32) for block in blocks).astype(jnp.bfloat16)


def paired_plan(
    fwd_act, fwd_routes, bwd_saved, bwd_grad, bwd_routes, norm_gain, router, w_gate, w_up, w_down
):
    count, width = fwd_act.shape[1:]
    own, acts, gain_row, router_rows = pack_rows(
        fwd_act, fwd_routes, bwd_saved, bwd_grad, bwd_routes, norm_gain, router.T
    )
    across = swapped(own, SECTION)
    along = swapped(own, HALF)
    cuts = (width // 2, width)
    gate_hbm, up_hbm, down_hbm = w_gate[0], w_up[0], w_down[0]
    gate_mats, *ups = fetched((gate_hbm, 0, width), (up_hbm, 0, cuts[0]))
    along, gate_mats, ups = lax.optimization_barrier((along, gate_mats, ups))
    rows = jax.ShapeDtypeStruct((count, 3 * width + LANES), jnp.bfloat16)
    mine = in_vmem(merge_kernel, "merge", [rows], along, across)[0]
    down_hbm, up_hbm, _ = lax.optimization_barrier((down_hbm, up_hbm, mine))
    down_mats, *more = fetched(
        (down_hbm, 0, down_hbm.shape[0]), (up_hbm, cuts[0], cuts[1] - cuts[0])
    )
    ups = ups + more
    received = [swapped(mine, k) for k in SQUARE_CHIPS]
    early = jnp.concatenate([mine, received[EARLY]], axis=0)
    late = jnp.concatenate([b for i, b in enumerate(received) if i != EARLY], axis=0)
    early, ups, down_mats = lax.optimization_barrier((early, ups, down_mats))
    last = [swapped(b, CORE) for i, b in enumerate(received) if i != EARLY]
    blocks = [early, late, swapped(early, CORE), jnp.concatenate(last, axis=0)]

    weights = [m for mats in [gate_mats, down_mats] + ups for m in mats]
    kept = run_experts(blocks, router_rows, *weights)
    chips = [added(block, swapped(sent, CORE)) for block, sent in zip(kept[:2], kept[2:])]
    acts, last_chip = lax.optimization_barrier((acts, chips[1]))
    chips = [chips[0], last_chip]
    real = jax.ShapeDtypeStruct((count, width), jnp.float32)
    wide = jax.ShapeDtypeStruct((count, width + 2 * (width // count)), jnp.bfloat16)
    raw = swapped(in_vmem(widen_kernel, "widen", [wide], acts, gain_row)[0], SECTION)
    pieces = [chips[0][:count]]
    order = [EARLY] + [i for i in range(len(SQUARE_CHIPS)) if i != EARLY]
    for i, distance in enumerate(SQUARE_CHIPS):
        chip, place = divmod(order.index(i) + 1, 2)
        pieces.append(swapped(chips[chip][place * count : (place + 1) * count], distance))
    ending = in_vmem(ending_kernel, "endings", [real] * 4, across, raw)
    small = jax.ShapeDtypeStruct((count, width), jnp.bfloat16)
    leaving, staying = in_vmem(leave_kernel, "leave", [small, real], *pieces)
    other = swapped(leaving, SECTION + HALF)
    return tuple(finish(staying, other, *ending))


def per_device(fwd_act, fwd_routes, *rest):
    sections, devices = lax.axis_size("section"), lax.axis_size("expert")
    tokens, top_count = fwd_routes.shape[1:]
    router = rest[4]
    paired = sections == 2 and devices == 2 * SQUARE and router.shape == (16 * LANES, devices)
    paired = paired and tokens == 8 and top_count == TOP_COUNT
    plan = paired_plan if paired else routed_plan
    return plan(fwd_act, fwd_routes, *rest)


def solution(mesh):
    in_specs = (
        P("section", "expert", None),
        P("section", "expert", None),
        P("section", "expert", None),
        P("section", "expert", None),
        P("section", "expert", None),
        P("section", None),
        P(),
        P("expert", None, None),
        P("expert", None, None),
        P("expert", None, None),
    )
    out_specs = (P("section", "expert", None), P("section", "expert", None))
    return jax.shard_map(
        per_device, mesh=mesh, in_specs=in_specs, out_specs=out_specs, check_vma=False
    )
```

```python
import functools
import jax
import jax.numpy as jnp
from jax import lax
from jax.experimental import pallas as pl
from jax.experimental.pallas import tpu as pltpu
from jax.sharding import PartitionSpec as P

EPSILON = 1e-06


def shifted(block, axis, distance):
    devices = range(lax.axis_size(axis))
    route = [(i - distance, i) for i in devices if i - distance in devices]
    return lax.ppermute(block, axis, route)


def normalize(acts_in, gain_row):
    values = acts_in.astype(jnp.float32)
    factor = lax.rsqrt(jnp.mean(values * values, axis=-1, keepdims=True) + EPSILON)
    unit_rows = values * factor
    return ((unit_rows * gain_row).astype(jnp.bfloat16), unit_rows, factor)


def gate_values(normed, router, routes):
    logits = jnp.dot(normed, router, preferred_element_type=jnp.float32)
    chosen = jnp.take_along_axis(logits, routes, axis=1)
    raised = jnp.exp(chosen)
    return raised / jnp.sum(raised, axis=-1, keepdims=True)


def expert_forward(rows_in, gate_mat, up_mat, down_mat):
    pre_gate = jnp.dot(rows_in, gate_mat, preferred_element_type=jnp.float32)
    pre_up = jnp.dot(rows_in, up_mat, preferred_element_type=jnp.float32)
    sigma = jax.nn.sigmoid(pre_gate)
    hidden = (pre_gate * sigma * pre_up).astype(jnp.bfloat16)
    return jnp.dot(hidden, down_mat, preferred_element_type=jnp.float32).astype(jnp.bfloat16)


def expert_backward(rows_in, grads_in, gate_mat, up_mat, down_mat):
    pre_gate = jnp.dot(rows_in, gate_mat, preferred_element_type=jnp.float32)
    pre_up = jnp.dot(rows_in, up_mat, preferred_element_type=jnp.float32)
    sigma = jax.nn.sigmoid(pre_gate)
    silu_val = pre_gate * sigma
    hidden = (silu_val * pre_up).astype(jnp.bfloat16)
    expert_out = jnp.dot(hidden, down_mat, preferred_element_type=jnp.float32).astype(jnp.bfloat16)
    dgate = jnp.sum(grads_in.astype(jnp.float32) * expert_out.astype(jnp.float32), axis=-1).astype(
        jnp.bfloat16
    )
    contract = (((1,), (1,)), ((), ()))
    d_hidden = lax.dot_general(grads_in, down_mat, contract, preferred_element_type=jnp.float32)
    d_up = (d_hidden * silu_val).astype(jnp.bfloat16)
    d_pre = (d_hidden * pre_up * sigma * (1.0 + pre_gate * (1.0 - sigma))).astype(jnp.bfloat16)
    d_rows = lax.dot_general(d_pre, gate_mat, contract, preferred_element_type=jnp.float32)
    d_rows = d_rows + lax.dot_general(d_up, up_mat, contract, preferred_element_type=jnp.float32)
    return (d_rows.astype(jnp.bfloat16), dgate)


def input_gradient(gates, dgate, pair_grads, routes, router, unit_rows, factor, gain_row, grads_in):
    d_normed = jnp.sum(gates[:, :, None] * pair_grads, axis=1)
    d_chosen = gates * (dgate - jnp.sum(gates * dgate, axis=-1, keepdims=True))
    labels = jnp.arange(router.shape[1], dtype=jnp.int32)
    hits = (routes[:, :, None] == labels[None, None, :]).astype(jnp.float32)
    d_logits = jnp.sum(hits * d_chosen[:, :, None], axis=1)
    d_normed = d_normed + lax.dot_general(
        d_logits,
        router.astype(jnp.float32),
        (((1,), (1,)), ((), ())),
        precision=lax.Precision.HIGHEST,
    )
    d_unit = d_normed * gain_row
    result = factor * (d_unit - unit_rows * jnp.mean(d_unit * unit_rows, axis=-1, keepdims=True))
    return (result + grads_in.astype(jnp.float32)).astype(jnp.bfloat16)


def placement(routes, expert_count, capacity):
    flat_ids = routes.reshape(-1)
    labels = jnp.arange(expert_count, dtype=jnp.int32)
    onehot = (flat_ids[:, None] == labels[None, :]).astype(jnp.int32)
    before = jnp.cumsum(onehot, axis=0) - onehot
    slot_ids = jnp.sum(before * onehot, axis=1)
    target = flat_ids * capacity + slot_ids
    slot_labels = jnp.arange(expert_count * capacity, dtype=jnp.int32)
    select = (slot_labels[:, None] == target[None, :]).astype(jnp.bfloat16)
    spread = jnp.sum(
        select.reshape(expert_count * capacity, routes.shape[0], routes.shape[1]), axis=2
    )
    return (target, spread)


def dispatch(spread, rows_in, expert_count, capacity):
    placed = jnp.dot(spread, rows_in, preferred_element_type=jnp.float32).astype(jnp.bfloat16)
    return placed.reshape(expert_count, capacity, rows_in.shape[1])


def routed_plan(
    fwd_act, fwd_routes, bwd_saved, bwd_grad, bwd_routes, norm_gain, router, w_gate, w_up, w_down
):
    tok_count = fwd_act.shape[1]
    top_count = fwd_routes.shape[2]
    model_width = fwd_act.shape[2]
    expert_count = router.shape[1]
    capacity = min(tok_count, max(2, 2 * tok_count * top_count // expert_count))
    gain_row = norm_gain[0]
    gate_mat = w_gate[0]
    up_mat = w_up[0]
    down_mat = w_down[0]
    acts_f = fwd_act[0]
    routes_f = fwd_routes[0]
    normed_f, unused_unit, unused_factor = normalize(acts_f, gain_row)
    gates_f = gate_values(normed_f, router, routes_f)
    target_f, spread_f = placement(routes_f, expert_count, capacity)
    send_f = dispatch(spread_f, normed_f, expert_count, capacity)
    saved_b = bwd_saved[0]
    grads_b = bwd_grad[0]
    routes_b = bwd_routes[0]
    normed_b, unit_b, factor_b = normalize(saved_b, gain_row)
    gates_b = gate_values(normed_b, router, routes_b)
    target_b, spread_b = placement(routes_b, expert_count, capacity)
    send_x = dispatch(spread_b, normed_b, expert_count, capacity)
    send_g = dispatch(spread_b, grads_b, expert_count, capacity)
    rows_in = lax.all_to_all(send_f, "expert", split_axis=0, concat_axis=0, tiled=True)
    sources = rows_in.shape[0]
    slots = rows_in.shape[1]
    result = expert_forward(rows_in.reshape(-1, model_width), gate_mat, up_mat, down_mat)
    back_f = lax.all_to_all(
        result.reshape(sources, slots, model_width),
        "expert",
        split_axis=0,
        concat_axis=0,
        tiled=True,
    )
    rows_in = lax.all_to_all(send_x, "expert", split_axis=0, concat_axis=0, tiled=True)
    grads_in = lax.all_to_all(send_g, "expert", split_axis=0, concat_axis=0, tiled=True)
    sources = rows_in.shape[0]
    slots = rows_in.shape[1]
    d_rows, d_gates = expert_backward(
        rows_in.reshape(-1, model_width),
        grads_in.reshape(-1, model_width),
        gate_mat,
        up_mat,
        down_mat,
    )
    back_rows = lax.all_to_all(
        d_rows.reshape(sources, slots, model_width),
        "expert",
        split_axis=0,
        concat_axis=0,
        tiled=True,
    )
    back_gates = lax.all_to_all(
        d_gates.reshape(sources, slots), "expert", split_axis=0, concat_axis=0, tiled=True
    )
    picked_f = jnp.take(back_f.reshape(expert_count * capacity, model_width), target_f, axis=0)
    picked_f = picked_f.reshape(tok_count, top_count, model_width).astype(jnp.float32)
    layer_out = (
        acts_f.astype(jnp.float32) + jnp.sum(gates_f[:, :, None] * picked_f, axis=1)
    ).astype(jnp.bfloat16)
    fwd_next = shifted(layer_out[None], "section", 1)
    pair_grads = jnp.take(back_rows.reshape(expert_count * capacity, model_width), target_b, axis=0)
    pair_grads = pair_grads.reshape(tok_count, top_count, model_width).astype(jnp.float32)
    dgate = (
        jnp.take(back_gates.reshape(-1), target_b, axis=0)
        .reshape(tok_count, top_count)
        .astype(jnp.float32)
    )
    d_input = input_gradient(
        gates_b, dgate, pair_grads, routes_b, router, unit_b, factor_b, gain_row, grads_b
    )
    grad_prev = shifted(d_input[None], "section", -1)
    return (fwd_next, grad_prev)


AXES = ("section", "expert")
SQUARE = 8
CORE, HALF, SECTION = 1, 9, 16
EARLY = 2
LANES = 128
SQUARE_CHIPS = (3, 5, 7)
TOP_COUNT = 8
VMEM = pl.BlockSpec(memory_space=pltpu.VMEM)
SMEM = pl.BlockSpec(memory_space=pltpu.SMEM)
HBM = pl.BlockSpec(memory_space=pltpu.HBM)
MIB = 1024 * 1024


def swapped(block, distance):
    count = lax.axis_size(AXES)
    return lax.ppermute(block, AXES, [(i, i ^ distance) for i in range(count)])


def in_hbm(array):
    return pltpu.with_memory_space_constraint(array, pltpu.HBM)


def root_factor(values):
    return lax.rsqrt(jnp.mean(values * values, axis=-1, keepdims=True) + EPSILON)


def in_first_section():
    return lax.axis_index("section") == 0


def pack_kernel(
    fwd_act, fwd_routes, bwd_saved, bwd_grad, bwd_routes, gain, router,
    rows_ref, acts_ref, gain_ref, router_ref, grads_ref, routes_ref, sems,
):
    first_section = in_first_section()
    grad_copy = pltpu.make_async_copy(bwd_grad.at[0], grads_ref, sems.at[0])
    gain_copy = pltpu.make_async_copy(gain, gain_ref, sems.at[1])
    router_copy = pltpu.make_async_copy(router, router_ref, sems.at[4])

    @pl.when(first_section)
    def _():
        pltpu.make_async_copy(fwd_act.at[0], acts_ref, sems.at[2]).start()
        pltpu.make_async_copy(fwd_routes.at[0], routes_ref, sems.at[3]).start()

    @pl.when(jnp.logical_not(first_section))
    def _():
        pltpu.make_async_copy(bwd_saved.at[0], acts_ref, sems.at[2]).start()
        pltpu.make_async_copy(bwd_routes.at[0], routes_ref, sems.at[3]).start()

    gain_copy.start()
    grad_copy.start()
    router_copy.start()
    pltpu.make_async_copy(fwd_act.at[0], acts_ref, sems.at[2]).wait()
    gain_copy.wait()
    acts = acts_ref[...].astype(jnp.float32)
    normed = acts * root_factor(acts) * gain_ref[...]
    pltpu.make_async_copy(fwd_routes.at[0], routes_ref, sems.at[3]).wait()
    grad_copy.wait()
    routes = routes_ref[...].astype(jnp.float32)
    blank = jnp.zeros_like(routes)
    routes = jnp.concatenate(
        [
            jnp.where(first_section, routes, blank),
            jnp.where(first_section, blank, routes),
            jnp.zeros((routes.shape[0], LANES - 2 * TOP_COUNT), jnp.float32),
        ],
        axis=1,
    )
    rows_ref[...] = jnp.concatenate(
        [normed, grads_ref[...].astype(jnp.float32), routes], axis=1
    ).astype(jnp.bfloat16)
    router_copy.wait()


def pack_rows(*arrays):
    fwd_act, fwd_routes, _, _, _, gain, router = arrays
    count, width = fwd_act.shape[1:]
    return pl.pallas_call(
        pack_kernel,
        out_shape=[
            jax.ShapeDtypeStruct((count, 2 * width + LANES), jnp.bfloat16),
            jax.ShapeDtypeStruct((count, width), jnp.bfloat16),
            jax.ShapeDtypeStruct(gain.shape, gain.dtype),
            jax.ShapeDtypeStruct(router.shape, router.dtype),
        ],
        in_specs=[HBM] * 7,
        out_specs=[VMEM] * 4,
        scratch_shapes=[
            pltpu.VMEM((count, width), jnp.bfloat16),
            pltpu.VMEM(fwd_routes.shape[1:], jnp.int32),
            pltpu.SemaphoreType.DMA((5,)),
        ],
        compiler_params=pltpu.CompilerParams(vmem_limit_bytes=4 * MIB),
        name="pack",
    )(*[in_hbm(x) for x in arrays])


def widen_kernel(acts_ref, gain_ref, raw_ref):
    gain_row = gain_ref[...]
    count = acts_ref.shape[0]
    pieces = [gain_row[:, k : k + LANES] for k in range(0, gain_row.shape[1], LANES)]
    gain_rows = jnp.concatenate(
        [jnp.concatenate(pieces[k : k + count], axis=0) for k in range(0, len(pieces), count)],
        axis=1,
    )
    gain_high = gain_rows.astype(jnp.bfloat16).astype(jnp.float32)
    raw_ref[...] = jnp.concatenate(
        [acts_ref[...].astype(jnp.float32), gain_high, gain_rows - gain_high], axis=1
    ).astype(jnp.bfloat16)


def in_vmem(body, name, out_shape, *arrays):
    return pl.pallas_call(
        body,
        out_shape=out_shape,
        in_specs=[VMEM] * len(arrays),
        out_specs=[VMEM] * len(out_shape),
        compiler_params=pltpu.CompilerParams(vmem_limit_bytes=4 * MIB),
        name=name,
    )(*arrays)


def merge_kernel(along_ref, across_ref, mine_ref):
    width = (across_ref.shape[1] - LANES) // 2
    first_section = in_first_section()

    def merge(forward_ref, backward_ref):
        mine_ref[:, :width] = forward_ref[:, :width]
        mine_ref[:, width : 3 * width] = backward_ref[:, : 2 * width]

    @pl.when(first_section)
    def _():
        merge(along_ref, across_ref)

    @pl.when(jnp.logical_not(first_section))
    def _():
        merge(across_ref, along_ref)

    tail = slice(2 * width, 2 * width + LANES)
    mine_ref[:, 3 * width :] = along_ref[:, tail] + across_ref[:, tail]


def leave_kernel(a_ref, b_ref, c_ref, d_ref, leaving_ref, staying_ref):
    first_section = in_first_section()
    width = leaving_ref.shape[1]
    total = a_ref[...].astype(jnp.float32) + b_ref[...].astype(jnp.float32)
    total = total + c_ref[...].astype(jnp.float32) + d_ref[...].astype(jnp.float32)
    forward, backward = total[:, :width], total[:, width:]
    leaving_ref[...] = jnp.where(first_section, forward, backward).astype(jnp.bfloat16)
    staying_ref[...] = jnp.where(first_section, backward, forward)


def finish_kernel(
    staying_ref, other_ref, scale_ref, towards_ref, back_ref, rest_ref, fwd_hbm, grad_hbm,
    result_ref, nothing_ref, sems,
):
    first_section = in_first_section()
    nothing_ref[...] = jnp.zeros_like(nothing_ref)

    @pl.when(first_section)
    def _():
        pltpu.make_async_copy(nothing_ref, fwd_hbm.at[0], sems.at[0]).start()

    @pl.when(jnp.logical_not(first_section))
    def _():
        pltpu.make_async_copy(nothing_ref, grad_hbm.at[0], sems.at[0]).start()

    sums = staying_ref[...] + other_ref[...].astype(jnp.float32)
    mean = jnp.mean(sums * towards_ref[...], axis=-1, keepdims=True)
    result = sums * scale_ref[...] + rest_ref[...] - back_ref[...] * mean
    result_ref[...] = result.astype(jnp.bfloat16)

    @pl.when(first_section)
    def _():
        pltpu.make_async_copy(result_ref, grad_hbm.at[0], sems.at[1]).start()

    @pl.when(jnp.logical_not(first_section))
    def _():
        pltpu.make_async_copy(result_ref, fwd_hbm.at[0], sems.at[1]).start()

    pltpu.make_async_copy(nothing_ref, fwd_hbm.at[0], sems.at[0]).wait()
    pltpu.make_async_copy(result_ref, grad_hbm.at[0], sems.at[1]).wait()


def finish(*arrays):
    count, width = arrays[0].shape
    return pl.pallas_call(
        finish_kernel,
        out_shape=[jax.ShapeDtypeStruct((1, count, width), jnp.bfloat16)] * 2,
        in_specs=[VMEM] * len(arrays),
        out_specs=[HBM] * 2,
        scratch_shapes=[
            pltpu.VMEM((count, width), jnp.bfloat16),
            pltpu.VMEM((count, width), jnp.bfloat16),
            pltpu.SemaphoreType.DMA((2,)),
        ],
        compiler_params=pltpu.CompilerParams(vmem_limit_bytes=4 * MIB),
        name="finish",
    )(*arrays)


def fetch_kernel(*refs, parts):
    count = len(parts)
    weights, held_refs, turned_refs = refs[:count], refs[count : 2 * count], refs[2 * count : 3 * count]
    sems = refs[-1]
    step = 256
    waiting = []
    for (first, rows), source, held, turned in zip(parts, weights, held_refs, turned_refs):
        for k in range(rows // step):
            copy = pltpu.make_async_copy(
                source.at[pl.ds(first + k * step, step)],
                held.at[pl.ds(k * step, step)],
                sems.at[len(waiting)],
            )
            copy.start()
            waiting.append((copy, held, turned, k * step))
    for copy, held, turned, start in waiting:
        copy.wait()
        turned[:, start : start + step] = held[start : start + step, :].T


def fetched(*parts):
    weights = [w for w, _, _ in parts]
    sizes = tuple((first, rows) for _, first, rows in parts)
    moved = sum(rows * w.shape[1] for w, _, rows in parts)
    held = [jax.ShapeDtypeStruct((rows, w.shape[1]), w.dtype) for w, _, rows in parts]
    turned = [jax.ShapeDtypeStruct((w.shape[1], rows), w.dtype) for w, _, rows in parts]
    outs = pl.pallas_call(
        functools.partial(fetch_kernel, parts=sizes),
        out_shape=held + turned,
        in_specs=[HBM] * len(parts),
        out_specs=[VMEM] * (2 * len(parts)),
        scratch_shapes=[pltpu.SemaphoreType.DMA((sum(rows for _, rows in sizes) // 256,))],
        compiler_params=pltpu.CompilerParams(vmem_limit_bytes=8 * MIB),
        cost_estimate=pl.CostEstimate(flops=0, bytes_accessed=4 * moved, transcendentals=0),
        name="fetch",
    )(*[in_hbm(w) for w in weights])
    return tuple(zip(outs[: len(parts)], outs[len(parts) :]))


def expert_kernel(
    near_ref, next_ref, far_ref, last_ref, router_ref,
    gate_ref, gate_turned_ref, down_ref, down_turned_ref, *refs,
):
    up_refs, up_turned_refs, out_refs = refs[:-4:2], refs[1:-4:2], refs[-4:]
    width, hidden_count = gate_ref.shape
    step = 256
    own_expert = lax.axis_index("expert")

    def both(first, last):
        blocks = (near_ref, next_ref, far_ref, last_ref)
        return jnp.concatenate([block[:, first:last] for block in blocks], axis=0)

    normed = jnp.concatenate([both(0, width), both(width, 2 * width)], axis=0)
    grads = both(2 * width, 3 * width)
    routes = both(3 * width, 3 * width + LANES).astype(jnp.float32)
    routes = jnp.concatenate([routes[:, :TOP_COUNT], routes[:, TOP_COUNT : 2 * TOP_COUNT]], axis=0)
    half = grads.shape[0]

    router = router_ref[...]
    contract = (((1,), (1,)), ((), ()))
    logits = lax.dot_general(normed, router, contract, preferred_element_type=jnp.float32)
    labels = lax.broadcasted_iota(jnp.int32, logits.shape, 1)
    labels_real = labels.astype(jnp.float32)
    chosen = routes[:, 0:1] == labels_real
    for k in range(1, TOP_COUNT):
        chosen = jnp.logical_or(chosen, routes[:, k : k + 1] == labels_real)
    raised = jnp.where(chosen, jnp.exp(logits), 0.0)
    gates = raised / jnp.sum(raised, axis=-1, keepdims=True)
    own = jnp.where(labels == own_expert, 1.0, 0.0)
    gate_own = jnp.sum(own * gates, axis=-1, keepdims=True)
    gate_f, gate_b = gate_own[:half], gate_own[half:]

    hiddens, d_pres, d_ups = [], [], []
    dgate = 0.0
    for piece in range(hidden_count // step):
        cols = slice(piece * step, piece * step + step)
        pre_gate = jnp.dot(normed, gate_ref[:, cols], preferred_element_type=jnp.float32)
        pre_up, start = 0.0, 0
        for ref in up_refs:
            rows = normed[:, start : start + ref.shape[0]]
            pre_up = pre_up + jnp.dot(rows, ref[:, cols], preferred_element_type=jnp.float32)
            start += ref.shape[0]
        d_hidden = jnp.dot(grads, down_turned_ref[:, cols], preferred_element_type=jnp.float32)
        sigma = jax.nn.sigmoid(pre_gate)
        silu_val = pre_gate * sigma
        hidden = silu_val * pre_up
        hiddens.append((hidden[:half] * gate_f).astype(jnp.bfloat16))
        dgate = dgate + jnp.sum(hidden[half:] * d_hidden, axis=-1, keepdims=True)
        d_hidden = d_hidden * gate_b
        d_ups.append((d_hidden * silu_val[half:]).astype(jnp.bfloat16))
        sigma_b = sigma[half:]
        slope = sigma_b * (1.0 + pre_gate[half:] * (1.0 - sigma_b))
        d_pres.append((d_hidden * pre_up[half:] * slope).astype(jnp.bfloat16))

    hidden = jnp.concatenate(hiddens, axis=1)
    d_pre = jnp.concatenate(d_pres, axis=1)
    d_up = jnp.concatenate(d_ups, axis=1)
    spread = gate_b * dgate * (own[half:] - gates[half:])
    spread_high = spread.astype(jnp.bfloat16)
    spread_low = (spread - spread_high.astype(jnp.float32)).astype(jnp.bfloat16)
    spread = jnp.concatenate([spread_high, spread_low], axis=1)
    routers = jnp.concatenate([router, router], axis=0)
    count = half // len(out_refs)
    start = 0
    for turned in up_turned_refs:
        span = turned.shape[1]
        cols = slice(start, start + span)
        out_f = jnp.dot(hidden, down_ref[:, cols], preferred_element_type=jnp.float32)
        d_normed = jnp.dot(d_up, turned[...], preferred_element_type=jnp.float32)
        d_normed = d_normed + jnp.dot(
            d_pre, gate_turned_ref[:, cols], preferred_element_type=jnp.float32
        )
        d_normed = d_normed + jnp.dot(
            spread, routers[:, cols], preferred_element_type=jnp.float32
        )
        for k, ref in enumerate(out_refs):
            rows = slice(k * count, (k + 1) * count)
            ref[:, cols] = out_f[rows].astype(jnp.bfloat16)
            ref[:, width + start : width + start + span] = d_normed[rows].astype(jnp.bfloat16)
        start += span


def run_experts(blocks, router, *weights):
    width = router.shape[1]
    return pl.pallas_call(
        expert_kernel,
        out_shape=[jax.ShapeDtypeStruct((b.shape[0], 2 * width), jnp.bfloat16) for b in blocks],
        in_specs=[VMEM] * (1 + len(blocks) + len(weights)),
        out_specs=[VMEM] * len(blocks),
        compiler_params=pltpu.CompilerParams(vmem_limit_bytes=24 * MIB),
        name="experts",
    )(*blocks, router, *weights)


def ending_kernel(across_ref, raw_ref, scale_ref, along_ref, back_ref, rest_ref):
    first_section = in_first_section()
    count, width = scale_ref.shape
    grads = across_ref[...].astype(jnp.float32)[:, width : 2 * width]
    raw = raw_ref[...].astype(jnp.float32)
    acts, gain_rows = raw[:, :width], raw[:, width:]
    spread = width // count
    gain_rows = gain_rows[:, :spread] + gain_rows[:, spread:]
    gain_row = jnp.concatenate(
        [
            gain_rows[row : row + 1, k : k + LANES]
            for k in range(0, spread, LANES)
            for row in range(count)
        ],
        axis=1,
    )
    factor = root_factor(acts)
    unit = acts * factor
    scale_ref[...] = jnp.where(first_section, factor * gain_row, 1.0)
    along_ref[...] = jnp.where(first_section, unit * gain_row, 0.0)
    back_ref[...] = jnp.where(first_section, unit * factor, 0.0)
    rest_ref[...] = jnp.where(first_section, grads, acts)


def added(*blocks):
    return sum(block.astype(jnp.float32) for block in blocks).astype(jnp.bfloat16)


def paired_plan(
    fwd_act, fwd_routes, bwd_saved, bwd_grad, bwd_routes, norm_gain, router, w_gate, w_up, w_down
):
    count, width = fwd_act.shape[1:]
    own, acts, gain_row, router_rows = pack_rows(
        fwd_act, fwd_routes, bwd_saved, bwd_grad, bwd_routes, norm_gain, router.T
    )
    across = swapped(own, SECTION)
    along = swapped(own, HALF)
    cuts = (3 * width // 8, width)
    gate_hbm, up_hbm, down_hbm = w_gate[0], w_up[0], w_down[0]
    gate_mats, *ups = fetched((gate_hbm, 0, width), (up_hbm, 0, cuts[0]))
    along, gate_mats, ups = lax.optimization_barrier((along, gate_mats, ups))
    rows = jax.ShapeDtypeStruct((count, 3 * width + LANES), jnp.bfloat16)
    mine = in_vmem(merge_kernel, "merge", [rows], along, across)[0]
    down_hbm, up_hbm, _ = lax.optimization_barrier((down_hbm, up_hbm, mine))
    down_mats, *more = fetched(
        (down_hbm, 0, down_hbm.shape[0]), (up_hbm, cuts[0], cuts[1] - cuts[0])
    )
    ups = ups + more
    received = [swapped(mine, k) for k in SQUARE_CHIPS]
    early = jnp.concatenate([mine, received[EARLY]], axis=0)
    late = jnp.concatenate([b for i, b in enumerate(received) if i != EARLY], axis=0)
    early, ups, down_mats = lax.optimization_barrier((early, ups, down_mats))
    last = [swapped(b, CORE) for i, b in enumerate(received) if i != EARLY]
    blocks = [early, late, swapped(early, CORE), jnp.concatenate(last, axis=0)]

    weights = [m for mats in [gate_mats, down_mats] + ups for m in mats]
    kept = run_experts(blocks, router_rows, *weights)
    chips = [added(block, swapped(sent, CORE)) for block, sent in zip(kept[:2], kept[2:])]
    acts, last_chip = lax.optimization_barrier((acts, chips[1]))
    chips = [chips[0], last_chip]
    real = jax.ShapeDtypeStruct((count, width), jnp.float32)
    wide = jax.ShapeDtypeStruct((count, width + 2 * (width // count)), jnp.bfloat16)
    raw = swapped(in_vmem(widen_kernel, "widen", [wide], acts, gain_row)[0], SECTION)
    pieces = [chips[0][:count]]
    order = [EARLY] + [i for i in range(len(SQUARE_CHIPS)) if i != EARLY]
    for i, distance in enumerate(SQUARE_CHIPS):
        chip, place = divmod(order.index(i) + 1, 2)
        pieces.append(swapped(chips[chip][place * count : (place + 1) * count], distance))
    ending = in_vmem(ending_kernel, "endings", [real] * 4, across, raw)
    small = jax.ShapeDtypeStruct((count, width), jnp.bfloat16)
    leaving, staying = in_vmem(leave_kernel, "leave", [small, real], *pieces)
    other = swapped(leaving, SECTION + HALF)
    return tuple(finish(staying, other, *ending))


def per_device(fwd_act, fwd_routes, *rest):
    sections, devices = lax.axis_size("section"), lax.axis_size("expert")
    tokens, top_count = fwd_routes.shape[1:]
    router = rest[4]
    paired = sections == 2 and devices == 2 * SQUARE and router.shape == (16 * LANES, devices)
    paired = paired and tokens == 8 and top_count == TOP_COUNT
    plan = paired_plan if paired else routed_plan
    return plan(fwd_act, fwd_routes, *rest)


def solution(mesh):
    in_specs = (
        P("section", "expert", None),
        P("section", "expert", None),
        P("section", "expert", None),
        P("section", "expert", None),
        P("section", "expert", None),
        P("section", None),
        P(),
        P("expert", None, None),
        P("expert", None, None),
        P("expert", None, None),
    )
    out_specs = (P("section", "expert", None), P("section", "expert", None))
    return jax.shard_map(
        per_device, mesh=mesh, in_specs=in_specs, out_specs=out_specs, check_vma=False
    )
```
